32 devices in a mesh: row: 8 (over z, x), col: 4 (over y, core).
Axes of the slice: x: 2, y: 2, z: 4, core: 2. Of those that a mesh axis runs over, the one named last changes fastest.
Arguments:
- node_feats: bfloat16 [8192, 256], P(('row', 'col')), may hold values from -6 to 6
- dest_grad: bfloat16 [4, 2048, 256], P('col', 'row'), may hold values from -6 to 6
- bases: bfloat16 [30, 256, 256], replicated, may hold values from -0.375 to 0.375
- coefs: bfloat16 [2000, 30], replicated, may hold values from -1 to 1
- src_ids: int32 [8, 4, 1024], P('row', 'col'), may hold values from 0 to 1023
- dst_ids: int32 [8, 4, 1024], P('row', 'col'), may hold values from 0 to 2047
- rel_ids: int32 [8, 4, 1024], P('row', 'col'), may hold values from 0 to 1999
- edge_norm: float32 [8, 4, 1024], P('row', 'col'), may hold values from 0.1 to 1
- block_fill: int32 [8, 4, 8], P('row', 'col'), may hold values from 0 to 128, as said below
Outputs:
- node_grad: bfloat16 [8192, 256], P(('row', 'col'))
- basis_grad: float32 [7680, 256], P(('row', 'col'))
- coef_grad: float32 [2000, 30], replicated
The draws below stay inside these ranges and needn't reach their ends.
Inputs may be any that keep to these rules, and one draw needn't show every extreme that they name: `block_fill`: the first block of every device is full, and blocks after a device's last live block are empty.
All inputs are finite; a program needn't handle non-finite values.
Results may differ from the reference program's by a relative error of at most 0.0049.
Values may be sent and summed in bfloat16 or wider, within the bound.
No kernel may reach another device: no remote copies, remote signals or barrier semaphores. Data moves between devices by JAX's collectives and lax.ppermute only.
A program may use at most 64 MiB of HBM per device.

```python
import math
import jax
import jax.numpy as jnp
from jax import lax

D = 256
BASES = 30
RELS = 2000
VS = 256
EBLK = 8
EDGE_BLOCK = 128
EDEV = 1024
VERTS = 8192
N_ROW = 8
N_COL = 4


def draw_block_fill(key, part):
    first_key = jax.random.fold_in(key, 11)
    second_key = jax.random.fold_in(key, 23)
    live_blocks = jax.random.randint(first_key, (N_ROW, N_COL, 1), 1, EBLK + 1)
    fills = jax.random.randint(second_key, (N_ROW, N_COL, EBLK), 1, EDGE_BLOCK + 1)
    index = jnp.arange(EBLK, dtype=jnp.int32)[None, None, :]
    fills = jnp.where(index == 0, EDGE_BLOCK, fills)
    return jnp.where(index < live_blocks, fills, 0).astype(jnp.int32)


def plant(entries, own_key, least, largest):
    dims = entries.shape
    place = [jax.random.randint(jax.random.fold_in(own_key, axis), (), 0, dims[axis]) for axis in range(len(dims))]
    entries = entries.at[tuple(place)].set(least)
    longest = dims.index(max(dims))
    place[longest] = (place[longest] + 1) % dims[longest]
    return entries.at[tuple(place)].set(largest)


def level_of(rng, shape, cuts, least, top_value):
    gain = 1.0
    for dim, blocks in cuts:
        heights = jax.random.uniform(jax.random.fold_in(jax.random.fold_in(rng, 6), dim), (blocks,), jnp.float32, least / len(cuts), top_value / len(cuts))
        gain = gain * jnp.repeat(jnp.exp(heights), shape[dim] // blocks).reshape((-1,) + (1,) * (len(shape) - 1 - dim))
    return gain


def centred(rng, extent, scale, bound, split=(), held_as=jnp.bfloat16):
    array = scale * jax.random.normal(rng, extent, jnp.float32)
    if split:
        array = array * level_of(rng, extent, split, -0.22, 0.18)
    return jnp.clip(array, -bound, bound).astype(held_as)


def setup_inputs(seed: int = 0) -> dict:
    streams_of = jax.random.split(jax.random.key(seed), 10)
    node_feats = centred(streams_of[0], (VERTS, D), 1.0, 6.0, ((0, 32),))
    dest_grad = centred(streams_of[1], (N_COL, N_ROW * VS, D), 1.0, 6.0, ((0, 4), (1, 8)))
    bases = centred(streams_of[2], (BASES, D, D), D ** -0.5, 0.375)
    coefs = centred(streams_of[3], (RELS, BASES), BASES ** -0.5, 1.0)
    src_ids = plant(jax.random.randint(streams_of[4], (N_ROW, N_COL, EDEV), 0, VS * N_COL), jax.random.fold_in(streams_of[4], 1), 0, (VS * N_COL) - 1).astype(jnp.int32)
    dst_ids = plant(jax.random.randint(streams_of[5], (N_ROW, N_COL, EDEV), 0, VS * N_ROW), jax.random.fold_in(streams_of[5], 1), 0, (VS * N_ROW) - 1).astype(jnp.int32)
    rel_ids = plant(jax.random.randint(streams_of[6], (N_ROW, N_COL, EDEV), 0, RELS), jax.random.fold_in(streams_of[6], 1), 0, RELS - 1).astype(jnp.int32)
    edge_norm = jnp.clip(jnp.exp(math.log(1.0) - 2.3025851 * jax.random.uniform(streams_of[7], (N_ROW, N_COL, EDEV), jnp.float32) ** level_of(streams_of[7], (N_ROW, N_COL, EDEV), ((0, 8), (1, 4)), -0.2, 0.2)), 0.1, 1.0)
    block_fill = draw_block_fill(jax.random.fold_in(streams_of[9], 71), 0)
    return dict(node_feats=node_feats, dest_grad=dest_grad, bases=bases, coefs=coefs, src_ids=src_ids, dst_ids=dst_ids, rel_ids=rel_ids, edge_norm=edge_norm, block_fill=block_fill)


def reference(node_feats, dest_grad, bases, coefs, src_ids, dst_ids, rel_ids, edge_norm, block_fill):
    verts = node_feats.shape[0]
    width = node_feats.shape[1]
    targets_all = dest_grad.reshape(verts, width)
    slot = jnp.arange(EDEV, dtype=jnp.int32)
    position = slot % EDGE_BLOCK
    which = slot // EDGE_BLOCK
    fills = jnp.take(block_fill, which, axis=2)
    live_mask = (position[None, None, :] < fills).astype(jnp.float32)
    weights = (edge_norm * live_mask).reshape(-1, EDEV)
    row_base = (jnp.arange(N_ROW, dtype=jnp.int32) * (VS * N_COL))[:, None, None]
    col_base = (jnp.arange(N_COL, dtype=jnp.int32) * (VS * N_ROW))[None, :, None]
    sources = (src_ids + row_base).astype(jnp.int32).reshape(-1, EDEV)
    targets = (dst_ids + col_base).astype(jnp.int32).reshape(-1, EDEV)
    relations = rel_ids.reshape(-1, EDEV)
    bases_wide = bases.astype(jnp.float32)

    def step(carry, block):
        node_part, coef_part, basis_part = carry
        weight, source, target, relation = block
        edge_grad = (weight[:, None] * targets_all[target].astype(jnp.float32)).astype(jnp.bfloat16)
        edge_rows = node_feats[source]
        edge_coefs = coefs[relation].astype(jnp.float32)
        backed = jnp.einsum('em,bkm->ebk', edge_grad.astype(jnp.float32), bases_wide)
        per_edge = jnp.sum(edge_coefs[:, :, None] * backed, axis=1)
        inner = jnp.sum(backed * edge_rows.astype(jnp.float32)[:, None, :], axis=2)
        basis_rows = (edge_coefs[:, :, None] * edge_rows.astype(jnp.float32)[:, None, :]).reshape(EDEV, BASES * D).astype(jnp.bfloat16)
        node_part = node_part + jax.ops.segment_sum(per_edge, source, num_segments=verts)
        coef_part = coef_part + jax.ops.segment_sum(inner, relation, num_segments=RELS)
        basis_part = basis_part + jnp.dot(basis_rows.T, edge_grad, preferred_element_type=jnp.float32)
        return (node_part, coef_part, basis_part), None

    start = (jnp.zeros((verts, width), jnp.float32), jnp.zeros((RELS, BASES), jnp.float32), jnp.zeros((BASES * D, D), jnp.float32))
    (node_part, coef_part, basis_part), _ = lax.scan(step, start, (weights, sources, targets, relations))
    return node_part.astype(jnp.bfloat16), basis_part / N_COL, coef_part / N_COL
```

```python
import functools
import jax
import jax.numpy as jnp
from jax import lax
from jax.experimental import pallas as pl
from jax.experimental.pallas import tpu as pltpu
from jax.sharding import PartitionSpec as P

EDGE_BLOCK = 128
TILE = 16
LANES = 128
PAIR = 2
F32 = jnp.float32
BF16 = jnp.bfloat16
I32 = jnp.int32
VMEM_LIMIT = 56 * 1024 * 1024


def round_up(value, unit):
    return (value + unit - 1) // unit * unit


def split_index(ids, size):
    if size & (size - 1) == 0:
        shift = size.bit_length() - 1
        return ids >> shift, ids & (size - 1)
    return ids // size, ids % size


def wrap(difference, size):
    return jnp.where(difference < 0, difference + size, difference)


def one_hot(ids, depth):
    rows = lax.broadcasted_iota(I32, (depth, ids.shape[1]), 0)
    return jnp.where(rows == ids, 1.0, 0.0).astype(BF16)


def eye(width):
    first = lax.broadcasted_iota(I32, (width, width), 0)
    second = lax.broadcasted_iota(I32, (width, width), 1)
    return jnp.where(first == second, 1.0, 0.0).astype(BF16)


def dot(left, right):
    return lax.dot_general(left, right, (((1,), (0,)), ((), ())), preferred_element_type=F32)


def dot_t(left, right):
    return lax.dot_general(left, right, (((1,), (1,)), ((), ())), preferred_element_type=F32)


def tree_sum(values):
    if len(values) == 1:
        return values[0]
    return tree_sum(values[0::2]) + tree_sum(values[1::2])


def vmem():
    return pl.BlockSpec(memory_space=pltpu.VMEM)


def smem():
    return pl.BlockSpec(memory_space=pltpu.SMEM)


def call(body, out_shape, n_in, scratch, flops, name):
    many = isinstance(out_shape, (tuple, list))
    moved = 1 << 22
    return pl.pallas_call(
        body,
        out_shape=out_shape,
        in_specs=[smem()] + [vmem()] * n_in,
        out_specs=[vmem()] * len(out_shape) if many else vmem(),
        scratch_shapes=scratch,
        compiler_params=pltpu.CompilerParams(vmem_limit_bytes=VMEM_LIMIT),
        cost_estimate=pl.CostEstimate(flops=flops, bytes_accessed=moved, transcendentals=0),
        name=name,
    )


def source_kernel(
    sizes, place, meta, meta_core, feats, feats_core, coefs, xt_ref, ct_ref, table
):
    cols, shard, span, heads, padded = sizes
    count = cols // PAIR
    y, core = place[2], place[3]
    width = feats.shape[-1]
    edges = meta.shape[-1]
    unit = eye(width)
    for far, block in enumerate((feats, feats_core)):
        for sy in range(count):
            for xr in range(PAIR):
                at = (far * count + sy) * shard
                table[xr, :, at : at + shard] = dot_t(unit, block[sy, xr]).astype(BF16)
    for far, source in enumerate((meta, meta_core)):

        def step(index, carry, far=far, source=source):
            xr = index // (edges // span)
            at = pl.multiple_of(index % (edges // span) * span, span)
            ids = source[xr, 0:1, pl.ds(at, span)].astype(I32)
            owner, local = split_index(ids, shard)
            owner_y, owner_core = split_index(owner, PAIR)
            slot = (owner_core ^ core) * count + wrap(y - owner_y, count)
            rows = dot(table[xr], one_hot(slot * shard + local, cols * shard))
            xt_ref[far * PAIR + xr, :, pl.ds(at, span)] = rows.astype(BF16)
            relation = source[xr, 2:3, pl.ds(at, span)].astype(I32)
            high, low = split_index(relation, LANES)
            parts = dot(coefs[...], one_hot(low, LANES))
            total = jnp.zeros((padded, span), F32)
            for head in range(heads):
                total = total + jnp.where(
                    high == head, parts[head * padded : (head + 1) * padded], 0.0
                )
            ct_ref[far * PAIR + xr, :, pl.ds(at, span)] = total
            return carry

        lax.fori_loop(0, PAIR * (edges // span), step, 0)


def grad_kernel(sizes, place, meta, *refs):
    rows_total, shard, span = sizes
    count = rows_total // PAIR
    blocks = refs[:rows_total]
    gt_ref, table = refs[rows_total:]
    a, x = place[0], place[1]
    width = blocks[0].shape[-1]
    edges = meta.shape[-1]
    unit = eye(width)
    for at, block in enumerate(blocks):
        table[:, at * shard : (at + 1) * shard] = dot_t(unit, block[...]).astype(BF16)

    def step(index, carry):
        xr = index // (edges // span)
        at = pl.multiple_of(index % (edges // span) * span, span)
        ids = meta[xr, 1:2, pl.ds(at, span)].astype(I32)
        owner, local = split_index(ids, shard)
        owner_a, owner_x = split_index(owner, PAIR)
        slot = (owner_x ^ x) * count + wrap(a - owner_a, count)
        rows = dot(table[...], one_hot(slot * shard + local, rows_total * shard))
        weight = meta[xr, 3:4, pl.ds(at, span)]
        gt_ref[:, pl.ds(pl.multiple_of(index * span, span), span)] = (rows * weight).astype(BF16)
        return carry

    lax.fori_loop(0, PAIR * (edges // span), step, 0)


def forward_kernel(
    sizes, place, meta, gt_ref, xt_ref, ct_ref, bases_ref, out_ref, total, inner, wide, coef_sum
):
    cols, shard, span, heads, padded = sizes
    count = cols // PAIR
    y, core = place[2], place[3]
    edges = meta.shape[-1]
    width = bases_ref.shape[-1]
    group = bases_ref.shape[0]
    step = pl.program_id(0)

    @pl.when(step == 0)
    def _():
        total[...] = jnp.zeros_like(total)
        inner[...] = jnp.zeros_like(inner)

    def chunk(index, carry):
        at = pl.ds(pl.multiple_of(index * span, span), span)
        grads = gt_ref[:, at]
        rows = xt_ref[0, :, at].astype(F32)
        sums = total[:, at]
        for t in range(group):
            base = step * group + t
            backed = dot(bases_ref[t], grads)
            sums = sums + ct_ref[0, pl.ds(base, 1), at] * backed
            inner[pl.ds(base, 1), at] = jnp.sum(backed * rows, axis=0, keepdims=True)
        total[:, at] = sums
        return carry

    lax.fori_loop(0, edges // span, chunk, 0)

    @pl.when(step == pl.num_programs(0) - 1)
    def _():
        ids = meta[0, 0:1, :].astype(I32)
        owner, local = split_index(ids, shard)
        owner_y, owner_core = split_index(owner, PAIR)
        slot = (owner_core ^ core) * count + wrap(owner_y - y, count)
        place_of = slot * shard + local
        values = total[...].astype(BF16)
        for at in range(cols):
            hot = one_hot(place_of - at * shard, shard)
            out_ref[at, 0:shard, :] = dot_t(hot, values).astype(BF16)
        high, low = split_index(meta[0, 2:3, :].astype(I32), LANES)
        for head in range(heads):
            wide[head * padded : (head + 1) * padded, :] = jnp.where(
                high == head, inner[...], 0.0
            ).astype(BF16)
        coef_sum[...] = dot_t(wide[...], one_hot(low, LANES))
        share = heads * padded // cols
        half = share // 2
        for far in range(PAIR):
            for sy in range(count):
                target = (y + sy) % count * PAIR + (core ^ far)
                for side in range(2):
                    rows = coef_sum[pl.ds(pl.multiple_of(target * share + side * half, 8), half), :]
                    out_ref[
                        far * count + sy,
                        shard : shard + half,
                        side * LANES : (side + 1) * LANES,
                    ] = rows.astype(BF16)


def basis_kernel(sizes, place, gt_ref, gt_core, xt_ref, ct_ref, *refs):
    rows_total, cols, block, groups, basis_count, span = sizes
    a_count, y_count = rows_total // PAIR, cols // PAIR
    a, x, y, core = place[0], place[1], place[2], place[3]
    outs = refs[: 1 + (y_count - 1) * a_count]
    acc, left, tiles = refs[len(outs) :]
    width, edges = xt_ref.shape[1], xt_ref.shape[2]
    tiles_wide = width // TILE
    cover = groups * TILE
    steps = edges // span
    acc[...] = jnp.zeros_like(acc)
    for far, grads in enumerate((gt_ref, gt_core)):

        def step(index, carry, far=far, grads=grads):
            part = far * PAIR + index // steps
            at = pl.ds(pl.multiple_of(index % steps * span, span), span)
            for b in range(basis_count):
                row = ct_ref[part, b : b + 1, at]
                tiles[b] = jnp.broadcast_to(row, (TILE, span)).astype(BF16)
            for sy in range(y_count):
                for sz in range(a_count):
                    owner = ((a + sz) % a_count * PAIR + x) * cols + (y + sy) % y_count * PAIR + core
                    first = owner * block // TILE
                    for q in range(groups):
                        tile = jnp.minimum(first + q, basis_count * tiles_wide - 1)
                        lower = pl.multiple_of(tile % tiles_wide * TILE, TILE)
                        to = ((sy * a_count + sz) * groups + q) * TILE
                        left[to : to + TILE, :] = (
                            tiles[tile // tiles_wide] * xt_ref[part, pl.ds(lower, TILE), at]
                        )
            here = pl.ds(pl.multiple_of(index * span, span), span)
            acc[...] += dot_t(left[...], grads[:, here])
            return carry

        lax.fori_loop(0, PAIR * steps, step, 0)
    for sz in range(a_count):
        outs[0][sz] = acc[sz * cover : (sz + 1) * cover, :]
    for sy in range(1, y_count):
        for sz in range(a_count):
            at = (sy * a_count + sz) * cover
            outs[1 + (sy - 1) * a_count + sz][...] = acc[at : at + cover, :].astype(BF16)


def coef_kernel(sizes, place, *refs):
    cols, heads, padded, divisor = sizes
    count = cols // PAIR
    parts, (out_ref, whole) = refs[:cols], refs[cols:]
    y, core = place[2], place[3]
    share = heads * padded // cols
    half = share // 2
    for far in range(PAIR):
        for sy in range(count):
            target = wrap(y - sy, count) * PAIR + (core ^ far)
            for side in range(2):
                whole[pl.ds(pl.multiple_of(target * share + side * half, 8), half), :] = (
                    parts[far * count + sy][:, side * LANES : (side + 1) * LANES]
                )
    total, width = out_ref.shape
    for head in range(heads):
        piece = whole[head * padded : (head + 1) * padded, :].T
        live = min(LANES, total - head * LANES)
        out_ref[head * LANES : head * LANES + live, :] = piece[:live, :width] / divisor


def on_device(
    node_feats, dest_grad, bases, coefs, src_ids, dst_ids, rel_ids, edge_norm, block_fill
):
    rows_total = lax.axis_size("row")
    cols = lax.axis_size("col")
    a_count, y_count = rows_total // PAIR, cols // PAIR
    shard, width = node_feats.shape
    basis_count = bases.shape[0]
    relation_count = coefs.shape[0]
    edges = src_ids.size
    padded = round_up(basis_count, TILE)
    heads = round_up(relation_count, LANES) // LANES
    while heads * padded % (cols * 2 * TILE):
        heads += 1
    span = 256
    i = lax.axis_index("row")
    j = lax.axis_index("col")
    place = jnp.stack([i // PAIR, i % PAIR, j // PAIR, j % PAIR]).astype(I32)

    def flip_x(value):
        return lax.ppermute(value, "row", [(r, r ^ 1) for r in range(rows_total)])

    def flip_core(value):
        return lax.ppermute(value, "col", [(c, c ^ 1) for c in range(cols)])

    def turn_z(value, by):
        return lax.ppermute(
            value, "row", [(r, (r + by * PAIR) % rows_total) for r in range(rows_total)]
        )

    def turn_y(value, by):
        return lax.ppermute(value, "col", [(c, (c + by * PAIR) % cols) for c in range(cols)])

    own_dest = dest_grad[0]
    dest = [own_dest] + [turn_z(own_dest, s) for s in range(1, a_count)]
    dest = dest + [flip_x(value) for value in dest]

    fills = block_fill.reshape(-1)
    position = lax.broadcasted_iota(I32, (fills.shape[0], EDGE_BLOCK), 1)
    live = (position < fills[:, None]).reshape(-1).astype(F32)
    weights = edge_norm.reshape(-1) * live
    meta = jnp.stack(
        [
            src_ids.reshape(-1).astype(F32),
            dst_ids.reshape(-1).astype(F32),
            rel_ids.reshape(-1).astype(F32),
            weights,
        ]
    )
    meta = jnp.stack([meta, flip_x(meta)])
    meta_core = flip_core(meta)

    feats = jnp.stack([node_feats, flip_x(node_feats)])
    feats = jnp.stack([feats] + [turn_y(feats, s) for s in range(1, y_count)])
    feats_core = flip_core(feats)

    table = jnp.pad(coefs, ((0, heads * LANES - relation_count), (0, padded - basis_count)))
    table = table.reshape(heads, LANES, padded).transpose(0, 2, 1).reshape(heads * padded, LANES)

    xt, ct = call(
        functools.partial(source_kernel, (cols, shard, span, heads, padded)),
        (
            jax.ShapeDtypeStruct((2 * PAIR, width, edges), BF16),
            jax.ShapeDtypeStruct((2 * PAIR, padded, edges), F32),
        ),
        5,
        [pltpu.VMEM((PAIR, width, cols * shard), BF16)],
        2 * 4 * edges * cols * shard * width,
        "source_rows",
    )(place, meta, meta_core, feats, feats_core, table)

    dest_shard = own_dest.shape[0]
    gt = call(
        functools.partial(grad_kernel, (rows_total, dest_shard, span)),
        jax.ShapeDtypeStruct((width, PAIR * edges), BF16),
        1 + rows_total,
        [pltpu.VMEM((width, rows_total * dest_shard), BF16)],
        2 * 2 * edges * rows_total * dest_shard * width,
        "edge_grads",
    )(place, meta, *dest)
    gt_core = flip_core(gt)

    group = max(g for g in range(1, 6) if basis_count % g == 0)
    share_rows = heads * padded // cols // 2
    packed = pl.pallas_call(
        functools.partial(forward_kernel, (cols, shard, span, heads, padded)),
        grid=(basis_count // group,),
        in_specs=[
            smem(),
            pl.BlockSpec(meta.shape, lambda s: (0, 0, 0)),
            pl.BlockSpec((width, edges), lambda s: (0, 0)),
            pl.BlockSpec((1, width, edges), lambda s: (0, 0, 0)),
            pl.BlockSpec((1, padded, edges), lambda s: (0, 0, 0)),
            pl.BlockSpec((group, width, width), lambda s: (s, 0, 0)),
        ],
        out_specs=pl.BlockSpec((cols, shard + share_rows, width), lambda s: (0, 0, 0)),
        out_shape=jax.ShapeDtypeStruct((cols, shard + share_rows, width), BF16),
        scratch_shapes=[
            pltpu.VMEM((width, edges), F32),
            pltpu.VMEM((padded, edges), F32),
            pltpu.VMEM((heads * padded, edges), BF16),
            pltpu.VMEM((heads * padded, LANES), F32),
        ],
        compiler_params=pltpu.CompilerParams(vmem_limit_bytes=VMEM_LIMIT),
        cost_estimate=pl.CostEstimate(
            flops=2 * edges * width * width * basis_count,
            bytes_accessed=bases.size * 2,
            transcendentals=0,
        ),
        name="backed_sums",
    )(place, meta, gt, xt, ct, bases)

    block = basis_count * width // (rows_total * cols)
    cover = block if block % TILE == 0 else round_up(block, TILE) + TILE
    pieces = call(
        functools.partial(
            basis_kernel, (rows_total, cols, block, cover // TILE, basis_count, 2 * span)
        ),
        [jax.ShapeDtypeStruct((a_count, cover, width), F32)]
        + [jax.ShapeDtypeStruct((cover, width), BF16)] * ((y_count - 1) * a_count),
        4,
        [
            pltpu.VMEM((y_count * a_count * cover, width), F32),
            pltpu.VMEM((y_count * a_count * cover, 2 * span), BF16),
            pltpu.VMEM((padded, TILE, 2 * span), BF16),
        ],
        2 * 4 * edges * y_count * a_count * cover * width,
        "basis_terms",
    )(place, gt, gt_core, xt, ct)
    kept, sent = pieces[0], pieces[1:]

    got = {}
    order = list(range(1, a_count)) + [0]
    for sz in order:
        for sy in range(1, y_count):
            got[sz, sy] = turn_y(sent[(sy - 1) * a_count + sz], sy)
    basis_sum = None
    arrived = []
    for sz in order:
        value = kept[sz]
        for sy in range(1, y_count):
            value = value + got[sz, sy].astype(F32)
        if sz:
            arrived.append(turn_z(value.astype(BF16), sz))
        else:
            basis_sum = value
    for value in arrived:
        basis_sum = basis_sum + value.astype(F32)
    if cover != block:
        owner = i * cols + j
        basis_sum = lax.dynamic_slice_in_dim(basis_sum, owner * block % TILE, block, axis=0)
    basis_grad = basis_sum / cols

    joined = packed[0].astype(F32)
    for far in range(PAIR):
        for sy in range(y_count):
            if far or sy:
                target = [
                    (c, ((c // PAIR + sy) % y_count) * PAIR + (c % PAIR ^ far)) for c in range(cols)
                ]
                joined = joined + lax.ppermute(packed[far * y_count + sy], "col", target).astype(
                    F32
                )
    node_grad = joined[:shard].astype(BF16)
    coef_part = joined[shard:]
    low = coef_part.astype(BF16)
    low = (low.astype(F32) + flip_x(low).astype(F32)).astype(BF16)
    coef_part = tree_sum([low.astype(F32)] + [turn_z(low, s).astype(F32) for s in range(1, a_count)])
    shares = []
    for far in range(PAIR):
        for sy in range(y_count):
            target = [
                (c, ((c // PAIR + sy) % y_count) * PAIR + (c % PAIR ^ far)) for c in range(cols)
            ]
            shares.append(lax.ppermute(coef_part, "col", target) if far or sy else coef_part)
    coef_grad = call(
        functools.partial(coef_kernel, (cols, heads, padded, cols)),
        jax.ShapeDtypeStruct((relation_count, basis_count), F32),
        cols,
        [pltpu.VMEM((heads * padded, LANES), F32)],
        1 << 20,
        "coef_rows",
    )(place, *shares)
    return (node_grad, basis_grad, coef_grad)


def solution(mesh):
    in_specs = (
        P(("row", "col"), None),
        P("col", "row", None),
        P(),
        P(),
        P("row", "col", None),
        P("row", "col", None),
        P("row", "col", None),
        P("row", "col", None),
        P("row", "col", None),
    )
    out_specs = (P(("row", "col"), None), P(("row", "col"), None), P())
    return jax.shard_map(
        on_device, mesh=mesh, in_specs=in_specs, out_specs=out_specs, check_vma=False
    )
```

```python
import functools
import jax
import jax.numpy as jnp
from jax import lax
from jax.experimental import pallas as pl
from jax.experimental.pallas import tpu as pltpu
from jax.sharding import PartitionSpec as P

EDGE_BLOCK = 128
TILE = 16
LANES = 128
PAIR = 2
F32 = jnp.float32
BF16 = jnp.bfloat16
I32 = jnp.int32
VMEM_LIMIT = 56 * 1024 * 1024


def round_up(value, unit):
    return (value + unit - 1) // unit * unit


def split_index(ids, size):
    if size & (size - 1) == 0:
        shift = size.bit_length() - 1
        return ids >> shift, ids & (size - 1)
    return ids // size, ids % size


def wrap(difference, size):
    return jnp.where(difference < 0, difference + size, difference)


def one_hot(ids, depth):
    if depth <= 256:
        rows = lax.broadcasted_iota(I32, (depth, ids.shape[1]), 0).astype(F32).astype(BF16)
        one, zero = jnp.ones((), BF16), jnp.zeros((), BF16)
        return jnp.where(rows == ids.astype(F32).astype(BF16), one, zero)
    rows = lax.broadcasted_iota(I32, (depth, ids.shape[1]), 0)
    return jnp.where(rows == ids, 1.0, 0.0).astype(BF16)


def slot_hot(slot, local, slots, depth):
    return jnp.concatenate(
        [one_hot(jnp.where(slot == at, local, -1), depth) for at in range(slots)], axis=0
    )


def eye(width):
    first = lax.broadcasted_iota(I32, (width, width), 0)
    second = lax.broadcasted_iota(I32, (width, width), 1)
    return jnp.where(first == second, 1.0, 0.0).astype(BF16)


def dot(left, right):
    return lax.dot_general(left, right, (((1,), (0,)), ((), ())), preferred_element_type=F32)


def dot_t(left, right):
    return lax.dot_general(left, right, (((1,), (1,)), ((), ())), preferred_element_type=F32)


def tree_sum(values):
    if len(values) == 1:
        return values[0]
    return tree_sum(values[0::2]) + tree_sum(values[1::2])


def vmem():
    return pl.BlockSpec(memory_space=pltpu.VMEM)


def smem():
    return pl.BlockSpec(memory_space=pltpu.SMEM)


def call(body, out_shape, n_in, scratch, flops, name, unread=0):
    many = isinstance(out_shape, (tuple, list))
    moved = 1 << 22
    return pl.pallas_call(
        body,
        out_shape=out_shape,
        in_specs=[smem()] + [vmem()] * n_in + [pl.BlockSpec(memory_space=pl.ANY)] * unread,
        out_specs=[vmem()] * len(out_shape) if many else vmem(),
        scratch_shapes=scratch,
        compiler_params=pltpu.CompilerParams(vmem_limit_bytes=VMEM_LIMIT),
        cost_estimate=pl.CostEstimate(flops=flops, bytes_accessed=moved, transcendentals=0),
        name=name,
    )


def prepare_kernel(fills, src, dst, rel, norm, out_ref):
    blocks = fills.shape[-1]
    out_ref[0:1, :] = src[0].astype(F32)
    out_ref[1:2, :] = dst[0].astype(F32)
    out_ref[2:3, :] = rel[0].astype(F32)
    lane = lax.broadcasted_iota(I32, (1, EDGE_BLOCK), 1)
    for at in range(blocks):
        here = slice(at * EDGE_BLOCK, (at + 1) * EDGE_BLOCK)
        live = jnp.where(lane < fills[0, 0, at], 1.0, 0.0)
        out_ref[3:4, here] = norm[0, :, here] * live


def source_kernel(sizes, place, meta, meta_core, feats, feats_core, coefs_t, *refs):
    cols, shard, span, heads, padded, extra = sizes
    xt_ref, ct_ref, table, coefs = refs[extra:]
    count = cols // PAIR
    y, core = place[2], place[3]
    width = feats.shape[-1]
    edges = meta.shape[-1]
    basis_count, relation_count = coefs_t.shape
    unit = eye(width)
    for far, block in enumerate((feats, feats_core)):
        for sy in range(count):
            for xr in range(PAIR):
                at = (far * count + sy) * shard
                table[xr, :, at : at + shard] = dot_t(unit, block[sy, xr]).astype(BF16)
    coefs[...] = jnp.zeros_like(coefs)
    for head in range(heads):
        live = min(LANES, relation_count - head * LANES)
        if live > 0:
            coefs[head * padded : head * padded + basis_count, 0:live] = coefs_t[
                :, head * LANES : head * LANES + live
            ]
    for far, source in enumerate((meta, meta_core)):

        def step(index, carry, far=far, source=source):
            xr = index // (edges // span)
            at = pl.multiple_of(index % (edges // span) * span, span)
            ids = source[xr, 0:1, pl.ds(at, span)].astype(I32)
            owner, local = split_index(ids, shard)
            owner_y, owner_core = split_index(owner, PAIR)
            slot = (owner_core ^ core) * count + wrap(y - owner_y, count)
            rows = dot(table[xr], slot_hot(slot, local, cols, shard))
            xt_ref[far * PAIR + xr, :, pl.ds(at, span)] = rows.astype(BF16)
            relation = source[xr, 2:3, pl.ds(at, span)].astype(I32)
            high, low = split_index(relation, LANES)
            parts = dot(coefs[...], one_hot(low, LANES))
            total = jnp.zeros((padded, span), F32)
            for head in range(heads):
                total = total + jnp.where(
                    high == head, parts[head * padded : (head + 1) * padded], 0.0
                )
            ct_ref[far * PAIR + xr, :, pl.ds(at, span)] = total
            return carry

        lax.fori_loop(0, PAIR * (edges // span), step, 0, unroll=2)


def grad_kernel(sizes, place, meta, *refs):
    rows_total, shard, span = sizes
    count = rows_total // PAIR
    blocks = refs[:rows_total]
    gt_ref, table = refs[rows_total + 1 :]
    a, x = place[0], place[1]
    width = blocks[0].shape[-1]
    edges = meta.shape[-1]
    unit = eye(width)
    for at, block in enumerate(blocks):
        table[:, at * shard : (at + 1) * shard] = dot_t(unit, block[...]).astype(BF16)

    def step(index, carry):
        xr = index // (edges // span)
        at = pl.multiple_of(index % (edges // span) * span, span)
        ids = meta[xr, 1:2, pl.ds(at, span)].astype(I32)
        owner, local = split_index(ids, shard)
        owner_a, owner_x = split_index(owner, PAIR)
        slot = (owner_x ^ x) * count + wrap(a - owner_a, count)
        rows = dot(table[...], slot_hot(slot, local, rows_total, shard))
        weight = meta[xr, 3:4, pl.ds(at, span)]
        gt_ref[:, pl.ds(pl.multiple_of(index * span, span), span)] = (rows * weight).astype(BF16)
        return carry

    lax.fori_loop(0, PAIR * (edges // span), step, 0, unroll=2)


def forward_kernel(
    sizes, place, meta, gt_ref, xt_ref, ct_ref, bases_ref, *refs
):
    cols, shard, span, heads, padded = sizes
    outs = refs[:cols]
    total, inner, wide, coef_sum = refs[cols:]
    count = cols // PAIR
    y, core = place[2], place[3]
    edges = meta.shape[-1]
    width = bases_ref.shape[-1]
    group = bases_ref.shape[0]
    step = pl.program_id(0)

    @pl.when(step == 0)
    def _():
        total[...] = jnp.zeros_like(total)
        inner[...] = jnp.zeros_like(inner)

    stacked = bases_ref[...].reshape(group * width, width)
    for index in range(edges // span):
        at = slice(index * span, (index + 1) * span)
        backed = dot(stacked, gt_ref[:, at])
        rows = xt_ref[0, :, at].astype(F32)
        sums = total[:, at]
        for t in range(group):
            base = step * group + t
            mine = backed[t * width : (t + 1) * width]
            sums = sums + ct_ref[0, pl.ds(base, 1), at] * mine
            inner[pl.ds(base, 1), at] = jnp.sum(mine * rows, axis=0, keepdims=True)
        total[:, at] = sums

    @pl.when(step == pl.num_programs(0) - 1)
    def _():
        ids = meta[0, 0:1, :].astype(I32)
        owner, local = split_index(ids, shard)
        owner_y, owner_core = split_index(owner, PAIR)
        slot = (owner_core ^ core) * count + wrap(owner_y - y, count)
        values = total[...].astype(BF16)
        for at in range(cols):
            hot = one_hot(jnp.where(slot == at, local, -1), shard)
            outs[at][0:shard, :] = dot_t(hot, values).astype(BF16)
        high, low = split_index(meta[0, 2:3, :].astype(I32), LANES)
        for head in range(heads):
            wide[head * padded : (head + 1) * padded, :] = jnp.where(
                high == head, inner[...], 0.0
            ).astype(BF16)
        coef_sum[...] = dot_t(wide[...], one_hot(low, LANES))
        share = heads * padded // cols
        half = share // 2
        for far in range(PAIR):
            for sy in range(count):
                target = (y + sy) % count * PAIR + (core ^ far)
                for side in range(2):
                    rows = coef_sum[pl.ds(pl.multiple_of(target * share + side * half, 8), half), :]
                    outs[far * count + sy][
                        shard : shard + half, side * LANES : (side + 1) * LANES
                    ] = rows.astype(BF16)


def basis_kernel(sizes, place, gt_ref, gt_core, xt_ref, ct_ref, *refs):
    rows_total, cols, block, groups, basis_count, span, turns = sizes
    a_count, y_count = rows_total // PAIR, cols // PAIR
    a, x, y, core = place[0], place[1], place[2], place[3]
    outs = refs[: y_count * len(turns)]
    acc, left_even, left_odd, tiles = refs[len(outs) :]
    width, edges = xt_ref.shape[1], xt_ref.shape[2]
    tiles_wide = width // TILE
    cover = groups * TILE
    spread = tiles.shape[0] // len(outs)
    steps = edges // span
    firsts = []
    for sz in turns:
        for sy in range(y_count):
            owner = ((a + sz) % a_count * PAIR + x) * cols + (y + sy) % y_count * PAIR + core
            firsts.append(owner * block // TILE)

    def build(part, at, left):
        for order, first in enumerate(firsts):
            base = first // tiles_wide
            for extra in range(spread):
                row = ct_ref[part, pl.ds(jnp.minimum(base + extra, basis_count - 1), 1), at]
                tiles[order * spread + extra] = jnp.broadcast_to(row, (TILE, span)).astype(BF16)
            for q in range(groups):
                tile = jnp.minimum(first + q, basis_count * tiles_wide - 1)
                lower = pl.multiple_of(tile % tiles_wide * TILE, TILE)
                to = (order * groups + q) * TILE
                left[to : to + TILE, :] = (
                    tiles[order * spread + tile // tiles_wide - base]
                    * xt_ref[part, pl.ds(lower, TILE), at]
                )

    for index in range(2 * PAIR * steps):
        part = index // steps
        at = slice(index % steps * span, (index % steps + 1) * span)
        left = left_even if index % 2 == 0 else left_odd
        build(part, at, left)
        grads = gt_ref if part < PAIR else gt_core
        here = index % (PAIR * steps) * span
        term = dot_t(left[...], grads[:, here : here + span])
        if index:
            acc[...] += term
        else:
            acc[...] = term
    for order, out in enumerate(outs):
        out[...] = acc[order * cover : (order + 1) * cover, :].astype(out.dtype)


def coef_kernel(sizes, place, *refs):
    cols, heads, padded, divisor = sizes
    count = cols // PAIR
    parts, (out_ref, whole) = refs[:cols], refs[cols:]
    y, core = place[2], place[3]
    share = heads * padded // cols
    half = share // 2
    for far in range(PAIR):
        for sy in range(count):
            target = wrap(y - sy, count) * PAIR + (core ^ far)
            for side in range(2):
                whole[pl.ds(pl.multiple_of(target * share + side * half, 8), half), :] = (
                    parts[far * count + sy][:, side * LANES : (side + 1) * LANES]
                )
    width, total = out_ref.shape
    for head in range(heads):
        live = min(LANES, total - head * LANES)
        if live > 0:
            out_ref[:, head * LANES : head * LANES + live] = (
                whole[head * padded : head * padded + width, 0:live] / divisor
            )


def on_device(
    node_feats, dest_grad, bases, coefs, src_ids, dst_ids, rel_ids, edge_norm, block_fill
):
    rows_total = lax.axis_size("row")
    cols = lax.axis_size("col")
    a_count, y_count = rows_total // PAIR, cols // PAIR
    shard, width = node_feats.shape
    basis_count = bases.shape[0]
    relation_count = coefs.shape[0]
    edges = src_ids.size
    padded = round_up(basis_count, TILE)
    heads = round_up(relation_count, LANES) // LANES
    while heads * padded % (cols * 2 * TILE):
        heads += 1
    span = 256
    i = lax.axis_index("row")
    j = lax.axis_index("col")
    place = jnp.stack([i // PAIR, i % PAIR, j // PAIR, j % PAIR]).astype(I32)

    def flip_x(value):
        return lax.ppermute(value, "row", [(r, r ^ 1) for r in range(rows_total)])

    def flip_core(value):
        return lax.ppermute(value, "col", [(c, c ^ 1) for c in range(cols)])

    def turn_z(value, by):
        return lax.ppermute(
            value, "row", [(r, (r + by * PAIR) % rows_total) for r in range(rows_total)]
        )

    def turn_y(value, by):
        return lax.ppermute(value, "col", [(c, (c + by * PAIR) % cols) for c in range(cols)])

    own_dest = dest_grad[0]
    dest = [own_dest] + [turn_z(own_dest, s) for s in range(1, a_count)]
    across = [flip_x(own_dest)]
    near = flip_x(node_feats)

    meta = pl.pallas_call(
        prepare_kernel,
        out_shape=jax.ShapeDtypeStruct((4, edges), F32),
        in_specs=[smem()] + [vmem()] * 4,
        out_specs=vmem(),
        name="edge_table",
    )(block_fill, src_ids, dst_ids, rel_ids, edge_norm)
    meta = jnp.stack([meta, flip_x(meta)])
    meta_core = flip_core(meta)

    feats = jnp.stack([node_feats, near])
    feats, across[0] = lax.optimization_barrier((feats, across[0]))
    feats = jnp.stack([feats] + [turn_y(feats, s) for s in range(1, y_count)])
    across += [flip_x(value) for value in dest[1:]]
    feats_core = flip_core(feats)

    xt, ct = call(
        functools.partial(source_kernel, (cols, shard, span, heads, padded, a_count)),
        (
            jax.ShapeDtypeStruct((2 * PAIR, width, edges), BF16),
            jax.ShapeDtypeStruct((2 * PAIR, padded, edges), F32),
        ),
        5,
        [
            pltpu.VMEM((PAIR, width, cols * shard), BF16),
            pltpu.VMEM((heads * padded, LANES), BF16),
        ],
        2 * 4 * edges * cols * shard * width,
        "source_rows",
        a_count,
    )(place, meta, meta_core, feats, feats_core, coefs.T, *dest)

    dest_shard = own_dest.shape[0]
    gt = call(
        functools.partial(grad_kernel, (rows_total, dest_shard, span)),
        jax.ShapeDtypeStruct((width, PAIR * edges), BF16),
        1 + rows_total,
        [pltpu.VMEM((width, rows_total * dest_shard), BF16)],
        2 * 2 * edges * rows_total * dest_shard * width,
        "edge_grads",
        1,
    )(place, meta, *dest, *across, xt)
    gt_core = flip_core(gt)

    group = max(g for g in range(1, 6) if basis_count % g == 0)
    share_rows = heads * padded // cols // 2
    packed = pl.pallas_call(
        functools.partial(forward_kernel, (cols, shard, span, heads, padded)),
        grid=(basis_count // group,),
        in_specs=[
            smem(),
            pl.BlockSpec(meta.shape, lambda s: (0, 0, 0)),
            pl.BlockSpec((width, edges), lambda s: (0, 0)),
            pl.BlockSpec((1, width, edges), lambda s: (0, 0, 0)),
            pl.BlockSpec((1, padded, edges), lambda s: (0, 0, 0)),
            pl.BlockSpec((group, width, width), lambda s: (s, 0, 0)),
        ],
        out_specs=[pl.BlockSpec((shard + share_rows, width), lambda s: (0, 0))] * cols,
        out_shape=[jax.ShapeDtypeStruct((shard + share_rows, width), BF16)] * cols,
        scratch_shapes=[
            pltpu.VMEM((width, edges), F32),
            pltpu.VMEM((padded, edges), F32),
            pltpu.VMEM((heads * padded, edges), BF16),
            pltpu.VMEM((heads * padded, LANES), F32),
        ],
        compiler_params=pltpu.CompilerParams(vmem_limit_bytes=VMEM_LIMIT),
        cost_estimate=pl.CostEstimate(
            flops=2 * edges * width * width * basis_count,
            bytes_accessed=bases.size * 2,
            transcendentals=0,
        ),
        name="backed_sums",
    )(place, meta, gt, xt, ct, bases)

    block = basis_count * width // (rows_total * cols)
    cover = block if block % TILE == 0 else round_up(block, TILE) + TILE

    def basis_blocks(turns):
        count = len(turns) * y_count
        return call(
            functools.partial(
                basis_kernel,
                (rows_total, cols, block, cover // TILE, basis_count, 2 * span, turns),
            ),
            [
                jax.ShapeDtypeStruct((cover, width), BF16 if sy else F32)
                for _ in turns
                for sy in range(y_count)
            ],
            4,
            [
                pltpu.VMEM((count * cover, width), F32),
                pltpu.VMEM((count * cover, 2 * span), BF16),
                pltpu.VMEM((count * cover, 2 * span), BF16),
                pltpu.VMEM((count * (round_up(cover, width) // width + 1), TILE, 2 * span), BF16),
            ],
            2 * 4 * edges * count * cover * width,
            "basis_terms",
        )(place, gt, gt_core, xt, ct)

    def over_y(turns):
        blocks = basis_blocks(turns)
        for order, sz in enumerate(turns):
            mine = blocks[order * y_count : (order + 1) * y_count]
            value = mine[0]
            for sy in range(1, y_count):
                value = value + turn_y(mine[sy], sy).astype(F32)
            sums[sz] = value

    sums = {}
    order = tuple(range(1, a_count)) + (0,)
    half = a_count // 2
    over_y(order[:half])
    over_y(order[half:])
    basis_sum = sums[0]
    for sz in range(1, a_count):
        basis_sum = basis_sum + turn_z(sums[sz].astype(BF16), sz).astype(F32)
    if cover != block:
        owner = i * cols + j
        basis_sum = lax.dynamic_slice_in_dim(basis_sum, owner * block % TILE, block, axis=0)
    basis_grad = basis_sum / cols

    joined = packed[0].astype(F32)
    for far in range(PAIR):
        for sy in range(y_count):
            if far or sy:
                target = [
                    (c, ((c // PAIR + sy) % y_count) * PAIR + (c % PAIR ^ far)) for c in range(cols)
                ]
                joined = joined + lax.ppermute(packed[far * y_count + sy], "col", target).astype(
                    F32
                )
    node_grad = joined[:shard].astype(BF16)
    coef_part = joined[shard:]
    low = coef_part.astype(BF16)
    low = (low.astype(F32) + flip_x(low).astype(F32)).astype(BF16)
    coef_part = tree_sum([low.astype(F32)] + [turn_z(low, s).astype(F32) for s in range(1, a_count)])
    shares = []
    for far in range(PAIR):
        for sy in range(y_count):
            target = [
                (c, ((c // PAIR + sy) % y_count) * PAIR + (c % PAIR ^ far)) for c in range(cols)
            ]
            shares.append(lax.ppermute(coef_part, "col", target) if far or sy else coef_part)
    coef_grad = call(
        functools.partial(coef_kernel, (cols, heads, padded, cols)),
        jax.ShapeDtypeStruct((basis_count, relation_count), F32),
        cols,
        [pltpu.VMEM((heads * padded, LANES), F32)],
        1 << 20,
        "coef_rows",
    )(place, *shares)
    return (node_grad, basis_grad, coef_grad.T)


def solution(mesh):
    in_specs = (
        P(("row", "col"), None),
        P("col", "row", None),
        P(),
        P(),
        P("row", "col", None),
        P("row", "col", None),
        P("row", "col", None),
        P("row", "col", None),
        P("row", "col", None),
    )
    out_specs = (P(("row", "col"), None), P(("row", "col"), None), P())
    return jax.shard_map(
        on_device, mesh=mesh, in_specs=in_specs, out_specs=out_specs, check_vma=False
    )
```

```python
import functools
import jax
import jax.numpy as jnp
from jax import lax
from jax.experimental import pallas as pl
from jax.experimental.pallas import tpu as pltpu
from jax.sharding import PartitionSpec as P

EDGE_BLOCK = 128
TILE = 16
LANES = 128
PAIR = 2
F32 = jnp.float32
BF16 = jnp.bfloat16
I32 = jnp.int32
VMEM_LIMIT = 32 * 1024 * 1024


def round_up(value, unit):
    return (value + unit - 1) // unit * unit


def split_index(ids, size):
    if size & (size - 1) == 0:
        shift = size.bit_length() - 1
        return ids >> shift, ids & (size - 1)
    return ids // size, ids % size


def wrap(difference, size):
    return jnp.where(difference < 0, difference + size, difference)


def one_hot(ids, depth):
    if depth <= 256:
        rows = lax.broadcasted_iota(I32, (depth, ids.shape[1]), 0).astype(F32).astype(BF16)
        one, zero = jnp.ones((), BF16), jnp.zeros((), BF16)
        return jnp.where(rows == ids.astype(F32).astype(BF16), one, zero)
    rows = lax.broadcasted_iota(I32, (depth, ids.shape[1]), 0)
    return jnp.where(rows == ids, 1.0, 0.0).astype(BF16)


def slot_hot(slot, local, slots, depth):
    return jnp.concatenate(
        [one_hot(jnp.where(slot == at, local, -1), depth) for at in range(slots)], axis=0
    )


def eye(width):
    first = lax.broadcasted_iota(I32, (width, width), 0)
    second = lax.broadcasted_iota(I32, (width, width), 1)
    return jnp.where(first == second, 1.0, 0.0).astype(BF16)


def dot(left, right):
    return lax.dot_general(left, right, (((1,), (0,)), ((), ())), preferred_element_type=F32)


def dot_t(left, right):
    return lax.dot_general(left, right, (((1,), (1,)), ((), ())), preferred_element_type=F32)


def tree_sum(values):
    if len(values) == 1:
        return values[0]
    return tree_sum(values[0::2]) + tree_sum(values[1::2])


def vmem():
    return pl.BlockSpec(memory_space=pltpu.VMEM)


def smem():
    return pl.BlockSpec(memory_space=pltpu.SMEM)


def call(body, out_shape, n_in, scratch, flops, name, unread=0):
    many = isinstance(out_shape, (tuple, list))
    moved = 1 << 22
    return pl.pallas_call(
        body,
        out_shape=out_shape,
        in_specs=[smem()] + [vmem()] * n_in + [pl.BlockSpec(memory_space=pl.ANY)] * unread,
        out_specs=[vmem()] * len(out_shape) if many else vmem(),
        scratch_shapes=scratch,
        compiler_params=pltpu.CompilerParams(vmem_limit_bytes=VMEM_LIMIT),
        cost_estimate=pl.CostEstimate(flops=flops, bytes_accessed=moved, transcendentals=0),
        name=name,
    )


def prepare_kernel(fills, src, dst, rel, norm, out_ref):
    blocks = fills.shape[-1]
    out_ref[0:1, :] = src[0].astype(F32)
    out_ref[1:2, :] = dst[0].astype(F32)
    out_ref[2:3, :] = rel[0].astype(F32)
    lane = lax.broadcasted_iota(I32, (1, EDGE_BLOCK), 1)
    for at in range(blocks):
        here = slice(at * EDGE_BLOCK, (at + 1) * EDGE_BLOCK)
        live = jnp.where(lane < fills[0, 0, at], 1.0, 0.0)
        out_ref[3:4, here] = norm[0, :, here] * live


def source_kernel(sizes, place, meta, meta_core, feats, feats_core, coefs_t, *refs):
    cols, shard, span, heads, padded, extra = sizes
    xt_ref, ct_ref, table, coefs = refs[extra:]
    count = cols // PAIR
    y, core = place[2], place[3]
    width = feats.shape[-1]
    edges = meta.shape[-1]
    basis_count, relation_count = coefs_t.shape
    unit = eye(width)
    for far, block in enumerate((feats, feats_core)):
        for sy in range(count):
            for xr in range(PAIR):
                at = (far * count + sy) * shard
                table[xr, :, at : at + shard] = dot_t(unit, block[sy, xr]).astype(BF16)
    coefs[...] = jnp.zeros_like(coefs)
    for head in range(heads):
        live = min(LANES, relation_count - head * LANES)
        if live > 0:
            coefs[head * padded : head * padded + basis_count, 0:live] = coefs_t[
                :, head * LANES : head * LANES + live
            ]
    for far, source in enumerate((meta, meta_core)):

        def step(index, carry, far=far, source=source):
            xr = index // (edges // span)
            at = pl.multiple_of(index % (edges // span) * span, span)
            ids = source[xr, 0:1, pl.ds(at, span)].astype(I32)
            owner, local = split_index(ids, shard)
            owner_y, owner_core = split_index(owner, PAIR)
            slot = (owner_core ^ core) * count + wrap(y - owner_y, count)
            rows = dot(table[xr], slot_hot(slot, local, cols, shard))
            xt_ref[far * PAIR + xr, :, pl.ds(at, span)] = rows.astype(BF16)
            relation = source[xr, 2:3, pl.ds(at, span)].astype(I32)
            high, low = split_index(relation, LANES)
            parts = dot(coefs[...], one_hot(low, LANES))
            total = jnp.zeros((padded, span), F32)
            for head in range(heads):
                total = total + jnp.where(
                    high == head, parts[head * padded : (head + 1) * padded], 0.0
                )
            ct_ref[far * PAIR + xr, :, pl.ds(at, span)] = total
            return carry

        lax.fori_loop(0, PAIR * (edges // span), step, 0, unroll=2)


def grad_kernel(sizes, place, meta, *refs):
    rows_total, shard, span = sizes
    count = rows_total // PAIR
    blocks = refs[:rows_total]
    gt_ref, table = refs[rows_total + 1 :]
    a, x = place[0], place[1]
    width = blocks[0].shape[-1]
    edges = meta.shape[-1]
    unit = eye(width)
    for at, block in enumerate(blocks):
        table[:, at * shard : (at + 1) * shard] = dot_t(unit, block[...]).astype(BF16)

    def step(index, carry):
        xr = index // (edges // span)
        at = pl.multiple_of(index % (edges // span) * span, span)
        ids = meta[xr, 1:2, pl.ds(at, span)].astype(I32)
        owner, local = split_index(ids, shard)
        owner_a, owner_x = split_index(owner, PAIR)
        slot = (owner_x ^ x) * count + wrap(a - owner_a, count)
        rows = dot(table[...], slot_hot(slot, local, rows_total, shard))
        weight = meta[xr, 3:4, pl.ds(at, span)]
        gt_ref[:, pl.ds(pl.multiple_of(index * span, span), span)] = (rows * weight).astype(BF16)
        return carry

    lax.fori_loop(0, PAIR * (edges // span), step, 0, unroll=2)


def forward_kernel(
    sizes, place, meta, gt_ref, xt_ref, ct_ref, bases_ref, *refs
):
    cols, shard, span, heads, padded, group = sizes
    outs = refs[:cols]
    total, inner, wide, coef_sum = refs[cols:]
    count = cols // PAIR
    y, core = place[2], place[3]
    edges = meta.shape[-1]
    width = bases_ref.shape[-1]
    total[...] = jnp.zeros_like(total)
    inner[...] = jnp.zeros_like(inner)

    def step(number, carry):
        stacked = bases_ref[pl.ds(number * group, group)].reshape(group * width, width)
        for index in range(edges // span):
            at = slice(index * span, (index + 1) * span)
            backed = dot(stacked, gt_ref[:, at])
            rows = xt_ref[0, :, at].astype(F32)
            sums = total[:, at]
            for t in range(group):
                base = number * group + t
                mine = backed[t * width : (t + 1) * width]
                sums = sums + ct_ref[0, pl.ds(base, 1), at] * mine
                inner[pl.ds(base, 1), at] = jnp.sum(mine * rows, axis=0, keepdims=True)
            total[:, at] = sums
        return carry

    lax.fori_loop(0, bases_ref.shape[0] // group, step, 0)

    ids = meta[0, 0:1, :].astype(I32)
    owner, local = split_index(ids, shard)
    owner_y, owner_core = split_index(owner, PAIR)
    slot = (owner_core ^ core) * count + wrap(owner_y - y, count)
    values = total[...].astype(BF16)
    for at in range(cols):
        hot = one_hot(jnp.where(slot == at, local, -1), shard)
        outs[at][0:shard, :] = dot_t(hot, values).astype(BF16)
    high, low = split_index(meta[0, 2:3, :].astype(I32), LANES)
    for head in range(heads):
        wide[head * padded : (head + 1) * padded, :] = jnp.where(
            high == head, inner[...], 0.0
        ).astype(BF16)
    coef_sum[...] = dot_t(wide[...], one_hot(low, LANES))
    share = heads * padded // cols
    half = share // 2
    for far in range(PAIR):
        for sy in range(count):
            target = (y + sy) % count * PAIR + (core ^ far)
            for side in range(2):
                rows = coef_sum[pl.ds(pl.multiple_of(target * share + side * half, 8), half), :]
                outs[far * count + sy][
                    shard : shard + half, side * LANES : (side + 1) * LANES
                ] = rows.astype(BF16)


def basis_kernel(sizes, place, gt_ref, gt_core, xt_ref, ct_ref, *refs):
    rows_total, cols, block, groups, basis_count, span, turns = sizes
    a_count, y_count = rows_total // PAIR, cols // PAIR
    a, x, y, core = place[0], place[1], place[2], place[3]
    outs = refs[: y_count * len(turns)]
    acc, left_even, left_odd, tiles = refs[len(outs) :]
    width, edges = xt_ref.shape[1], xt_ref.shape[2]
    tiles_wide = width // TILE
    cover = groups * TILE
    spread = tiles.shape[0] // len(outs)
    steps = edges // span
    firsts = []
    for sz in turns:
        for sy in range(y_count):
            owner = ((a + sz) % a_count * PAIR + x) * cols + (y + sy) % y_count * PAIR + core
            firsts.append(owner * block // TILE)

    def build(part, at, left):
        for order, first in enumerate(firsts):
            base = first // tiles_wide
            for extra in range(spread):
                row = ct_ref[part, pl.ds(jnp.minimum(base + extra, basis_count - 1), 1), at]
                tiles[order * spread + extra] = jnp.broadcast_to(row, (TILE, span)).astype(BF16)
            for q in range(groups):
                tile = jnp.minimum(first + q, basis_count * tiles_wide - 1)
                lower = pl.multiple_of(tile % tiles_wide * TILE, TILE)
                to = (order * groups + q) * TILE
                left[to : to + TILE, :] = (
                    tiles[order * spread + tile // tiles_wide - base]
                    * xt_ref[part, pl.ds(lower, TILE), at]
                )

    for index in range(2 * PAIR * steps):
        part = index // steps
        at = slice(index % steps * span, (index % steps + 1) * span)
        left = left_even if index % 2 == 0 else left_odd
        build(part, at, left)
        grads = gt_ref if part < PAIR else gt_core
        here = index % (PAIR * steps) * span
        term = dot_t(left[...], grads[:, here : here + span])
        if index:
            acc[...] += term
        else:
            acc[...] = term
    for order, out in enumerate(outs):
        out[...] = acc[order * cover : (order + 1) * cover, :].astype(out.dtype)


def coef_kernel(sizes, place, *refs):
    cols, heads, padded, divisor = sizes
    count = cols // PAIR
    parts, (out_ref, whole) = refs[:cols], refs[cols:]
    y, core = place[2], place[3]
    share = heads * padded // cols
    half = share // 2
    for far in range(PAIR):
        for sy in range(count):
            target = wrap(y - sy, count) * PAIR + (core ^ far)
            for side in range(2):
                whole[pl.ds(pl.multiple_of(target * share + side * half, 8), half), :] = (
                    parts[far * count + sy][:, side * LANES : (side + 1) * LANES]
                )
    width, total = out_ref.shape
    for head in range(heads):
        live = min(LANES, total - head * LANES)
        if live > 0:
            out_ref[:, head * LANES : head * LANES + live] = (
                whole[head * padded : head * padded + width, 0:live] / divisor
            )


def on_device(
    node_feats, dest_grad, bases, coefs, src_ids, dst_ids, rel_ids, edge_norm, block_fill
):
    rows_total = lax.axis_size("row")
    cols = lax.axis_size("col")
    a_count, y_count = rows_total // PAIR, cols // PAIR
    shard, width = node_feats.shape
    basis_count = bases.shape[0]
    relation_count = coefs.shape[0]
    edges = src_ids.size
    padded = round_up(basis_count, TILE)
    heads = round_up(relation_count, LANES) // LANES
    while heads * padded % (cols * 2 * TILE):
        heads += 1
    span = 256
    i = lax.axis_index("row")
    j = lax.axis_index("col")
    place = jnp.stack([i // PAIR, i % PAIR, j // PAIR, j % PAIR]).astype(I32)

    def flip_x(value):
        return lax.ppermute(value, "row", [(r, r ^ 1) for r in range(rows_total)])

    def flip_core(value):
        return lax.ppermute(value, "col", [(c, c ^ 1) for c in range(cols)])

    def turn_z(value, by):
        return lax.ppermute(
            value, "row", [(r, (r + by * PAIR) % rows_total) for r in range(rows_total)]
        )

    def turn_y(value, by):
        return lax.ppermute(value, "col", [(c, (c + by * PAIR) % cols) for c in range(cols)])

    own_dest = dest_grad[0]
    turned = [turn_z(own_dest, s) for s in range(1, a_count)]
    across_own = flip_x(own_dest)
    near = flip_x(node_feats)
    meta = pl.pallas_call(
        prepare_kernel,
        out_shape=jax.ShapeDtypeStruct((4, edges), F32),
        in_specs=[smem()] + [vmem()] * 4,
        out_specs=vmem(),
        name="edge_table",
    )(block_fill, src_ids, dst_ids, rel_ids, edge_norm)
    meta = jnp.stack([meta, flip_x(meta)])
    feats, turned[0] = lax.optimization_barrier((jnp.stack([node_feats, near]), turned[0]))
    feats = jnp.stack([feats] + [turn_y(feats, s) for s in range(1, y_count)])
    across = [across_own, flip_x(turned[0])]
    feats, meta, across[0], across[1], *turned[1:] = lax.optimization_barrier(
        (feats, meta, *across, *turned[1:])
    )
    dest = [own_dest] + turned
    across += [flip_x(value) for value in turned[1:]]
    meta_core = flip_core(meta)
    feats_core = flip_core(feats)

    xt, ct = call(
        functools.partial(source_kernel, (cols, shard, span, heads, padded, a_count)),
        (
            jax.ShapeDtypeStruct((2 * PAIR, width, edges), BF16),
            jax.ShapeDtypeStruct((2 * PAIR, padded, edges), F32),
        ),
        5,
        [
            pltpu.VMEM((PAIR, width, cols * shard), BF16),
            pltpu.VMEM((heads * padded, LANES), BF16),
        ],
        2 * 4 * edges * cols * shard * width,
        "source_rows",
        a_count,
    )(place, meta, meta_core, feats, feats_core, coefs.T, *dest)

    dest_shard = own_dest.shape[0]
    gt = call(
        functools.partial(grad_kernel, (rows_total, dest_shard, span)),
        jax.ShapeDtypeStruct((width, PAIR * edges), BF16),
        1 + rows_total,
        [pltpu.VMEM((width, rows_total * dest_shard), BF16)],
        2 * 2 * edges * rows_total * dest_shard * width,
        "edge_grads",
        1,
    )(place, meta, *dest, *across, xt)
    gt_core = flip_core(gt)

    group = max(g for g in range(1, 6) if basis_count % g == 0)
    share_rows = heads * padded // cols // 2
    packed = call(
        functools.partial(forward_kernel, (cols, shard, span, heads, padded, group)),
        [jax.ShapeDtypeStruct((shard + share_rows, width), BF16)] * cols,
        5,
        [
            pltpu.VMEM((width, edges), F32),
            pltpu.VMEM((padded, edges), F32),
            pltpu.VMEM((heads * padded, edges), BF16),
            pltpu.VMEM((heads * padded, LANES), F32),
        ],
        2 * edges * width * width * basis_count,
        "backed_sums",
    )(place, meta, gt, xt, ct, bases)

    block = basis_count * width // (rows_total * cols)
    cover = block if block % TILE == 0 else round_up(block, TILE) + TILE

    def basis_blocks(place, turns):
        count = len(turns) * y_count
        return call(
            functools.partial(
                basis_kernel,
                (rows_total, cols, block, cover // TILE, basis_count, 2 * span, turns),
            ),
            [
                jax.ShapeDtypeStruct((cover, width), BF16 if sy else F32)
                for _ in turns
                for sy in range(y_count)
            ],
            4,
            [
                pltpu.VMEM((count * cover, width), F32),
                pltpu.VMEM((count * cover, 2 * span), BF16),
                pltpu.VMEM((count * cover, 2 * span), BF16),
                pltpu.VMEM((count * (round_up(cover, width) // width + 1), TILE, 2 * span), BF16),
            ],
            2 * 4 * edges * count * cover * width,
            "basis_terms",
        )(place, gt, gt_core, xt, ct)

    def to_col(value, far, sy):
        return lax.ppermute(
            value,
            "col",
            [(c, (c // PAIR + sy) % y_count * PAIR + (c % PAIR ^ far)) for c in range(cols)],
        )

    def after(value, other):
        return lax.optimization_barrier((value, other))[0]

    others = [(far, sy) for far in range(PAIR) for sy in range(y_count) if far or sy]
    received = [to_col(packed[far * y_count + sy], far, sy) for far, sy in others]

    sums, passed, marks = {}, [], []
    order = tuple(range(1, a_count)) + (0,)
    for at, sz in enumerate(order):
        where = place
        if at >= 2:
            where = after(where, passed[at - 2])
        blocks = basis_blocks(where, (sz,))
        value = blocks[0]
        arrived = [turn_y(blocks[sy], sy) for sy in range(1, y_count)]
        for piece in arrived:
            value = value + piece.astype(F32)
        sums[sz] = turn_z(value.astype(BF16), sz) if sz else value
        passed.append(arrived[-1] if arrived else blocks[0])
        marks.append(blocks[0])
    joined = packed[0].astype(F32)
    for value in received:
        joined = joined + after(value, marks[min(1, a_count - 1)]).astype(F32)
    basis_sum = sums[0]
    for sz in range(1, a_count):
        basis_sum = basis_sum + sums[sz].astype(F32)
    if cover != block:
        owner = i * cols + j
        basis_sum = lax.dynamic_slice_in_dim(basis_sum, owner * block % TILE, block, axis=0)
    basis_grad = basis_sum / cols

    node_grad = joined[:shard].astype(BF16)
    coef_part = joined[shard:]
    low = coef_part.astype(BF16)
    low = (low.astype(F32) + after(flip_x(low), marks[max(a_count - 2, 0)]).astype(F32)).astype(BF16)
    around = [after(turn_z(low, s), marks[-1]).astype(F32) for s in range(1, a_count)]
    coef_part = tree_sum([low.astype(F32)] + around)
    shares = [coef_part] + [to_col(coef_part, far, sy) for far, sy in others]
    coef_grad = call(
        functools.partial(coef_kernel, (cols, heads, padded, cols)),
        jax.ShapeDtypeStruct((basis_count, relation_count), F32),
        cols,
        [pltpu.VMEM((heads * padded, LANES), F32)],
        1 << 20,
        "coef_rows",
    )(place, *shares)
    return (node_grad, basis_grad, coef_grad.T)


def solution(mesh):
    in_specs = (
        P(("row", "col"), None),
        P("col", "row", None),
        P(),
        P(),
        P("row", "col", None),
        P("row", "col", None),
        P("row", "col", None),
        P("row", "col", None),
        P("row", "col", None),
    )
    out_specs = (P(("row", "col"), None), P(("row", "col"), None), P())
    return jax.shard_map(
        on_device, mesh=mesh, in_specs=in_specs, out_specs=out_specs, check_vma=False
    )
```

```python
import functools
import jax
import jax.numpy as jnp
from jax import lax
from jax.experimental import pallas as pl
from jax.experimental.pallas import tpu as pltpu
from jax.sharding import PartitionSpec as P

EDGE_BLOCK = 128
TILE = 16
DIGIT = 256
LANES = 128
PAIR = 2
F32 = jnp.float32
BF16 = jnp.bfloat16
I32 = jnp.int32
VMEM_LIMIT = 32 * 1024 * 1024


def round_up(value, unit):
    return (value + unit - 1) // unit * unit


def split_index(ids, size):
    if size & (size - 1) == 0:
        shift = size.bit_length() - 1
        return ids >> shift, ids & (size - 1)
    return ids // size, ids % size


def wrap(difference, size):
    return jnp.where(difference < 0, difference + size, difference)


def one_hot(ids, depth):
    if depth <= 256:
        rows = lax.broadcasted_iota(I32, (depth, ids.shape[1]), 0).astype(F32).astype(BF16)
        one, zero = jnp.ones((), BF16), jnp.zeros((), BF16)
        return jnp.where(rows == ids.astype(F32).astype(BF16), one, zero)
    rows = lax.broadcasted_iota(I32, (depth, ids.shape[1]), 0)
    return jnp.where(rows == ids, 1.0, 0.0).astype(BF16)


def slot_hot(slot, local, slots, depth):
    return jnp.concatenate(
        [one_hot(jnp.where(slot == at, local, -1), depth) for at in range(slots)], axis=0
    )


def eye(width):
    first = lax.broadcasted_iota(I32, (width, width), 0)
    second = lax.broadcasted_iota(I32, (width, width), 1)
    return jnp.where(first == second, 1.0, 0.0).astype(BF16)


def dot(left, right):
    return lax.dot_general(left, right, (((1,), (0,)), ((), ())), preferred_element_type=F32)


def dot_t(left, right):
    return lax.dot_general(left, right, (((1,), (1,)), ((), ())), preferred_element_type=F32)


def vmem():
    return pl.BlockSpec(memory_space=pltpu.VMEM)


def smem():
    return pl.BlockSpec(memory_space=pltpu.SMEM)


def call(body, out_shape, n_in, scratch, flops, name, unread=0):
    many = isinstance(out_shape, (tuple, list))
    moved = 1 << 22
    return pl.pallas_call(
        body,
        out_shape=out_shape,
        in_specs=[smem()] + [vmem()] * n_in + [pl.BlockSpec(memory_space=pl.ANY)] * unread,
        out_specs=[vmem()] * len(out_shape) if many else vmem(),
        scratch_shapes=scratch,
        compiler_params=pltpu.CompilerParams(vmem_limit_bytes=VMEM_LIMIT),
        cost_estimate=pl.CostEstimate(flops=flops, bytes_accessed=moved, transcendentals=0),
        name=name,
    )


def prepare_kernel(fills, src, dst, rel, norm, dest, feats, out_ref):
    rows = dest.shape[0]
    out_ref[0:rows, :] = dest[...]
    out_ref[rows : rows + feats.shape[0], :] = feats[...]
    base = rows + feats.shape[0]
    span = out_ref.shape[1]
    lane = lax.broadcasted_iota(I32, (1, EDGE_BLOCK), 1)
    for q in range(src.shape[-1] // span):
        here = slice(q * span, (q + 1) * span)
        lines = []
        for ids in (src, dst, rel):
            high, low = split_index(ids[0, :, here], DIGIT)
            lines += [low.astype(F32), high.astype(F32)]
        live = []
        for at in range(q * span // EDGE_BLOCK, (q + 1) * span // EDGE_BLOCK):
            live.append(jnp.where(lane < fills[0, 0, at], 1.0, 0.0))
        rest = norm[0, :, here] * jnp.concatenate(live, axis=1)
        for _ in range(3):
            digit = rest.astype(BF16).astype(F32)
            lines.append(digit)
            rest = rest - digit
        lines.append(jnp.zeros((TILE - len(lines), span), F32))
        out_ref[base + q * TILE : base + (q + 1) * TILE, :] = jnp.concatenate(
            lines, axis=0
        ).astype(BF16)


def read_table(ref, at):
    tile = ref[pl.ds(at, TILE), :].astype(F32)
    ids = []
    for kind in range(3):
        low, high = tile[2 * kind : 2 * kind + 1], tile[2 * kind + 1 : 2 * kind + 2]
        ids.append((high * DIGIT + low).astype(I32))
    return (*ids, (tile[6:7] + tile[7:8]) + tile[8:9])


def near_kernel(own, other, out_ref):
    shard = out_ref.shape[0] // PAIR
    for xr, source in enumerate((own, other)):
        out_ref[xr * shard : (xr + 1) * shard, :] = source[shard : 2 * shard, :]


def pack_kernel(own, other, *refs):
    parts, out_ref = refs[:-1], refs[-1]
    size = parts[0].shape[0]
    for at, part in enumerate(parts):
        out_ref[at * size : (at + 1) * size, :] = part[...]
    base = len(parts) * size
    lines = (out_ref.shape[0] - base) // PAIR
    for xr, source in enumerate((own, other)):
        out_ref[base + xr * lines : base + (xr + 1) * lines, :] = source[
            source.shape[0] - lines :, :
        ]


def source_kernel(sizes, place, own, other, coefs_t, *refs):
    cols, shard, edges, heads, padded, extra = sizes
    xt_ref, ct_ref, table, coefs = refs[extra:]
    count = cols // PAIR
    y, core = place[2], place[3]
    span = width = own.shape[-1]
    base = cols * shard
    lines = edges // span * TILE
    basis_count, relation_count = coefs_t.shape
    unit = eye(width)
    for far, block in enumerate((own, other)):
        for sy in range(count):
            for xr in range(PAIR):
                at = (far * count + sy) * shard
                rows = block[(sy * PAIR + xr) * shard : (sy * PAIR + xr + 1) * shard, :]
                table[xr, :, at : at + shard] = dot_t(unit, rows).astype(BF16)
    coefs[...] = jnp.zeros_like(coefs)
    for head in range(heads):
        live = min(LANES, relation_count - head * LANES)
        if live > 0:
            coefs[head * padded : head * padded + basis_count, 0:live] = coefs_t[
                :, head * LANES : head * LANES + live
            ]
    for far, source in enumerate((own, other)):

        def step(index, carry, far=far, source=source):
            xr = index // (edges // span)
            at = pl.multiple_of(index % (edges // span) * span, span)
            ids, _, relation, _ = read_table(source, pl.multiple_of(base + index * TILE, TILE))
            owner, local = split_index(ids, shard)
            owner_y, owner_core = split_index(owner, PAIR)
            slot = (owner_core ^ core) * count + wrap(y - owner_y, count)
            rows = dot(table[xr], slot_hot(slot, local, cols, shard))
            xt_ref[far * PAIR + xr, :, pl.ds(at, span)] = rows.astype(BF16)
            high, low = split_index(relation, LANES)
            parts = dot(coefs[...], one_hot(low, LANES))
            total = jnp.zeros((padded, span), F32)
            for head in range(heads):
                total = total + jnp.where(
                    high == head, parts[head * padded : (head + 1) * padded], 0.0
                )
            ct_ref[far * PAIR + xr, :, pl.ds(at, span)] = total
            return carry

        lax.fori_loop(0, PAIR * (edges // span), step, 0, unroll=2)


def grad_kernel(sizes, place, packed, *refs):
    rows_total, shard, edges = sizes
    count = rows_total // PAIR
    blocks = refs[:rows_total]
    gt_ref, table = refs[rows_total + 1 :]
    a, x = place[0], place[1]
    span = width = blocks[0].shape[-1]
    lines = edges // span * TILE
    base = packed.shape[0] - PAIR * lines
    unit = eye(width)
    for at, block in enumerate(blocks):
        table[:, at * shard : (at + 1) * shard] = dot_t(unit, block[0:shard, :]).astype(BF16)

    def step(index, carry):
        _, ids, _, weight = read_table(packed, pl.multiple_of(base + index * TILE, TILE))
        owner, local = split_index(ids, shard)
        owner_a, owner_x = split_index(owner, PAIR)
        slot = (owner_x ^ x) * count + wrap(a - owner_a, count)
        rows = dot(table[...], slot_hot(slot, local, rows_total, shard))
        gt_ref[:, pl.ds(pl.multiple_of(index * span, span), span)] = (rows * weight).astype(BF16)
        return carry

    lax.fori_loop(0, PAIR * (edges // span), step, 0, unroll=2)


def forward_kernel(
    sizes, place, table, gt_ref, xt_ref, ct_ref, bases_ref, *refs
):
    cols, shard, edges, heads, padded, group = sizes
    outs = refs[:cols]
    total, inner, wide, coef_sum = refs[cols:]
    count = cols // PAIR
    y, core = place[2], place[3]
    span = width = bases_ref.shape[-1]
    lines = edges // span * TILE
    base_row = table.shape[0] - PAIR * lines
    total[...] = jnp.zeros_like(total)
    inner[...] = jnp.zeros_like(inner)

    def step(number, carry):
        stacked = bases_ref[pl.ds(number * group, group)].reshape(group * width, width)
        for index in range(edges // span):
            at = slice(index * span, (index + 1) * span)
            backed = dot(stacked, gt_ref[:, at])
            rows = xt_ref[0, :, at].astype(F32)
            sums = total[:, at]
            for t in range(group):
                base = number * group + t
                mine = backed[t * width : (t + 1) * width]
                sums = sums + ct_ref[0, pl.ds(base, 1), at] * mine
                inner[pl.ds(base, 1), at] = jnp.sum(mine * rows, axis=0, keepdims=True)
            total[:, at] = sums
        return carry

    lax.fori_loop(0, bases_ref.shape[0] // group, step, 0)

    tables = [read_table(table, base_row + q * TILE) for q in range(edges // span)]
    ids = jnp.concatenate([part[0] for part in tables], axis=1)
    owner, local = split_index(ids, shard)
    owner_y, owner_core = split_index(owner, PAIR)
    slot = (owner_core ^ core) * count + wrap(owner_y - y, count)
    values = total[...].astype(BF16)
    for at in range(cols):
        hot = one_hot(jnp.where(slot == at, local, -1), shard)
        outs[at][0:shard, :] = dot_t(hot, values).astype(BF16)
    high, low = split_index(jnp.concatenate([part[2] for part in tables], axis=1), LANES)
    for head in range(heads):
        wide[head * padded : (head + 1) * padded, :] = jnp.where(
            high == head, inner[...], 0.0
        ).astype(BF16)
    coef_sum[...] = dot_t(wide[...], one_hot(low, LANES))
    share = heads * padded // cols
    half = share // 2
    for far in range(PAIR):
        for sy in range(count):
            target = (y + sy) % count * PAIR + (core ^ far)
            for side in range(2):
                rows = coef_sum[pl.ds(pl.multiple_of(target * share + side * half, 8), half), :]
                outs[far * count + sy][
                    shard : shard + half, side * LANES : (side + 1) * LANES
                ] = rows.astype(BF16)


def basis_kernel(sizes, place, gt_ref, gt_core, xt_ref, ct_ref, *refs):
    rows_total, cols, block, groups, basis_count, span, turns = sizes
    a_count, y_count = rows_total // PAIR, cols // PAIR
    a, x, y, core = place[0], place[1], place[2], place[3]
    outs = refs[:y_count]
    acc, left_even, left_odd, tiles = refs[len(outs) :]
    width, edges = xt_ref.shape[1], xt_ref.shape[2]
    tiles_wide = width // TILE
    cover = groups * TILE
    spread = tiles.shape[0] // (y_count * len(turns))
    steps = edges // span
    firsts = []
    for sy in range(y_count):
        for sz in turns:
            owner = ((a + sz) % a_count * PAIR + x) * cols + (y + sy) % y_count * PAIR + core
            firsts.append(owner * block // TILE)

    def build(part, at, left):
        for order, first in enumerate(firsts):
            base = first // tiles_wide
            for extra in range(spread):
                row = ct_ref[part, pl.ds(jnp.minimum(base + extra, basis_count - 1), 1), at]
                tiles[order * spread + extra] = jnp.broadcast_to(row, (TILE, span)).astype(BF16)
            for q in range(groups):
                tile = jnp.minimum(first + q, basis_count * tiles_wide - 1)
                lower = pl.multiple_of(tile % tiles_wide * TILE, TILE)
                to = (order * groups + q) * TILE
                left[to : to + TILE, :] = (
                    tiles[order * spread + tile // tiles_wide - base]
                    * xt_ref[part, pl.ds(lower, TILE), at]
                )

    for index in range(2 * PAIR * steps):
        part = index // steps
        at = slice(index % steps * span, (index % steps + 1) * span)
        left = left_even if index % 2 == 0 else left_odd
        build(part, at, left)
        grads = gt_ref if part < PAIR else gt_core
        here = index % (PAIR * steps) * span
        term = dot_t(left[...], grads[:, here : here + span])
        if index:
            acc[...] += term
        else:
            acc[...] = term
    size = len(turns) * cover
    for sy, out in enumerate(outs):
        out[...] = acc[sy * size : (sy + 1) * size, :].astype(out.dtype)


def coef_kernel(sizes, parts, out_ref, whole):
    cols, heads, padded, divisor = sizes
    share = heads * padded // cols
    half = share // 2
    for target in range(cols):
        for side in range(2):
            at = target * share + side * half
            whole[at : at + half, :] = parts[target, :, side * LANES : (side + 1) * LANES]
    width, total = out_ref.shape
    for head in range(heads):
        live = min(LANES, total - head * LANES)
        if live > 0:
            out_ref[:, head * LANES : head * LANES + live] = (
                whole[head * padded : head * padded + width, 0:live] / divisor
            )


def on_device(
    node_feats, dest_grad, bases, coefs, src_ids, dst_ids, rel_ids, edge_norm, block_fill
):
    rows_total = lax.axis_size("row")
    cols = lax.axis_size("col")
    a_count, y_count = rows_total // PAIR, cols // PAIR
    shard, width = node_feats.shape
    basis_count = bases.shape[0]
    relation_count = coefs.shape[0]
    edges = src_ids.size
    padded = round_up(basis_count, TILE)
    heads = round_up(relation_count, LANES) // LANES
    while heads * padded % (cols * 2 * TILE):
        heads += 1
    i = lax.axis_index("row")
    j = lax.axis_index("col")
    place = jnp.stack([i // PAIR, i % PAIR, j // PAIR, j % PAIR]).astype(I32)

    def plain(body, rows, n_in, name, *first):
        return pl.pallas_call(
            body,
            out_shape=jax.ShapeDtypeStruct((rows, width), BF16),
            in_specs=[*first] + [vmem()] * n_in,
            out_specs=vmem(),
            name=name,
        )

    def flip_x(value):
        return lax.ppermute(value, "row", [(r, r ^ 1) for r in range(rows_total)])

    def flip_core(value):
        return lax.ppermute(value, "col", [(c, c ^ 1) for c in range(cols)])

    def turn_z(value, by):
        return lax.ppermute(
            value, "row", [(r, (r + by * PAIR) % rows_total) for r in range(rows_total)]
        )

    def turn_y(value, by):
        return lax.ppermute(value, "col", [(c, (c + by * PAIR) % cols) for c in range(cols)])

    own_dest = dest_grad[0]
    dest_shard = own_dest.shape[0]
    turned = [turn_z(own_dest, s) for s in range(1, a_count)]
    lines = edges // width * TILE
    mine = plain(
        prepare_kernel, dest_shard + shard + lines, 6, "edge_table", smem()
    )(block_fill, src_ids, dst_ids, rel_ids, edge_norm, own_dest, node_feats)
    other = flip_x(mine)
    feats = plain(near_kernel, PAIR * shard, 2, "near_rows")(mine, other)
    feats, *turned[:2] = lax.optimization_barrier((feats, *turned[:2]))
    feats = [feats] + [turn_y(feats, s) for s in range(1, y_count)]
    across = [other] + [flip_x(value) for value in turned[:2]]
    feats[-1], *rest = lax.optimization_barrier((feats[-1], *across[1:], *turned[2:]))
    across[1:], turned[2:] = rest[: len(across) - 1], rest[len(across) - 1 :]
    across += [flip_x(value) for value in turned[2:]]
    dest = [own_dest] + turned
    packed = plain(pack_kernel, cols * shard + PAIR * lines, 2 + y_count, "packed_rows")(
        mine, other, *feats
    )
    packed_core = flip_core(packed)

    xt, ct = call(
        functools.partial(source_kernel, (cols, shard, edges, heads, padded, a_count)),
        (
            jax.ShapeDtypeStruct((2 * PAIR, width, edges), BF16),
            jax.ShapeDtypeStruct((2 * PAIR, padded, edges), F32),
        ),
        3,
        [
            pltpu.VMEM((PAIR, width, cols * shard), BF16),
            pltpu.VMEM((heads * padded, LANES), BF16),
        ],
        2 * 4 * edges * cols * shard * width,
        "source_rows",
        a_count,
    )(place, packed, packed_core, coefs.T, *dest)

    gt = call(
        functools.partial(grad_kernel, (rows_total, dest_shard, edges)),
        jax.ShapeDtypeStruct((width, PAIR * edges), BF16),
        1 + rows_total,
        [pltpu.VMEM((width, rows_total * dest_shard), BF16)],
        2 * 2 * edges * rows_total * dest_shard * width,
        "edge_grads",
        1,
    )(place, packed, *dest, *across, xt)
    gt_core = flip_core(gt)

    group = max(g for g in range(1, 6) if basis_count % g == 0)
    share_rows = heads * padded // cols // 2
    partial = call(
        functools.partial(forward_kernel, (cols, shard, edges, heads, padded, group)),
        [jax.ShapeDtypeStruct((shard + share_rows, width), BF16)] * cols,
        5,
        [
            pltpu.VMEM((width, edges), F32),
            pltpu.VMEM((padded, edges), F32),
            pltpu.VMEM((heads * padded, edges), BF16),
            pltpu.VMEM((heads * padded, LANES), F32),
        ],
        2 * edges * width * width * basis_count,
        "backed_sums",
    )(place, packed, gt, xt, ct, bases)

    block = basis_count * width // (rows_total * cols)
    cover = block if block % TILE == 0 else round_up(block, TILE) + TILE

    def basis_blocks(place, turns):
        count = len(turns) * y_count
        return call(
            functools.partial(
                basis_kernel,
                (rows_total, cols, block, cover // TILE, basis_count, 2 * width, turns),
            ),
            [
                jax.ShapeDtypeStruct((len(turns) * cover, width), BF16 if sy else F32)
                for sy in range(y_count)
            ],
            4,
            [
                pltpu.VMEM((count * cover, width), F32),
                pltpu.VMEM((count * cover, 2 * width), BF16),
                pltpu.VMEM((count * cover, 2 * width), BF16),
                pltpu.VMEM((count * (round_up(cover, width) // width + 1), TILE, 2 * width), BF16),
            ],
            2 * 4 * edges * count * cover * width,
            "basis_terms",
        )(place, gt, gt_core, xt, ct)

    def to_col(value, far, sy):
        return lax.ppermute(
            value,
            "col",
            [(c, (c // PAIR + sy) % y_count * PAIR + (c % PAIR ^ far)) for c in range(cols)],
        )

    def after(value, other):
        return lax.optimization_barrier((value, other))[0]

    others = [(far, sy) for far in range(PAIR) for sy in range(y_count) if far or sy]
    received = [to_col(partial[far * y_count + sy], far, sy) for far, sy in others]

    order = tuple(range(1, a_count)) + (0,)
    half = (a_count + 1) // 2
    sums = {}
    for turns in (order[:half], order[half:]):
        if turns:
            blocks = basis_blocks(place, turns)
            value = blocks[0]
            for sy in range(1, y_count):
                value = value + turn_y(blocks[sy], sy).astype(F32)
            for at, sz in enumerate(turns):
                piece = value[at * cover : (at + 1) * cover]
                sums[sz] = turn_z(piece.astype(BF16), sz) if sz else piece
    joined = partial[0].astype(F32)
    for value in received:
        joined = joined + after(value, blocks[0]).astype(F32)
    basis_sum = sums[0]
    for sz in range(1, a_count):
        basis_sum = basis_sum + sums[sz].astype(F32)
    if cover != block:
        owner = i * cols + j
        basis_sum = lax.dynamic_slice_in_dim(basis_sum, owner * block % TILE, block, axis=0)
    basis_grad = basis_sum / cols

    node_grad = joined[:shard].astype(BF16)
    coef_part = joined[shard:]
    rows_of = lax.all_gather(coef_part.astype(BF16), "row")
    coef_part = jnp.sum(rows_of.astype(F32), axis=0)
    coef_grad = pl.pallas_call(
        functools.partial(coef_kernel, (cols, heads, padded, cols)),
        out_shape=jax.ShapeDtypeStruct((basis_count, relation_count), F32),
        in_specs=[vmem()],
        out_specs=vmem(),
        scratch_shapes=[pltpu.VMEM((heads * padded, LANES), F32)],
        name="coef_rows",
    )(lax.all_gather(coef_part, "col"))
    return (node_grad, basis_grad, coef_grad.T)


def solution(mesh):
    in_specs = (
        P(("row", "col"), None),
        P("col", "row", None),
        P(),
        P(),
        P("row", "col", None),
        P("row", "col", None),
        P("row", "col", None),
        P("row", "col", None),
        P("row", "col", None),
    )
    out_specs = (P(("row", "col"), None), P(("row", "col"), None), P())
    return jax.shard_map(
        on_device, mesh=mesh, in_specs=in_specs, out_specs=out_specs, check_vma=False
    )
```

```python
import functools
import jax
import jax.numpy as jnp
from jax import lax
from jax.experimental import pallas as pl
from jax.experimental.pallas import tpu as pltpu
from jax.sharding import PartitionSpec as P

EDGE_BLOCK = 128
TILE = 16
BAND = 64
LANES = 128
PAIR = 2
F32 = jnp.float32
BF16 = jnp.bfloat16
I32 = jnp.int32
VMEM_LIMIT = 32 * 1024 * 1024


def round_up(value, unit):
    return (value + unit - 1) // unit * unit


def split_index(ids, size):
    if size & (size - 1) == 0:
        shift = size.bit_length() - 1
        return ids >> shift, ids & (size - 1)
    return ids // size, ids % size


def wrap(difference, size):
    return jnp.where(difference < 0, difference + size, difference)


def one_hot(ids, depth):
    if depth <= 256:
        rows = lax.broadcasted_iota(I32, (depth, ids.shape[1]), 0).astype(F32).astype(BF16)
        one, zero = jnp.ones((), BF16), jnp.zeros((), BF16)
        return jnp.where(rows == ids.astype(F32).astype(BF16), one, zero)
    rows = lax.broadcasted_iota(I32, (depth, ids.shape[1]), 0)
    return jnp.where(rows == ids, 1.0, 0.0).astype(BF16)


def slot_hot(slot, local, slots, depth):
    return jnp.concatenate(
        [one_hot(jnp.where(slot == at, local, -1), depth) for at in range(slots)], axis=0
    )


def eye(width):
    first = lax.broadcasted_iota(I32, (width, width), 0)
    second = lax.broadcasted_iota(I32, (width, width), 1)
    return jnp.where(first == second, 1.0, 0.0).astype(BF16)


def dot(left, right):
    return lax.dot_general(left, right, (((1,), (0,)), ((), ())), preferred_element_type=F32)


def dot_t(left, right):
    return lax.dot_general(left, right, (((1,), (1,)), ((), ())), preferred_element_type=F32)


def tree_sum(values):
    if len(values) == 1:
        return values[0]
    return tree_sum(values[0::2]) + tree_sum(values[1::2])


def vmem():
    return pl.BlockSpec(memory_space=pltpu.VMEM)


def smem():
    return pl.BlockSpec(memory_space=pltpu.SMEM)


def call(body, out_shape, n_in, scratch, flops, name, unread=0):
    many = isinstance(out_shape, (tuple, list))
    moved = 1 << 22
    return pl.pallas_call(
        body,
        out_shape=out_shape,
        in_specs=[smem()] + [vmem()] * n_in + [pl.BlockSpec(memory_space=pl.ANY)] * unread,
        out_specs=[vmem()] * len(out_shape) if many else vmem(),
        scratch_shapes=scratch,
        compiler_params=pltpu.CompilerParams(vmem_limit_bytes=VMEM_LIMIT),
        cost_estimate=pl.CostEstimate(flops=flops, bytes_accessed=moved, transcendentals=0),
        name=name,
    )


def prepare_kernel(heads, padded, fills, src, dst, rel, norm, coefs_t, dest, *outs):
    out_ref, coefs, dest_out = outs
    blocks = fills.shape[-1]
    out_ref[0:1, :] = src[0].astype(F32)
    out_ref[1:2, :] = dst[0].astype(F32)
    out_ref[2:3, :] = rel[0].astype(F32)
    lane = lax.broadcasted_iota(I32, (1, EDGE_BLOCK), 1)
    for at in range(blocks):
        here = slice(at * EDGE_BLOCK, (at + 1) * EDGE_BLOCK)
        live = jnp.where(lane < fills[0, 0, at], 1.0, 0.0)
        out_ref[3:4, here] = norm[0, :, here] * live
    dest_out[...] = dest[...]
    basis_count, relation_count = coefs_t.shape
    coefs[...] = jnp.zeros_like(coefs)
    for head in range(heads):
        live = min(LANES, relation_count - head * LANES)
        if live > 0:
            coefs[head * padded : head * padded + basis_count, 0:live] = coefs_t[
                :, head * LANES : head * LANES + live
            ]


def source_kernel(sizes, place, meta, meta_core, feats, feats_core, coefs, *refs):
    cols, shard, span, heads, padded, extra = sizes
    xt_ref, ct_ref, table = refs[extra:]
    count = cols // PAIR
    y, core = place[2], place[3]
    width = feats.shape[-1]
    edges = meta.shape[-1]
    unit = eye(width)
    for far, block in enumerate((feats, feats_core)):
        for sy in range(count):
            for xr in range(PAIR):
                at = (far * count + sy) * shard
                table[xr, :, at : at + shard] = dot_t(unit, block[sy, xr]).astype(BF16)
    for far, source in enumerate((meta, meta_core)):

        def step(index, carry, far=far, source=source):
            xr = index // (edges // span)
            at = pl.multiple_of(index % (edges // span) * span, span)
            ids = source[xr, 0:1, pl.ds(at, span)].astype(I32)
            owner, local = split_index(ids, shard)
            owner_y, owner_core = split_index(owner, PAIR)
            slot = (owner_core ^ core) * count + wrap(y - owner_y, count)
            rows = dot(table[xr], slot_hot(slot, local, cols, shard))
            xt_ref[far * PAIR + xr, :, pl.ds(at, span)] = rows.astype(BF16)
            relation = source[xr, 2:3, pl.ds(at, span)].astype(I32)
            high, low = split_index(relation, LANES)
            parts = dot(coefs[...], one_hot(low, LANES))
            total = jnp.zeros((padded, span), F32)
            for head in range(heads):
                total = total + jnp.where(
                    high == head, parts[head * padded : (head + 1) * padded], 0.0
                )
            ct_ref[far * PAIR + xr, :, pl.ds(at, span)] = total
            return carry

        lax.fori_loop(0, PAIR * (edges // span), step, 0, unroll=2)


def grad_kernel(sizes, place, meta, *refs):
    rows_total, shard, span = sizes
    count = rows_total // PAIR
    blocks = refs[:rows_total]
    gt_ref, table = refs[rows_total + 1 :]
    a, x = place[0], place[1]
    width = blocks[0].shape[-1]
    edges = meta.shape[-1]
    unit = eye(width)
    for at, block in enumerate(blocks):
        table[:, at * shard : (at + 1) * shard] = dot_t(unit, block[...]).astype(BF16)

    def step(index, carry):
        xr = index // (edges // span)
        at = pl.multiple_of(index % (edges // span) * span, span)
        ids = meta[xr, 1:2, pl.ds(at, span)].astype(I32)
        owner, local = split_index(ids, shard)
        owner_a, owner_x = split_index(owner, PAIR)
        slot = (owner_x ^ x) * count + wrap(a - owner_a, count)
        rows = dot(table[...], slot_hot(slot, local, rows_total, shard))
        weight = meta[xr, 3:4, pl.ds(at, span)]
        gt_ref[:, pl.ds(pl.multiple_of(index * span, span), span)] = (rows * weight).astype(BF16)
        return carry

    lax.fori_loop(0, PAIR * (edges // span), step, 0, unroll=2)


def forward_kernel(
    sizes, place, meta, gt_ref, xt_ref, ct_ref, bases_ref, *refs
):
    cols, shard, span, heads, padded, group = sizes
    outs = refs[:cols]
    total, inner, wide, coef_sum, *buffers = refs[cols:]
    count = cols // PAIR
    y, core = place[2], place[3]
    edges = meta.shape[-1]
    width = bases_ref.shape[-1]
    total[...] = jnp.zeros_like(total)
    inner[...] = jnp.zeros_like(inner)
    steps = bases_ref.shape[0] // group
    chunks = edges // span

    def product(number, index, buffer):
        stacked = bases_ref[pl.ds(number * group, group)].reshape(group * width, width)
        buffer[...] = dot(stacked, gt_ref[:, index * span : (index + 1) * span])

    def reduce(number, index, buffer):
        at = slice(index * span, (index + 1) * span)
        scales = [ct_ref[0, pl.ds(number * group + t, 1), at] for t in range(group)]
        parts = [jnp.zeros((8, span), F32) for _ in range(group)]
        for low in range(0, width, BAND):
            sums = total[low : low + BAND, at]
            rows = xt_ref[0, low : low + BAND, at].astype(F32)
            for t in range(group):
                mine = buffer[t * width + low : t * width + low + BAND, :]
                sums = sums + scales[t] * mine
                parts[t] = parts[t] + jnp.sum((mine * rows).reshape(BAND // 8, 8, span), axis=0)
            total[low : low + BAND, at] = sums
        for t in range(group):
            inner[pl.ds(number * group + t, 1), at] = jnp.sum(parts[t], axis=0, keepdims=True)

    product(0, 0, buffers[0])

    def step(number, carry):
        for index in range(chunks):
            if index + 1 < chunks:
                product(number, index + 1, buffers[(index + 1) % 2])
            else:
                product(jnp.minimum(number + 1, steps - 1), 0, buffers[(index + 1) % 2])
            reduce(number, index, buffers[index % 2])
        return carry

    lax.fori_loop(0, steps, step, 0)

    ids = meta[0, 0:1, :].astype(I32)
    owner, local = split_index(ids, shard)
    owner_y, owner_core = split_index(owner, PAIR)
    slot = (owner_core ^ core) * count + wrap(owner_y - y, count)
    values = total[...].astype(BF16)
    for at in range(cols):
        hot = one_hot(jnp.where(slot == at, local, -1), shard)
        outs[at][0:shard, :] = dot_t(hot, values).astype(BF16)
    high, low = split_index(meta[0, 2:3, :].astype(I32), LANES)
    for head in range(heads):
        wide[head * padded : (head + 1) * padded, :] = jnp.where(
            high == head, inner[...], 0.0
        ).astype(BF16)
    coef_sum[...] = dot_t(wide[...], one_hot(low, LANES))
    share = heads * padded // PAIR
    half = share // 2
    for far in range(PAIR):
        for side in range(2):
            at = pl.multiple_of((core ^ far) * share + side * half, 8)
            rows = coef_sum[pl.ds(at, half), :].astype(BF16)
            for sy in range(count):
                outs[far * count + sy][
                    shard : shard + half, side * LANES : (side + 1) * LANES
                ] = rows


def basis_kernel(sizes, place, gt_ref, gt_core, xt_ref, ct_ref, *refs):
    rows_total, cols, block, groups, basis_count, span, turns = sizes
    a_count, y_count = rows_total // PAIR, cols // PAIR
    a, x, y, core = place[0], place[1], place[2], place[3]
    outs = refs[:y_count]
    acc, left_even, left_odd, tiles = refs[len(outs) :]
    width, edges = xt_ref.shape[1], xt_ref.shape[2]
    tiles_wide = width // TILE
    cover = groups * TILE
    spread = tiles.shape[0] // (y_count * len(turns))
    steps = edges // span
    firsts = []
    for sy in range(y_count):
        for sz in turns:
            owner = ((a + sz) % a_count * PAIR + x) * cols + (y + sy) % y_count * PAIR + core
            firsts.append(owner * block // TILE)

    def build(part, at, left):
        for order, first in enumerate(firsts):
            base = first // tiles_wide
            for extra in range(spread):
                row = ct_ref[part, pl.ds(jnp.minimum(base + extra, basis_count - 1), 1), at]
                tiles[order * spread + extra] = jnp.broadcast_to(row, (TILE, span)).astype(BF16)
            for q in range(groups):
                tile = jnp.minimum(first + q, basis_count * tiles_wide - 1)
                lower = pl.multiple_of(tile % tiles_wide * TILE, TILE)
                to = (order * groups + q) * TILE
                left[to : to + TILE, :] = (
                    tiles[order * spread + tile // tiles_wide - base]
                    * xt_ref[part, pl.ds(lower, TILE), at]
                )

    for index in range(2 * PAIR * steps):
        part = index // steps
        at = slice(index % steps * span, (index % steps + 1) * span)
        left = left_even if index % 2 == 0 else left_odd
        build(part, at, left)
        grads = gt_ref if part < PAIR else gt_core
        here = index % (PAIR * steps) * span
        term = dot_t(left[...], grads[:, here : here + span])
        if index:
            acc[...] += term
        else:
            acc[...] = term
    size = len(turns) * cover
    for sy, out in enumerate(outs):
        out[...] = acc[sy * size : (sy + 1) * size, :].astype(out.dtype)


def coef_kernel(sizes, place, own, other, out_ref, whole):
    heads, padded, divisor = sizes
    core = place[3]
    share = heads * padded // PAIR
    half = share // 2
    for far, part in enumerate((own, other)):
        for side in range(2):
            at = pl.multiple_of((core ^ far) * share + side * half, 8)
            whole[pl.ds(at, half), :] = part[:, side * LANES : (side + 1) * LANES]
    width, total = out_ref.shape
    for head in range(heads):
        live = min(LANES, total - head * LANES)
        if live > 0:
            out_ref[:, head * LANES : head * LANES + live] = (
                whole[head * padded : head * padded + width, 0:live] / divisor
            )


def on_device(
    node_feats, dest_grad, bases, coefs, src_ids, dst_ids, rel_ids, edge_norm, block_fill
):
    rows_total = lax.axis_size("row")
    cols = lax.axis_size("col")
    a_count, y_count = rows_total // PAIR, cols // PAIR
    shard, width = node_feats.shape
    basis_count = bases.shape[0]
    relation_count = coefs.shape[0]
    edges = src_ids.size
    padded = round_up(basis_count, TILE)
    heads = round_up(relation_count, LANES) // LANES
    while heads * padded % (PAIR * 2 * TILE):
        heads += 1
    span = 256
    i = lax.axis_index("row")
    j = lax.axis_index("col")
    place = jnp.stack([i // PAIR, i % PAIR, j // PAIR, j % PAIR]).astype(I32)

    def flip_x(value):
        return lax.ppermute(value, "row", [(r, r ^ 1) for r in range(rows_total)])

    def flip_core(value):
        return lax.ppermute(value, "col", [(c, c ^ 1) for c in range(cols)])

    def turn_z(value, by):
        return lax.ppermute(
            value, "row", [(r, (r + by * PAIR) % rows_total) for r in range(rows_total)]
        )

    def turn_y(value, by):
        return lax.ppermute(value, "col", [(c, (c + by * PAIR) % cols) for c in range(cols)])

    own_dest = dest_grad[0]
    turned = [turn_z(own_dest, s) for s in range(1, a_count)]
    across_own = flip_x(own_dest)
    near = flip_x(node_feats)
    meta, coefs, own_dest = pl.pallas_call(
        functools.partial(prepare_kernel, heads, padded),
        out_shape=(
            jax.ShapeDtypeStruct((4, edges), F32),
            jax.ShapeDtypeStruct((heads * padded, LANES), BF16),
            jax.ShapeDtypeStruct(own_dest.shape, BF16),
        ),
        in_specs=[smem()] + [vmem()] * 6,
        out_specs=[vmem()] * 3,
        name="edge_table",
    )(block_fill, src_ids, dst_ids, rel_ids, edge_norm, coefs.T, own_dest)
    meta = jnp.stack([meta, flip_x(meta)])
    first = a_count // 2 - 1
    feats, turned[first] = lax.optimization_barrier(
        (jnp.stack([node_feats, near]), turned[first])
    )
    feats = jnp.stack([feats] + [turn_y(feats, s) for s in range(1, y_count)])
    across = [flip_x(turned[s]) if s == first else None for s in range(a_count - 1)]
    feats, meta, across_own, across[first], *turned = lax.optimization_barrier(
        (feats, meta, across_own, across[first], *turned)
    )
    dest = [own_dest] + turned
    across = [across_own] + [
        across[s] if s == first else flip_x(turned[s]) for s in range(a_count - 1)
    ]
    meta_core = flip_core(meta)
    feats_core = flip_core(feats)

    xt, ct = call(
        functools.partial(source_kernel, (cols, shard, span, heads, padded, a_count)),
        (
            jax.ShapeDtypeStruct((2 * PAIR, width, edges), BF16),
            jax.ShapeDtypeStruct((2 * PAIR, padded, edges), F32),
        ),
        5,
        [
            pltpu.VMEM((PAIR, width, cols * shard), BF16),
        ],
        2 * 4 * edges * cols * shard * width,
        "source_rows",
        a_count,
    )(place, meta, meta_core, feats, feats_core, coefs, *dest)

    dest_shard = own_dest.shape[0]
    gt = call(
        functools.partial(grad_kernel, (rows_total, dest_shard, span)),
        jax.ShapeDtypeStruct((width, PAIR * edges), BF16),
        1 + rows_total,
        [pltpu.VMEM((width, rows_total * dest_shard), BF16)],
        2 * 2 * edges * rows_total * dest_shard * width,
        "edge_grads",
        1,
    )(place, meta, *dest, *across, xt)
    gt_core = flip_core(gt)

    group = max(g for g in range(1, 6) if basis_count % g == 0)
    share_rows = heads * padded // PAIR // 2
    packed = call(
        functools.partial(forward_kernel, (cols, shard, span, heads, padded, group)),
        [jax.ShapeDtypeStruct((shard + share_rows, width), BF16)] * cols,
        5,
        [
            pltpu.VMEM((width, edges), F32),
            pltpu.VMEM((padded, edges), F32),
            pltpu.VMEM((heads * padded, edges), BF16),
            pltpu.VMEM((heads * padded, LANES), F32),
            pltpu.VMEM((group * width, span), F32),
            pltpu.VMEM((group * width, span), F32),
        ],
        2 * edges * width * width * basis_count,
        "backed_sums",
    )(place, meta, gt, xt, ct, bases)

    block = basis_count * width // (rows_total * cols)
    cover = block if block % TILE == 0 else round_up(block, TILE) + TILE

    def basis_blocks(place, turns):
        count = len(turns) * y_count
        return call(
            functools.partial(
                basis_kernel,
                (rows_total, cols, block, cover // TILE, basis_count, 2 * span, turns),
            ),
            [
                jax.ShapeDtypeStruct((len(turns) * cover, width), BF16 if sy else F32)
                for sy in range(y_count)
            ],
            4,
            [
                pltpu.VMEM((count * cover, width), F32),
                pltpu.VMEM((count * cover, 2 * span), BF16),
                pltpu.VMEM((count * cover, 2 * span), BF16),
                pltpu.VMEM((count * (round_up(cover, width) // width + 1), TILE, 2 * span), BF16),
            ],
            2 * 4 * edges * count * cover * width,
            "basis_terms",
        )(place, gt, gt_core, xt, ct)

    def to_col(value, far, sy):
        return lax.ppermute(
            value,
            "col",
            [(c, (c // PAIR + sy) % y_count * PAIR + (c % PAIR ^ far)) for c in range(cols)],
        )

    def after(value, other):
        return lax.optimization_barrier((value, other))[0]

    others = [(far, sy) for far in range(PAIR) for sy in range(y_count) if far or sy]
    received = [to_col(packed[far * y_count + sy], far, sy) for far, sy in others]

    order = tuple(range(1, a_count)) + (0,)
    half = (a_count + 1) // 2
    sums, where, landed = {}, place, []
    for turns in (order[:half], order[half:]):
        if turns:
            blocks = basis_blocks(where, turns)
            where = after(place, blocks[0])
            value = blocks[0]
            for sy in range(1, y_count):
                landed.append(turn_y(blocks[sy], sy))
                value = value + landed[-1].astype(F32)
            for at, sz in enumerate(turns):
                piece = value[at * cover : (at + 1) * cover]
                sums[sz] = turn_z(piece.astype(BF16), sz) if sz else piece
    joined = packed[0].astype(F32)
    for value in received:
        joined = joined + after(value, blocks[0]).astype(F32)
    basis_sum = sums[0]
    for sz in range(1, a_count):
        basis_sum = basis_sum + sums[sz].astype(F32)
    if cover != block:
        owner = i * cols + j
        basis_sum = lax.dynamic_slice_in_dim(basis_sum, owner * block % TILE, block, axis=0)
    basis_grad = basis_sum / cols

    node_grad = joined[:shard].astype(BF16)
    coef_part = joined[shard:]
    low = coef_part.astype(BF16)
    low = (low.astype(F32) + flip_x(low).astype(F32)).astype(BF16)
    low = after(low, landed[0])
    around = [turn_z(low, s).astype(F32) for s in range(1, a_count)]
    coef_part = tree_sum([low.astype(F32)] + around)
    coef_grad = call(
        functools.partial(coef_kernel, (heads, padded, cols)),
        jax.ShapeDtypeStruct((basis_count, relation_count), F32),
        2,
        [pltpu.VMEM((heads * padded, LANES), F32)],
        1 << 20,
        "coef_rows",
    )(place, coef_part, flip_core(coef_part))
    return (node_grad, basis_grad, coef_grad.T)


def solution(mesh):
    in_specs = (
        P(("row", "col"), None),
        P("col", "row", None),
        P(),
        P(),
        P("row", "col", None),
        P("row", "col", None),
        P("row", "col", None),
        P("row", "col", None),
        P("row", "col", None),
    )
    out_specs = (P(("row", "col"), None), P(("row", "col"), None), P())
    return jax.shard_map(
        on_device, mesh=mesh, in_specs=in_specs, out_specs=out_specs, check_vma=False
    )
```

```python
import functools
import jax
import jax.numpy as jnp
from jax import lax
from jax.experimental import pallas as pl
from jax.experimental.pallas import tpu as pltpu
from jax.sharding import PartitionSpec as P

EDGE_BLOCK = 128
TILE = 16
LANES = 128
PAIR = 2
F32 = jnp.float32
BF16 = jnp.bfloat16
I32 = jnp.int32
VMEM_LIMIT = 32 * 1024 * 1024


def round_up(value, unit):
    return (value + unit - 1) // unit * unit


def split_index(ids, size):
    if size & (size - 1) == 0:
        shift = size.bit_length() - 1
        return ids >> shift, ids & (size - 1)
    return ids // size, ids % size


def wrap(difference, size):
    return jnp.where(difference < 0, difference + size, difference)


def one_hot(ids, depth):
    if depth <= 256:
        rows = lax.broadcasted_iota(I32, (depth, ids.shape[1]), 0).astype(F32).astype(BF16)
        one, zero = jnp.ones((), BF16), jnp.zeros((), BF16)
        return jnp.where(rows == ids.astype(F32).astype(BF16), one, zero)
    rows = lax.broadcasted_iota(I32, (depth, ids.shape[1]), 0)
    return jnp.where(rows == ids, 1.0, 0.0).astype(BF16)


def slot_hot(slot, local, slots, depth):
    return jnp.concatenate(
        [one_hot(jnp.where(slot == at, local, -1), depth) for at in range(slots)], axis=0
    )


def eye(width):
    first = lax.broadcasted_iota(I32, (width, width), 0)
    second = lax.broadcasted_iota(I32, (width, width), 1)
    return jnp.where(first == second, 1.0, 0.0).astype(BF16)


def dot(left, right):
    return lax.dot_general(left, right, (((1,), (0,)), ((), ())), preferred_element_type=F32)


def dot_t(left, right):
    return lax.dot_general(left, right, (((1,), (1,)), ((), ())), preferred_element_type=F32)


def tree_sum(values):
    if len(values) == 1:
        return values[0]
    return tree_sum(values[0::2]) + tree_sum(values[1::2])


def vmem():
    return pl.BlockSpec(memory_space=pltpu.VMEM)


def smem():
    return pl.BlockSpec(memory_space=pltpu.SMEM)


def call(body, out_shape, n_in, scratch, flops, name, unread=0):
    many = isinstance(out_shape, (tuple, list))
    moved = 1 << 22
    return pl.pallas_call(
        body,
        out_shape=out_shape,
        in_specs=[smem()] + [vmem()] * n_in + [pl.BlockSpec(memory_space=pl.ANY)] * unread,
        out_specs=[vmem()] * len(out_shape) if many else vmem(),
        scratch_shapes=scratch,
        compiler_params=pltpu.CompilerParams(vmem_limit_bytes=VMEM_LIMIT),
        cost_estimate=pl.CostEstimate(flops=flops, bytes_accessed=moved, transcendentals=0),
        name=name,
    )


def prepare_kernel(heads, padded, fills, src, dst, rel, norm, coefs_t, dest, *outs):
    out_ref, coefs, dest_out = outs
    blocks = fills.shape[-1]
    out_ref[0:1, :] = src[0].astype(F32)
    out_ref[1:2, :] = dst[0].astype(F32)
    out_ref[2:3, :] = rel[0].astype(F32)
    lane = lax.broadcasted_iota(I32, (1, EDGE_BLOCK), 1)
    for at in range(blocks):
        here = slice(at * EDGE_BLOCK, (at + 1) * EDGE_BLOCK)
        live = jnp.where(lane < fills[0, 0, at], 1.0, 0.0)
        out_ref[3:4, here] = norm[0, :, here] * live
    dest_out[...] = dest[...]
    basis_count, relation_count = coefs_t.shape
    coefs[...] = jnp.zeros_like(coefs)
    for head in range(heads):
        live = min(LANES, relation_count - head * LANES)
        if live > 0:
            coefs[head * padded : head * padded + basis_count, 0:live] = coefs_t[
                :, head * LANES : head * LANES + live
            ]


def source_kernel(sizes, place, meta, meta_core, feats, feats_core, coefs, *refs):
    cols, shard, span, heads, padded, extra = sizes
    xt_ref, ct_ref, table = refs[extra:]
    count = cols // PAIR
    y, core = place[2], place[3]
    width = feats.shape[-1]
    edges = meta.shape[-1]
    unit = eye(width)
    for far, block in enumerate((feats, feats_core)):
        for sy in range(count):
            for xr in range(PAIR):
                at = (far * count + sy) * shard
                table[xr, :, at : at + shard] = dot_t(unit, block[sy, xr]).astype(BF16)
    for far, source in enumerate((meta, meta_core)):

        def step(index, carry, far=far, source=source):
            xr = index // (edges // span)
            at = pl.multiple_of(index % (edges // span) * span, span)
            ids = source[xr, 0:1, pl.ds(at, span)].astype(I32)
            owner, local = split_index(ids, shard)
            owner_y, owner_core = split_index(owner, PAIR)
            slot = (owner_core ^ core) * count + wrap(y - owner_y, count)
            rows = dot(table[xr], slot_hot(slot, local, cols, shard))
            xt_ref[far * PAIR + xr, :, pl.ds(at, span)] = rows.astype(BF16)
            relation = source[xr, 2:3, pl.ds(at, span)].astype(I32)
            high, low = split_index(relation, LANES)
            parts = dot(coefs[...], one_hot(low, LANES))
            total = jnp.zeros((padded, span), F32)
            for head in range(heads):
                total = total + jnp.where(
                    high == head, parts[head * padded : (head + 1) * padded], 0.0
                )
            ct_ref[far * PAIR + xr, :, pl.ds(at, span)] = total
            return carry

        lax.fori_loop(0, PAIR * (edges // span), step, 0, unroll=2)


def grad_kernel(sizes, place, meta, *refs):
    rows_total, shard, span = sizes
    count = rows_total // PAIR
    blocks = refs[:rows_total]
    gt_ref, table = refs[rows_total + 1 :]
    a, x = place[0], place[1]
    width = blocks[0].shape[-1]
    edges = meta.shape[-1]
    unit = eye(width)
    for at, block in enumerate(blocks):
        table[:, at * shard : (at + 1) * shard] = dot_t(unit, block[...]).astype(BF16)

    def step(index, carry):
        xr = index // (edges // span)
        at = pl.multiple_of(index % (edges // span) * span, span)
        ids = meta[xr, 1:2, pl.ds(at, span)].astype(I32)
        owner, local = split_index(ids, shard)
        owner_a, owner_x = split_index(owner, PAIR)
        slot = (owner_x ^ x) * count + wrap(a - owner_a, count)
        rows = dot(table[...], slot_hot(slot, local, rows_total, shard))
        weight = meta[xr, 3:4, pl.ds(at, span)]
        gt_ref[:, pl.ds(pl.multiple_of(index * span, span), span)] = (rows * weight).astype(BF16)
        return carry

    lax.fori_loop(0, PAIR * (edges // span), step, 0, unroll=2)


def forward_kernel(
    sizes, place, meta, gt_ref, xt_ref, ct_ref, bases_ref, *refs
):
    cols, shard, span, heads, padded, group = sizes
    outs = refs[:cols]
    total, inner, wide, coef_sum = refs[cols:]
    count = cols // PAIR
    y, core = place[2], place[3]
    edges = meta.shape[-1]
    width = bases_ref.shape[-1]
    total[...] = jnp.zeros_like(total)
    inner[...] = jnp.zeros_like(inner)

    def step(number, carry):
        stacked = bases_ref[pl.ds(number * group, group)].reshape(group * width, width)
        for index in range(edges // span):
            at = slice(index * span, (index + 1) * span)
            backed = dot(stacked, gt_ref[:, at])
            rows = xt_ref[0, :, at].astype(F32)
            sums = total[:, at]
            for t in range(group):
                base = number * group + t
                mine = backed[t * width : (t + 1) * width]
                sums = sums + ct_ref[0, pl.ds(base, 1), at] * mine
                inner[pl.ds(base, 1), at] = jnp.sum(mine * rows, axis=0, keepdims=True)
            total[:, at] = sums
        return carry

    lax.fori_loop(0, bases_ref.shape[0] // group, step, 0)

    ids = meta[0, 0:1, :].astype(I32)
    owner, local = split_index(ids, shard)
    owner_y, owner_core = split_index(owner, PAIR)
    slot = (owner_core ^ core) * count + wrap(owner_y - y, count)
    values = total[...].astype(BF16)
    for at in range(cols):
        hot = one_hot(jnp.where(slot == at, local, -1), shard)
        outs[at][0:shard, :] = dot_t(hot, values).astype(BF16)
    high, low = split_index(meta[0, 2:3, :].astype(I32), LANES)
    for head in range(heads):
        wide[head * padded : (head + 1) * padded, :] = jnp.where(
            high == head, inner[...], 0.0
        ).astype(BF16)
    coef_sum[...] = dot_t(wide[...], one_hot(low, LANES))
    share = heads * padded // PAIR
    half = share // 2
    for far in range(PAIR):
        for side in range(2):
            at = pl.multiple_of((core ^ far) * share + side * half, 8)
            rows = coef_sum[pl.ds(at, half), :].astype(BF16)
            for sy in range(count):
                outs[far * count + sy][
                    shard : shard + half, side * LANES : (side + 1) * LANES
                ] = rows


def basis_kernel(sizes, place, gt_ref, gt_core, xt_ref, ct_ref, *refs):
    rows_total, cols, block, groups, basis_count, span, turns = sizes
    a_count, y_count = rows_total // PAIR, cols // PAIR
    a, x, y, core = place[0], place[1], place[2], place[3]
    outs = refs[:y_count]
    acc, left_even, left_odd, tiles = refs[len(outs) :]
    width, edges = xt_ref.shape[1], xt_ref.shape[2]
    tiles_wide = width // TILE
    cover = groups * TILE
    spread = tiles.shape[0] // (y_count * len(turns))
    steps = edges // span
    firsts = []
    for sy in range(y_count):
        for sz in turns:
            owner = ((a + sz) % a_count * PAIR + x) * cols + (y + sy) % y_count * PAIR + core
            firsts.append(owner * block // TILE)

    def build(part, at, left):
        for order, first in enumerate(firsts):
            base = first // tiles_wide
            for extra in range(spread):
                row = ct_ref[part, pl.ds(jnp.minimum(base + extra, basis_count - 1), 1), at]
                tiles[order * spread + extra] = jnp.broadcast_to(row, (TILE, span)).astype(BF16)
            for q in range(groups):
                tile = jnp.minimum(first + q, basis_count * tiles_wide - 1)
                lower = pl.multiple_of(tile % tiles_wide * TILE, TILE)
                to = (order * groups + q) * TILE
                left[to : to + TILE, :] = (
                    tiles[order * spread + tile // tiles_wide - base]
                    * xt_ref[part, pl.ds(lower, TILE), at]
                )

    for index in range(2 * PAIR * steps):
        part = index // steps
        at = slice(index % steps * span, (index % steps + 1) * span)
        left = left_even if index % 2 == 0 else left_odd
        build(part, at, left)
        grads = gt_ref if part < PAIR else gt_core
        here = index % (PAIR * steps) * span
        term = dot_t(left[...], grads[:, here : here + span])
        if index:
            acc[...] += term
        else:
            acc[...] = term
    size = len(turns) * cover
    for sy, out in enumerate(outs):
        out[...] = acc[sy * size : (sy + 1) * size, :].astype(out.dtype)


def coef_kernel(sizes, place, own, other, out_ref, whole):
    heads, padded, divisor = sizes
    core = place[3]
    share = heads * padded // PAIR
    half = share // 2
    for far, part in enumerate((own, other)):
        for side in range(2):
            at = pl.multiple_of((core ^ far) * share + side * half, 8)
            whole[pl.ds(at, half), :] = part[:, side * LANES : (side + 1) * LANES]
    width, total = out_ref.shape
    for head in range(heads):
        live = min(LANES, total - head * LANES)
        if live > 0:
            out_ref[:, head * LANES : head * LANES + live] = (
                whole[head * padded : head * padded + width, 0:live] / divisor
            )


def on_device(
    node_feats, dest_grad, bases, coefs, src_ids, dst_ids, rel_ids, edge_norm, block_fill
):
    rows_total = lax.axis_size("row")
    cols = lax.axis_size("col")
    a_count, y_count = rows_total // PAIR, cols // PAIR
    shard, width = node_feats.shape
    basis_count = bases.shape[0]
    relation_count = coefs.shape[0]
    edges = src_ids.size
    padded = round_up(basis_count, TILE)
    heads = round_up(relation_count, LANES) // LANES
    while heads * padded % (PAIR * 2 * TILE):
        heads += 1
    span = 256
    i = lax.axis_index("row")
    j = lax.axis_index("col")
    place = jnp.stack([i // PAIR, i % PAIR, j // PAIR, j % PAIR]).astype(I32)

    def flip_x(value):
        return lax.ppermute(value, "row", [(r, r ^ 1) for r in range(rows_total)])

    def flip_core(value):
        return lax.ppermute(value, "col", [(c, c ^ 1) for c in range(cols)])

    def turn_z(value, by):
        return lax.ppermute(
            value, "row", [(r, (r + by * PAIR) % rows_total) for r in range(rows_total)]
        )

    def turn_y(value, by):
        return lax.ppermute(value, "col", [(c, (c + by * PAIR) % cols) for c in range(cols)])

    own_dest = dest_grad[0]
    turned = [turn_z(own_dest, s) for s in range(1, a_count)]
    across_own = flip_x(own_dest)
    near = flip_x(node_feats)
    meta, coefs, own_dest = pl.pallas_call(
        functools.partial(prepare_kernel, heads, padded),
        out_shape=(
            jax.ShapeDtypeStruct((4, edges), F32),
            jax.ShapeDtypeStruct((heads * padded, LANES), BF16),
            jax.ShapeDtypeStruct(own_dest.shape, BF16),
        ),
        in_specs=[smem()] + [vmem()] * 6,
        out_specs=[vmem()] * 3,
        compiler_params=pltpu.CompilerParams(vmem_limit_bytes=VMEM_LIMIT),
        name="edge_table",
    )(block_fill, src_ids, dst_ids, rel_ids, edge_norm, coefs.T, own_dest)
    meta = jnp.stack([meta, flip_x(meta)])
    middle = (a_count - 1) // 2
    sides = [s for s in range(a_count - 1) if s != middle]
    feats, *early = lax.optimization_barrier(
        (jnp.stack([node_feats, near]), *[turned[s] for s in sides])
    )
    for s, value in zip(sides, early):
        turned[s] = value
    feats = jnp.stack([feats] + [turn_y(feats, s) for s in range(1, y_count)])
    across = [None if s == middle else flip_x(turned[s]) for s in range(a_count - 1)]
    feats, meta, across_own, turned[middle], *early = lax.optimization_barrier(
        (feats, meta, across_own, turned[middle], *[across[s] for s in sides])
    )
    for s, value in zip(sides, early):
        across[s] = value
    across[middle] = flip_x(turned[middle])
    dest = [own_dest] + turned
    across = [across_own] + across
    meta_core = flip_core(meta)
    feats_core = flip_core(feats)

    xt, ct = call(
        functools.partial(source_kernel, (cols, shard, span, heads, padded, a_count)),
        (
            jax.ShapeDtypeStruct((2 * PAIR, width, edges), BF16),
            jax.ShapeDtypeStruct((2 * PAIR, padded, edges), F32),
        ),
        5,
        [
            pltpu.VMEM((PAIR, width, cols * shard), BF16),
        ],
        2 * 4 * edges * cols * shard * width,
        "source_rows",
        a_count,
    )(place, meta, meta_core, feats, feats_core, coefs, *dest)

    dest_shard = own_dest.shape[0]
    gt = call(
        functools.partial(grad_kernel, (rows_total, dest_shard, span)),
        jax.ShapeDtypeStruct((width, PAIR * edges), BF16),
        1 + rows_total,
        [pltpu.VMEM((width, rows_total * dest_shard), BF16)],
        2 * 2 * edges * rows_total * dest_shard * width,
        "edge_grads",
        1,
    )(place, meta, *dest, *across, xt)
    gt_core = flip_core(gt)

    group = max(g for g in range(1, 6) if basis_count % g == 0)
    share_rows = heads * padded // PAIR // 2
    packed = call(
        functools.partial(forward_kernel, (cols, shard, span, heads, padded, group)),
        [jax.ShapeDtypeStruct((shard + share_rows, width), BF16)] * cols,
        5,
        [
            pltpu.VMEM((width, edges), F32),
            pltpu.VMEM((padded, edges), F32),
            pltpu.VMEM((heads * padded, edges), BF16),
            pltpu.VMEM((heads * padded, LANES), F32),
        ],
        2 * edges * width * width * basis_count,
        "backed_sums",
    )(place, meta, gt, xt, ct, bases)

    block = basis_count * width // (rows_total * cols)
    cover = block if block % TILE == 0 else round_up(block, TILE) + TILE

    def basis_blocks(place, turns):
        count = len(turns) * y_count
        return call(
            functools.partial(
                basis_kernel,
                (rows_total, cols, block, cover // TILE, basis_count, 2 * span, turns),
            ),
            [
                jax.ShapeDtypeStruct((len(turns) * cover, width), BF16 if sy else F32)
                for sy in range(y_count)
            ],
            4,
            [
                pltpu.VMEM((count * cover, width), F32),
                pltpu.VMEM((count * cover, 2 * span), BF16),
                pltpu.VMEM((count * cover, 2 * span), BF16),
                pltpu.VMEM((count * (round_up(cover, width) // width + 1), TILE, 2 * span), BF16),
            ],
            2 * 4 * edges * count * cover * width,
            "basis_terms",
        )(place, gt, gt_core, xt, ct)

    def to_col(value, far, sy):
        return lax.ppermute(
            value,
            "col",
            [(c, (c // PAIR + sy) % y_count * PAIR + (c % PAIR ^ far)) for c in range(cols)],
        )

    def after(value, other):
        return lax.optimization_barrier((value, other))[0]

    others = [(far, sy) for far in range(PAIR) for sy in range(y_count) if far or sy]
    received = [to_col(packed[far * y_count + sy], far, sy) for far, sy in others]

    order = tuple(range(1, a_count)) + (0,)
    half = (a_count + 1) // 2
    sums, where, landed = {}, place, []
    for turns in (order[:half], order[half:]):
        if turns:
            blocks = basis_blocks(where, turns)
            where = after(place, blocks[0])
            value = blocks[0]
            for sy in range(1, y_count):
                landed.append(turn_y(blocks[sy], sy))
                value = value + landed[-1].astype(F32)
            for at, sz in enumerate(turns):
                piece = value[at * cover : (at + 1) * cover]
                sums[sz] = turn_z(piece.astype(BF16), sz) if sz else piece
    joined = packed[0].astype(F32)
    for value in received:
        joined = joined + after(value, blocks[0]).astype(F32)
    basis_sum = sums[0]
    for sz in range(1, a_count):
        basis_sum = basis_sum + sums[sz].astype(F32)
    if cover != block:
        owner = i * cols + j
        basis_sum = lax.dynamic_slice_in_dim(basis_sum, owner * block % TILE, block, axis=0)
    basis_grad = basis_sum / cols

    node_grad = joined[:shard].astype(BF16)
    coef_part = joined[shard:]
    low = after(coef_part.astype(BF16), landed[0])
    low = (low.astype(F32) + flip_x(low).astype(F32)).astype(BF16)
    around = [turn_z(low, s).astype(F32) for s in range(1, a_count)]
    coef_part = tree_sum([low.astype(F32)] + around)
    coef_grad = call(
        functools.partial(coef_kernel, (heads, padded, cols)),
        jax.ShapeDtypeStruct((basis_count, relation_count), F32),
        2,
        [pltpu.VMEM((heads * padded, LANES), F32)],
        1 << 20,
        "coef_rows",
    )(place, coef_part, flip_core(coef_part))
    return (node_grad, basis_grad, coef_grad.T)


def solution(mesh):
    in_specs = (
        P(("row", "col"), None),
        P("col", "row", None),
        P(),
        P(),
        P("row", "col", None),
        P("row", "col", None),
        P("row", "col", None),
        P("row", "col", None),
        P("row", "col", None),
    )
    out_specs = (P(("row", "col"), None), P(("row", "col"), None), P())
    return jax.shard_map(
        on_device, mesh=mesh, in_specs=in_specs, out_specs=out_specs, check_vma=False
    )
```

```python
import functools
import jax
import jax.numpy as jnp
from jax import lax
from jax.experimental import pallas as pl
from jax.experimental.pallas import tpu as pltpu
from jax.sharding import PartitionSpec as P

EDGE_BLOCK = 128
TILE = 16
LANES = 128
PAIR = 2
F32 = jnp.float32
BF16 = jnp.bfloat16
I32 = jnp.int32
VMEM_LIMIT = 32 * 1024 * 1024


def round_up(value, unit):
    return (value + unit - 1) // unit * unit


def split_index(ids, size):
    if size & (size - 1) == 0:
        shift = size.bit_length() - 1
        return ids >> shift, ids & (size - 1)
    return ids // size, ids % size


def wrap(difference, size):
    return jnp.where(difference < 0, difference + size, difference)


def one_hot(ids, depth):
    if depth <= 256:
        rows = lax.broadcasted_iota(I32, (depth, ids.shape[1]), 0).astype(F32).astype(BF16)
        one, zero = jnp.ones((), BF16), jnp.zeros((), BF16)
        return jnp.where(rows == ids.astype(F32).astype(BF16), one, zero)
    rows = lax.broadcasted_iota(I32, (depth, ids.shape[1]), 0)
    return jnp.where(rows == ids, 1.0, 0.0).astype(BF16)


def slot_hot(slot, local, slots, depth):
    return jnp.concatenate(
        [one_hot(jnp.where(slot == at, local, -1), depth) for at in range(slots)], axis=0
    )


def eye(width):
    first = lax.broadcasted_iota(I32, (width, width), 0)
    second = lax.broadcasted_iota(I32, (width, width), 1)
    return jnp.where(first == second, 1.0, 0.0).astype(BF16)


def dot(left, right):
    return lax.dot_general(left, right, (((1,), (0,)), ((), ())), preferred_element_type=F32)


def dot_t(left, right):
    return lax.dot_general(left, right, (((1,), (1,)), ((), ())), preferred_element_type=F32)


def tree_sum(values):
    if len(values) == 1:
        return values[0]
    return tree_sum(values[0::2]) + tree_sum(values[1::2])


def vmem():
    return pl.BlockSpec(memory_space=pltpu.VMEM)


def smem():
    return pl.BlockSpec(memory_space=pltpu.SMEM)


def call(body, out_shape, n_in, scratch, flops, name, unread=0):
    many = isinstance(out_shape, (tuple, list))
    moved = 1 << 22
    return pl.pallas_call(
        body,
        out_shape=out_shape,
        in_specs=[smem()] + [vmem()] * n_in + [pl.BlockSpec(memory_space=pl.ANY)] * unread,
        out_specs=[vmem()] * len(out_shape) if many else vmem(),
        scratch_shapes=scratch,
        compiler_params=pltpu.CompilerParams(vmem_limit_bytes=VMEM_LIMIT),
        cost_estimate=pl.CostEstimate(flops=flops, bytes_accessed=moved, transcendentals=0),
        name=name,
    )


def prepare_kernel(fills, src, dst, rel, norm, out_ref):
    blocks = fills.shape[-1]
    out_ref[0:1, :] = src[0].astype(F32)
    out_ref[1:2, :] = dst[0].astype(F32)
    out_ref[2:3, :] = rel[0].astype(F32)
    lane = lax.broadcasted_iota(I32, (1, EDGE_BLOCK), 1)
    for at in range(blocks):
        here = slice(at * EDGE_BLOCK, (at + 1) * EDGE_BLOCK)
        live = jnp.where(lane < fills[0, 0, at], 1.0, 0.0)
        out_ref[3:4, here] = norm[0, :, here] * live


def source_kernel(sizes, place, meta, meta_core, feats, feats_core, *refs):
    cols, shard, span, extra = sizes
    xt_ref, table = refs[extra:]
    count = cols // PAIR
    y, core = place[2], place[3]
    width = feats.shape[-1]
    edges = meta.shape[-1]
    unit = eye(width)
    for far, block in enumerate((feats, feats_core)):
        for sy in range(count):
            for xr in range(PAIR):
                at = (far * count + sy) * shard
                table[xr, :, at : at + shard] = dot_t(unit, block[sy, xr]).astype(BF16)
    for far, source in enumerate((meta, meta_core)):

        def step(index, carry, far=far, source=source):
            xr = index // (edges // span)
            at = pl.multiple_of(index % (edges // span) * span, span)
            ids = source[xr, 0:1, pl.ds(at, span)].astype(I32)
            owner, local = split_index(ids, shard)
            owner_y, owner_core = split_index(owner, PAIR)
            slot = (owner_core ^ core) * count + wrap(y - owner_y, count)
            rows = dot(table[xr], slot_hot(slot, local, cols, shard))
            xt_ref[far * PAIR + xr, :, pl.ds(at, span)] = rows.astype(BF16)
            return carry

        lax.fori_loop(0, PAIR * (edges // span), step, 0, unroll=2)


def grad_kernel(sizes, place, meta, meta_core, coefs_t, *refs):
    rows_total, shard, span, heads, padded = sizes
    count = rows_total // PAIR
    blocks = refs[:rows_total]
    gt_ref, ct_ref, table, coefs = refs[rows_total + 1 :]
    a, x = place[0], place[1]
    width = blocks[0].shape[-1]
    edges = meta.shape[-1]
    unit = eye(width)
    for at, block in enumerate(blocks):
        table[:, at * shard : (at + 1) * shard] = dot_t(unit, block[...]).astype(BF16)

    basis_count, relation_count = coefs_t.shape
    coefs[...] = jnp.zeros_like(coefs)
    for head in range(heads):
        live = min(LANES, relation_count - head * LANES)
        if live > 0:
            coefs[head * padded : head * padded + basis_count, 0:live] = coefs_t[
                :, head * LANES : head * LANES + live
            ]

    def step(index, carry):
        xr = index // (edges // span)
        at = pl.multiple_of(index % (edges // span) * span, span)
        ids = meta[xr, 1:2, pl.ds(at, span)].astype(I32)
        owner, local = split_index(ids, shard)
        owner_a, owner_x = split_index(owner, PAIR)
        slot = (owner_x ^ x) * count + wrap(a - owner_a, count)
        rows = dot(table[...], slot_hot(slot, local, rows_total, shard))
        weight = meta[xr, 3:4, pl.ds(at, span)]
        gt_ref[:, pl.ds(pl.multiple_of(index * span, span), span)] = (rows * weight).astype(BF16)
        for far, source in enumerate((meta, meta_core)):
            relation = source[xr, 2:3, pl.ds(at, span)].astype(I32)
            high, low = split_index(relation, LANES)
            parts = dot(coefs[...], one_hot(low, LANES))
            total = jnp.zeros((padded, span), F32)
            for head in range(heads):
                total = total + jnp.where(
                    high == head, parts[head * padded : (head + 1) * padded], 0.0
                )
            ct_ref[far * PAIR + xr, :, pl.ds(at, span)] = total
        return carry

    lax.fori_loop(0, PAIR * (edges // span), step, 0, unroll=2)


def forward_kernel(
    sizes, place, meta, gt_ref, xt_ref, ct_ref, bases_ref, *refs
):
    cols, shard, span, heads, padded, group = sizes
    outs = refs[:cols]
    total, inner, wide, coef_sum = refs[cols:]
    count = cols // PAIR
    y, core = place[2], place[3]
    edges = meta.shape[-1]
    width = bases_ref.shape[-1]
    total[...] = jnp.zeros_like(total)
    inner[...] = jnp.zeros_like(inner)

    def step(number, carry):
        stacked = bases_ref[pl.ds(number * group, group)].reshape(group * width, width)
        for index in range(edges // span):
            at = slice(index * span, (index + 1) * span)
            backed = dot(stacked, gt_ref[:, at])
            rows = xt_ref[0, :, at].astype(F32)
            sums = total[:, at]
            for t in range(group):
                base = number * group + t
                mine = backed[t * width : (t + 1) * width]
                sums = sums + ct_ref[0, pl.ds(base, 1), at] * mine
                inner[pl.ds(base, 1), at] = jnp.sum(mine * rows, axis=0, keepdims=True)
            total[:, at] = sums
        return carry

    lax.fori_loop(0, bases_ref.shape[0] // group, step, 0)

    ids = meta[0, 0:1, :].astype(I32)
    owner, local = split_index(ids, shard)
    owner_y, owner_core = split_index(owner, PAIR)
    slot = (owner_core ^ core) * count + wrap(owner_y - y, count)
    values = total[...].astype(BF16)
    for at in range(cols):
        hot = one_hot(jnp.where(slot == at, local, -1), shard)
        outs[at][0:shard, :] = dot_t(hot, values).astype(BF16)
    high, low = split_index(meta[0, 2:3, :].astype(I32), LANES)
    for head in range(heads):
        wide[head * padded : (head + 1) * padded, :] = jnp.where(
            high == head, inner[...], 0.0
        ).astype(BF16)
    coef_sum[...] = dot_t(wide[...], one_hot(low, LANES))
    share = heads * padded // PAIR
    half = share // 2
    for far in range(PAIR):
        for side in range(2):
            at = pl.multiple_of((core ^ far) * share + side * half, 8)
            rows = coef_sum[pl.ds(at, half), :].astype(BF16)
            for sy in range(count):
                outs[far * count + sy][
                    shard : shard + half, side * LANES : (side + 1) * LANES
                ] = rows


def basis_kernel(sizes, place, gt_ref, gt_core, xt_ref, ct_ref, *refs):
    rows_total, cols, block, groups, basis_count, span, turns = sizes
    a_count, y_count = rows_total // PAIR, cols // PAIR
    a, x, y, core = place[0], place[1], place[2], place[3]
    outs = refs[:y_count]
    acc, left_even, left_odd, tiles = refs[len(outs) :]
    width, edges = xt_ref.shape[1], xt_ref.shape[2]
    tiles_wide = width // TILE
    cover = groups * TILE
    spread = tiles.shape[0] // (y_count * len(turns))
    steps = edges // span
    firsts = []
    for sy in range(y_count):
        for sz in turns:
            owner = ((a + sz) % a_count * PAIR + x) * cols + (y + sy) % y_count * PAIR + core
            firsts.append(owner * block // TILE)

    def build(part, at, left):
        for order, first in enumerate(firsts):
            base = first // tiles_wide
            for extra in range(spread):
                row = ct_ref[part, pl.ds(jnp.minimum(base + extra, basis_count - 1), 1), at]
                tiles[order * spread + extra] = jnp.broadcast_to(row, (TILE, span)).astype(BF16)
            for q in range(groups):
                tile = jnp.minimum(first + q, basis_count * tiles_wide - 1)
                lower = pl.multiple_of(tile % tiles_wide * TILE, TILE)
                to = (order * groups + q) * TILE
                left[to : to + TILE, :] = (
                    tiles[order * spread + tile // tiles_wide - base]
                    * xt_ref[part, pl.ds(lower, TILE), at]
                )

    for index in range(2 * PAIR * steps):
        part = index // steps
        at = slice(index % steps * span, (index % steps + 1) * span)
        left = left_even if index % 2 == 0 else left_odd
        build(part, at, left)
        grads = gt_ref if part < PAIR else gt_core
        here = index % (PAIR * steps) * span
        term = dot_t(left[...], grads[:, here : here + span])
        if index:
            acc[...] += term
        else:
            acc[...] = term
    size = len(turns) * cover
    for sy, out in enumerate(outs):
        out[...] = acc[sy * size : (sy + 1) * size, :].astype(out.dtype)


def coef_kernel(sizes, place, own, other, out_ref, whole):
    heads, padded, divisor = sizes
    core = place[3]
    share = heads * padded // PAIR
    half = share // 2
    for far, part in enumerate((own, other)):
        for side in range(2):
            at = pl.multiple_of((core ^ far) * share + side * half, 8)
            whole[pl.ds(at, half), :] = part[:, side * LANES : (side + 1) * LANES]
    width, total = out_ref.shape
    for head in range(heads):
        live = min(LANES, total - head * LANES)
        if live > 0:
            out_ref[:, head * LANES : head * LANES + live] = (
                whole[head * padded : head * padded + width, 0:live] / divisor
            )


def on_device(
    node_feats, dest_grad, bases, coefs, src_ids, dst_ids, rel_ids, edge_norm, block_fill
):
    rows_total = lax.axis_size("row")
    cols = lax.axis_size("col")
    a_count, y_count = rows_total // PAIR, cols // PAIR
    shard, width = node_feats.shape
    basis_count = bases.shape[0]
    relation_count = coefs.shape[0]
    edges = src_ids.size
    padded = round_up(basis_count, TILE)
    heads = round_up(relation_count, LANES) // LANES
    while heads * padded % (PAIR * 2 * TILE):
        heads += 1
    span = 256
    i = lax.axis_index("row")
    j = lax.axis_index("col")
    place = jnp.stack([i // PAIR, i % PAIR, j // PAIR, j % PAIR]).astype(I32)

    def flip_x(value):
        return lax.ppermute(value, "row", [(r, r ^ 1) for r in range(rows_total)])

    def flip_core(value):
        return lax.ppermute(value, "col", [(c, c ^ 1) for c in range(cols)])

    def turn_z(value, by):
        return lax.ppermute(
            value, "row", [(r, (r + by * PAIR) % rows_total) for r in range(rows_total)]
        )

    def turn_y(value, by):
        return lax.ppermute(value, "col", [(c, (c + by * PAIR) % cols) for c in range(cols)])

    own_dest = dest_grad[0]
    turned = [turn_z(own_dest, s) for s in range(1, a_count)]
    across_own = flip_x(own_dest)
    near = flip_x(node_feats)
    meta = pl.pallas_call(
        prepare_kernel,
        out_shape=jax.ShapeDtypeStruct((4, edges), F32),
        in_specs=[smem()] + [vmem()] * 4,
        out_specs=vmem(),
        name="edge_table",
    )(block_fill, src_ids, dst_ids, rel_ids, edge_norm)
    meta = jnp.stack([meta, flip_x(meta)])
    middle = (a_count - 1) // 2
    sides = [s for s in range(a_count - 1) if s != middle]
    feats, meta, across_own, *early = lax.optimization_barrier(
        (jnp.stack([node_feats, near]), meta, across_own, *[turned[s] for s in sides])
    )
    for s, value in zip(sides, early):
        turned[s] = value
    feats = jnp.stack([feats] + [turn_y(feats, s) for s in range(1, y_count)])
    across = [None if s == middle else flip_x(turned[s]) for s in range(a_count - 1)]
    feats, turned[middle], *early = lax.optimization_barrier(
        (feats, turned[middle], *[across[s] for s in sides])
    )
    for s, value in zip(sides, early):
        across[s] = value
    across[middle] = flip_x(turned[middle])
    dest = [own_dest] + turned
    across = [across_own] + across
    meta_core = flip_core(meta)
    feats_core = flip_core(feats)

    xt = call(
        functools.partial(source_kernel, (cols, shard, span, a_count - 1)),
        jax.ShapeDtypeStruct((2 * PAIR, width, edges), BF16),
        4,
        [pltpu.VMEM((PAIR, width, cols * shard), BF16)],
        2 * 4 * edges * cols * shard * width,
        "source_rows",
        a_count - 1,
    )(place, meta, meta_core, feats, feats_core, *turned)

    dest_shard = own_dest.shape[0]
    gt, ct = call(
        functools.partial(grad_kernel, (rows_total, dest_shard, span, heads, padded)),
        (
            jax.ShapeDtypeStruct((width, PAIR * edges), BF16),
            jax.ShapeDtypeStruct((2 * PAIR, padded, edges), F32),
        ),
        3 + rows_total,
        [
            pltpu.VMEM((width, rows_total * dest_shard), BF16),
            pltpu.VMEM((heads * padded, LANES), BF16),
        ],
        2 * 2 * edges * rows_total * dest_shard * width,
        "edge_grads",
        1,
    )(place, meta, meta_core, coefs.T, *dest, *across, xt)
    gt_core = flip_core(gt)

    group = max(g for g in range(1, 6) if basis_count % g == 0)
    share_rows = heads * padded // PAIR // 2
    packed = call(
        functools.partial(forward_kernel, (cols, shard, span, heads, padded, group)),
        [jax.ShapeDtypeStruct((shard + share_rows, width), BF16)] * cols,
        5,
        [
            pltpu.VMEM((width, edges), F32),
            pltpu.VMEM((padded, edges), F32),
            pltpu.VMEM((heads * padded, edges), BF16),
            pltpu.VMEM((heads * padded, LANES), F32),
        ],
        2 * edges * width * width * basis_count,
        "backed_sums",
    )(place, meta, gt, xt, ct, bases)

    block = basis_count * width // (rows_total * cols)
    cover = block if block % TILE == 0 else round_up(block, TILE) + TILE

    def basis_blocks(place, turns):
        count = len(turns) * y_count
        return call(
            functools.partial(
                basis_kernel,
                (rows_total, cols, block, cover // TILE, basis_count, 2 * span, turns),
            ),
            [
                jax.ShapeDtypeStruct((len(turns) * cover, width), BF16 if sy else F32)
                for sy in range(y_count)
            ],
            4,
            [
                pltpu.VMEM((count * cover, width), F32),
                pltpu.VMEM((count * cover, 2 * span), BF16),
                pltpu.VMEM((count * cover, 2 * span), BF16),
                pltpu.VMEM((count * (round_up(cover, width) // width + 1), TILE, 2 * span), BF16),
            ],
            2 * 4 * edges * count * cover * width,
            "basis_terms",
        )(place, gt, gt_core, xt, ct)

    def to_col(value, far, sy):
        return lax.ppermute(
            value,
            "col",
            [(c, (c // PAIR + sy) % y_count * PAIR + (c % PAIR ^ far)) for c in range(cols)],
        )

    def after(value, other):
        return lax.optimization_barrier((value, other))[0]

    others = [(far, sy) for far in range(PAIR) for sy in range(y_count) if far or sy]
    received = [to_col(packed[far * y_count + sy], far, sy) for far, sy in others]

    order = tuple(range(1, a_count)) + (0,)
    half = (a_count + 1) // 2
    sums, landed = {}, []
    for turns in (order[:half], order[half:]):
        if turns:
            blocks = basis_blocks(place, turns)
            value = blocks[0]
            for sy in range(1, y_count):
                landed.append(turn_y(blocks[sy], sy))
                value = value + landed[-1].astype(F32)
            for at, sz in enumerate(turns):
                piece = value[at * cover : (at + 1) * cover]
                sums[sz] = turn_z(piece.astype(BF16), sz) if sz else piece
    joined = packed[0].astype(F32)
    for value in received:
        joined = joined + after(value, blocks[0]).astype(F32)
    basis_sum = sums[0]
    for sz in range(1, a_count):
        basis_sum = basis_sum + sums[sz].astype(F32)
    if cover != block:
        owner = i * cols + j
        basis_sum = lax.dynamic_slice_in_dim(basis_sum, owner * block % TILE, block, axis=0)
    basis_grad = basis_sum / cols

    node_grad = joined[:shard].astype(BF16)
    coef_part = joined[shard:]
    low = after(coef_part.astype(BF16), landed[0])
    low = (low.astype(F32) + flip_x(low).astype(F32)).astype(BF16)
    around = [turn_z(low, s).astype(F32) for s in range(1, a_count)]
    coef_part = tree_sum([low.astype(F32)] + around)
    coef_grad = call(
        functools.partial(coef_kernel, (heads, padded, cols)),
        jax.ShapeDtypeStruct((basis_count, relation_count), F32),
        2,
        [pltpu.VMEM((heads * padded, LANES), F32)],
        1 << 20,
        "coef_rows",
    )(place, coef_part, flip_core(coef_part))
    return (node_grad, basis_grad, coef_grad.T)


def solution(mesh):
    in_specs = (
        P(("row", "col"), None),
        P("col", "row", None),
        P(),
        P(),
        P("row", "col", None),
        P("row", "col", None),
        P("row", "col", None),
        P("row", "col", None),
        P("row", "col", None),
    )
    out_specs = (P(("row", "col"), None), P(("row", "col"), None), P())
    return jax.shard_map(
        on_device, mesh=mesh, in_specs=in_specs, out_specs=out_specs, check_vma=False
    )
```

```python
import functools
import jax
import jax.numpy as jnp
from jax import lax
from jax.experimental import pallas as pl
from jax.experimental.pallas import tpu as pltpu
from jax.sharding import PartitionSpec as P

EDGE_BLOCK = 128
TILE = 16
LANES = 128
PAIR = 2
F32 = jnp.float32
BF16 = jnp.bfloat16
I32 = jnp.int32
VMEM_LIMIT = 32 * 1024 * 1024


def round_up(value, unit):
    return (value + unit - 1) // unit * unit


def split_index(ids, size):
    if size & (size - 1) == 0:
        shift = size.bit_length() - 1
        return ids >> shift, ids & (size - 1)
    return ids // size, ids % size


def wrap(difference, size):
    return jnp.where(difference < 0, difference + size, difference)


def one_hot(ids, depth):
    if depth <= 256:
        rows = lax.broadcasted_iota(I32, (depth, ids.shape[1]), 0).astype(F32).astype(BF16)
        one, zero = jnp.ones((), BF16), jnp.zeros((), BF16)
        return jnp.where(rows == ids.astype(F32).astype(BF16), one, zero)
    rows = lax.broadcasted_iota(I32, (depth, ids.shape[1]), 0)
    return jnp.where(rows == ids, 1.0, 0.0).astype(BF16)


def slot_hot(slot, local, slots, depth):
    return jnp.concatenate(
        [one_hot(jnp.where(slot == at, local, -1), depth) for at in range(slots)], axis=0
    )


def eye(width):
    first = lax.broadcasted_iota(I32, (width, width), 0)
    second = lax.broadcasted_iota(I32, (width, width), 1)
    return jnp.where(first == second, 1.0, 0.0).astype(BF16)


def dot(left, right):
    return lax.dot_general(left, right, (((1,), (0,)), ((), ())), preferred_element_type=F32)


def dot_t(left, right):
    return lax.dot_general(left, right, (((1,), (1,)), ((), ())), preferred_element_type=F32)


def tree_sum(values):
    if len(values) == 1:
        return values[0]
    return tree_sum(values[0::2]) + tree_sum(values[1::2])


def vmem():
    return pl.BlockSpec(memory_space=pltpu.VMEM)


def smem():
    return pl.BlockSpec(memory_space=pltpu.SMEM)


def call(body, out_shape, n_in, scratch, flops, name, unread=0):
    many = isinstance(out_shape, (tuple, list))
    moved = 1 << 22
    return pl.pallas_call(
        body,
        out_shape=out_shape,
        in_specs=[smem()] + [vmem()] * n_in + [pl.BlockSpec(memory_space=pl.ANY)] * unread,
        out_specs=[vmem()] * len(out_shape) if many else vmem(),
        scratch_shapes=scratch,
        compiler_params=pltpu.CompilerParams(vmem_limit_bytes=VMEM_LIMIT),
        cost_estimate=pl.CostEstimate(flops=flops, bytes_accessed=moved, transcendentals=0),
        name=name,
    )


def prepare_kernel(fills, src, dst, rel, norm, out_ref):
    blocks = fills.shape[-1]
    out_ref[0:1, :] = src[0].astype(F32)
    out_ref[1:2, :] = dst[0].astype(F32)
    out_ref[2:3, :] = rel[0].astype(F32)
    lane = lax.broadcasted_iota(I32, (1, EDGE_BLOCK), 1)
    for at in range(blocks):
        here = slice(at * EDGE_BLOCK, (at + 1) * EDGE_BLOCK)
        live = jnp.where(lane < fills[0, 0, at], 1.0, 0.0)
        out_ref[3:4, here] = norm[0, :, here] * live


def source_kernel(sizes, place, meta, meta_core, feats, feats_core, *refs):
    cols, shard, span, extra = sizes
    xt_ref, table = refs[extra:]
    count = cols // PAIR
    y, core = place[2], place[3]
    width = feats.shape[-1]
    edges = meta.shape[-1]
    unit = eye(width)
    for far, block in enumerate((feats, feats_core)):
        for sy in range(count):
            for xr in range(PAIR):
                at = (far * count + sy) * shard
                table[xr, :, at : at + shard] = dot_t(unit, block[sy, xr]).astype(BF16)
    for far, source in enumerate((meta, meta_core)):

        def step(index, carry, far=far, source=source):
            xr = index // (edges // span)
            at = pl.multiple_of(index % (edges // span) * span, span)
            ids = source[xr, 0:1, pl.ds(at, span)].astype(I32)
            owner, local = split_index(ids, shard)
            owner_y, owner_core = split_index(owner, PAIR)
            slot = (owner_core ^ core) * count + wrap(y - owner_y, count)
            rows = dot(table[xr], slot_hot(slot, local, cols, shard))
            xt_ref[far * PAIR + xr, :, pl.ds(at, span)] = rows.astype(BF16)
            return carry

        lax.fori_loop(0, PAIR * (edges // span), step, 0, unroll=2)


def grad_kernel(sizes, place, meta, meta_core, coefs_t, *refs):
    rows_total, shard, span, heads, padded = sizes
    count = rows_total // PAIR
    blocks = refs[:rows_total]
    gt_ref, ct_ref, table, coefs = refs[rows_total + 1 :]
    a, x = place[0], place[1]
    width = blocks[0].shape[-1]
    edges = meta.shape[-1]
    unit = eye(width)
    for at, block in enumerate(blocks):
        table[:, at * shard : (at + 1) * shard] = dot_t(unit, block[...]).astype(BF16)

    basis_count, relation_count = coefs_t.shape
    coefs[...] = jnp.zeros_like(coefs)
    for head in range(heads):
        live = min(LANES, relation_count - head * LANES)
        if live > 0:
            coefs[head * padded : head * padded + basis_count, 0:live] = coefs_t[
                :, head * LANES : head * LANES + live
            ]

    def step(index, carry):
        xr = index // (edges // span)
        at = pl.multiple_of(index % (edges // span) * span, span)
        ids = meta[xr, 1:2, pl.ds(at, span)].astype(I32)
        owner, local = split_index(ids, shard)
        owner_a, owner_x = split_index(owner, PAIR)
        slot = (owner_x ^ x) * count + wrap(a - owner_a, count)
        rows = dot(table[...], slot_hot(slot, local, rows_total, shard))
        weight = meta[xr, 3:4, pl.ds(at, span)]
        gt_ref[:, pl.ds(pl.multiple_of(index * span, span), span)] = (rows * weight).astype(BF16)
        for far, source in enumerate((meta, meta_core)):
            relation = source[xr, 2:3, pl.ds(at, span)].astype(I32)
            high, low = split_index(relation, LANES)
            parts = dot(coefs[...], one_hot(low, LANES))
            total = jnp.zeros((padded, span), F32)
            for head in range(heads):
                total = total + jnp.where(
                    high == head, parts[head * padded : (head + 1) * padded], 0.0
                )
            ct_ref[far * PAIR + xr, :, pl.ds(at, span)] = total
        return carry

    lax.fori_loop(0, PAIR * (edges // span), step, 0, unroll=2)


def forward_kernel(
    sizes, place, meta, gt_ref, xt_ref, ct_ref, bases_ref, *refs
):
    cols, shard, span, heads, padded, group = sizes
    outs, halves = refs[:cols], refs[cols : cols + PAIR]
    total, inner, wide, coef_sum = refs[cols + PAIR :]
    count = cols // PAIR
    y, core = place[2], place[3]
    edges = meta.shape[-1]
    width = bases_ref.shape[-1]
    total[...] = jnp.zeros_like(total)
    inner[...] = jnp.zeros_like(inner)

    def step(number, carry):
        stacked = bases_ref[pl.ds(number * group, group)].reshape(group * width, width)
        for index in range(edges // span):
            at = slice(index * span, (index + 1) * span)
            backed = dot(stacked, gt_ref[:, at])
            rows = xt_ref[0, :, at].astype(F32)
            sums = total[:, at]
            for t in range(group):
                base = number * group + t
                mine = backed[t * width : (t + 1) * width]
                sums = sums + ct_ref[0, pl.ds(base, 1), at] * mine
                inner[pl.ds(base, 1), at] = jnp.sum(mine * rows, axis=0, keepdims=True)
            total[:, at] = sums
        return carry

    lax.fori_loop(0, bases_ref.shape[0] // group, step, 0)

    ids = meta[0, 0:1, :].astype(I32)
    owner, local = split_index(ids, shard)
    owner_y, owner_core = split_index(owner, PAIR)
    slot = (owner_core ^ core) * count + wrap(owner_y - y, count)
    values = total[...].astype(BF16)
    for at in range(cols):
        hot = one_hot(jnp.where(slot == at, local, -1), shard)
        outs[at][...] = dot_t(hot, values).astype(BF16)
    high, low = split_index(meta[0, 2:3, :].astype(I32), LANES)
    for head in range(heads):
        wide[head * padded : (head + 1) * padded, :] = jnp.where(
            high == head, inner[...], 0.0
        ).astype(BF16)
    coef_sum[...] = dot_t(wide[...], one_hot(low, LANES))
    share = heads * padded // PAIR
    half = share // 2
    for far in range(PAIR):
        for side in range(2):
            at = pl.multiple_of((core ^ far) * share + side * half, 8)
            halves[far][:, side * LANES : (side + 1) * LANES] = coef_sum[pl.ds(at, half), :]


def basis_kernel(sizes, place, gt_ref, gt_core, xt_ref, ct_ref, *refs):
    rows_total, cols, block, groups, basis_count, span, turns = sizes
    a_count, y_count = rows_total // PAIR, cols // PAIR
    a, x, y, core = place[0], place[1], place[2], place[3]
    outs = refs[:y_count]
    acc, left_even, left_odd, tiles = refs[len(outs) :]
    width, edges = xt_ref.shape[1], xt_ref.shape[2]
    tiles_wide = width // TILE
    cover = groups * TILE
    spread = tiles.shape[0] // (y_count * len(turns))
    steps = edges // span
    firsts = []
    for sy in range(y_count):
        for sz in turns:
            owner = ((a + sz) % a_count * PAIR + x) * cols + (y + sy) % y_count * PAIR + core
            firsts.append(owner * block // TILE)

    def build(part, at, left):
        for order, first in enumerate(firsts):
            base = first // tiles_wide
            for extra in range(spread):
                row = ct_ref[part, pl.ds(jnp.minimum(base + extra, basis_count - 1), 1), at]
                tiles[order * spread + extra] = jnp.broadcast_to(row, (TILE, span)).astype(BF16)
            for q in range(groups):
                tile = jnp.minimum(first + q, basis_count * tiles_wide - 1)
                lower = pl.multiple_of(tile % tiles_wide * TILE, TILE)
                to = (order * groups + q) * TILE
                left[to : to + TILE, :] = (
                    tiles[order * spread + tile // tiles_wide - base]
                    * xt_ref[part, pl.ds(lower, TILE), at]
                )

    for index in range(2 * PAIR * steps):
        part = index // steps
        at = slice(index % steps * span, (index % steps + 1) * span)
        left = left_even if index % 2 == 0 else left_odd
        build(part, at, left)
        grads = gt_ref if part < PAIR else gt_core
        here = index % (PAIR * steps) * span
        term = dot_t(left[...], grads[:, here : here + span])
        if index:
            acc[...] += term
        else:
            acc[...] = term
    size = len(turns) * cover
    for sy, out in enumerate(outs):
        out[...] = acc[sy * size : (sy + 1) * size, :].astype(out.dtype)


def coef_kernel(sizes, place, own, other, out_ref, whole):
    heads, padded, divisor = sizes
    core = place[3]
    share = heads * padded // PAIR
    half = share // 2
    for far, part in enumerate((own, other)):
        for side in range(2):
            at = pl.multiple_of((core ^ far) * share + side * half, 8)
            whole[pl.ds(at, half), :] = part[:, side * LANES : (side + 1) * LANES]
    width, total = out_ref.shape
    for head in range(heads):
        live = min(LANES, total - head * LANES)
        if live > 0:
            out_ref[:, head * LANES : head * LANES + live] = (
                whole[head * padded : head * padded + width, 0:live] / divisor
            )


def on_device(
    node_feats, dest_grad, bases, coefs, src_ids, dst_ids, rel_ids, edge_norm, block_fill
):
    rows_total = lax.axis_size("row")
    cols = lax.axis_size("col")
    a_count, y_count = rows_total // PAIR, cols // PAIR
    shard, width = node_feats.shape
    basis_count = bases.shape[0]
    relation_count = coefs.shape[0]
    edges = src_ids.size
    padded = round_up(basis_count, TILE)
    heads = round_up(relation_count, LANES) // LANES
    while heads * padded % (PAIR * 2 * TILE):
        heads += 1
    span = 256
    i = lax.axis_index("row")
    j = lax.axis_index("col")
    place = jnp.stack([i // PAIR, i % PAIR, j // PAIR, j % PAIR]).astype(I32)

    def flip_x(value):
        return lax.ppermute(value, "row", [(r, r ^ 1) for r in range(rows_total)])

    def flip_core(value):
        return lax.ppermute(value, "col", [(c, c ^ 1) for c in range(cols)])

    def turn_z(value, by):
        return lax.ppermute(
            value, "row", [(r, (r + by * PAIR) % rows_total) for r in range(rows_total)]
        )

    def turn_y(value, by):
        return lax.ppermute(value, "col", [(c, (c + by * PAIR) % cols) for c in range(cols)])

    own_dest = dest_grad[0]
    turned = [turn_z(own_dest, s) for s in range(1, a_count)]
    across_own = flip_x(own_dest)
    near = flip_x(node_feats)
    meta = pl.pallas_call(
        prepare_kernel,
        out_shape=jax.ShapeDtypeStruct((4, edges), F32),
        in_specs=[smem()] + [vmem()] * 4,
        out_specs=vmem(),
        name="edge_table",
    )(block_fill, src_ids, dst_ids, rel_ids, edge_norm)
    meta = jnp.stack([meta, flip_x(meta)])
    middle = (a_count - 1) // 2
    sides = [s for s in range(a_count - 1) if s != middle]
    feats, meta, across_own, *early = lax.optimization_barrier(
        (jnp.stack([node_feats, near]), meta, across_own, *[turned[s] for s in sides])
    )
    for s, value in zip(sides, early):
        turned[s] = value
    feats = jnp.stack([feats] + [turn_y(feats, s) for s in range(1, y_count)])
    across = [None if s == middle else flip_x(turned[s]) for s in range(a_count - 1)]
    feats, turned[middle], *early = lax.optimization_barrier(
        (feats, turned[middle], *[across[s] for s in sides])
    )
    for s, value in zip(sides, early):
        across[s] = value
    across[middle] = flip_x(turned[middle])
    dest = [own_dest] + turned
    across = [across_own] + across
    meta_core = flip_core(meta)
    feats_core = flip_core(feats)

    xt = call(
        functools.partial(source_kernel, (cols, shard, span, a_count - 1)),
        jax.ShapeDtypeStruct((2 * PAIR, width, edges), BF16),
        4,
        [pltpu.VMEM((PAIR, width, cols * shard), BF16)],
        2 * 4 * edges * cols * shard * width,
        "source_rows",
        a_count - 1,
    )(place, meta, meta_core, feats, feats_core, *turned)

    dest_shard = own_dest.shape[0]
    gt, ct = call(
        functools.partial(grad_kernel, (rows_total, dest_shard, span, heads, padded)),
        (
            jax.ShapeDtypeStruct((width, PAIR * edges), BF16),
            jax.ShapeDtypeStruct((2 * PAIR, padded, edges), F32),
        ),
        3 + rows_total,
        [
            pltpu.VMEM((width, rows_total * dest_shard), BF16),
            pltpu.VMEM((heads * padded, LANES), BF16),
        ],
        2 * 2 * edges * rows_total * dest_shard * width,
        "edge_grads",
        1,
    )(place, meta, meta_core, coefs.T, *dest, *across, xt)
    gt_core = flip_core(gt)

    group = max(g for g in range(1, 6) if basis_count % g == 0)
    share_rows = heads * padded // PAIR // 2
    packed = call(
        functools.partial(forward_kernel, (cols, shard, span, heads, padded, group)),
        [jax.ShapeDtypeStruct((shard, width), BF16)] * cols
        + [jax.ShapeDtypeStruct((share_rows, width), F32)] * PAIR,
        5,
        [
            pltpu.VMEM((width, edges), F32),
            pltpu.VMEM((padded, edges), F32),
            pltpu.VMEM((heads * padded, edges), BF16),
            pltpu.VMEM((heads * padded, LANES), F32),
        ],
        2 * edges * width * width * basis_count,
        "backed_sums",
    )(place, meta, gt, xt, ct, bases)

    block = basis_count * width // (rows_total * cols)
    cover = block if block % TILE == 0 else round_up(block, TILE) + TILE

    def basis_blocks(place, turns):
        count = len(turns) * y_count
        return call(
            functools.partial(
                basis_kernel,
                (rows_total, cols, block, cover // TILE, basis_count, 2 * span, turns),
            ),
            [
                jax.ShapeDtypeStruct((len(turns) * cover, width), BF16 if sy else F32)
                for sy in range(y_count)
            ],
            4,
            [
                pltpu.VMEM((count * cover, width), F32),
                pltpu.VMEM((count * cover, 2 * span), BF16),
                pltpu.VMEM((count * cover, 2 * span), BF16),
                pltpu.VMEM((count * (round_up(cover, width) // width + 1), TILE, 2 * span), BF16),
            ],
            2 * 4 * edges * count * cover * width,
            "basis_terms",
        )(place, gt, gt_core, xt, ct)

    def to_col(value, far, sy):
        return lax.ppermute(
            value,
            "col",
            [(c, (c // PAIR + sy) % y_count * PAIR + (c % PAIR ^ far)) for c in range(cols)],
        )

    def after(value, other):
        return lax.optimization_barrier((value, other))[0]

    others = [(far, sy) for far in range(PAIR) for sy in range(y_count) if far or sy]
    received = [to_col(packed[far * y_count + sy], far, sy) for far, sy in others]

    coef_part = packed[cols] + flip_core(packed[cols + 1])
    where = [after(place, coef_part)]
    coef_part = coef_part + flip_x(coef_part)
    where.append(after(place, coef_part))
    low = coef_part.astype(BF16)
    around = [turn_z(low, s) for s in range(1, a_count)]

    order = tuple(range(1, a_count)) + (0,)
    half = (a_count + 1) // 2
    sums, landed = {}, []
    for start, turns in zip(where, (order[:half], order[half:])):
        if turns:
            if sums:
                start = after(start, blocks[0])
            blocks = basis_blocks(start, turns)
            value = blocks[0]
            for sy in range(1, y_count):
                landed.append(turn_y(blocks[sy], sy))
                value = value + landed[-1].astype(F32)
            for at, sz in enumerate(turns):
                piece = value[at * cover : (at + 1) * cover]
                sums[sz] = turn_z(piece.astype(BF16), sz) if sz else piece
    around = [after(value, landed[0]) for value in around]
    coef_part = tree_sum([low.astype(F32)] + [value.astype(F32) for value in around])
    joined = packed[0].astype(F32)
    for value in received:
        joined = joined + after(value, blocks[0]).astype(F32)
    basis_sum = sums[0]
    for sz in range(1, a_count):
        basis_sum = basis_sum + sums[sz].astype(F32)
    if cover != block:
        owner = i * cols + j
        basis_sum = lax.dynamic_slice_in_dim(basis_sum, owner * block % TILE, block, axis=0)
    basis_grad = basis_sum / cols

    node_grad = joined.astype(BF16)
    low = after(coef_part.astype(BF16), landed[0])
    coef_part = tree_sum([low.astype(F32)] + [turn_y(low, s).astype(F32) for s in range(1, y_count)])
    coef_grad = call(
        functools.partial(coef_kernel, (heads, padded, cols)),
        jax.ShapeDtypeStruct((basis_count, relation_count), F32),
        2,
        [pltpu.VMEM((heads * padded, LANES), F32)],
        1 << 20,
        "coef_rows",
    )(place, coef_part, flip_core(coef_part))
    return (node_grad, basis_grad, coef_grad.T)


def solution(mesh):
    in_specs = (
        P(("row", "col"), None),
        P("col", "row", None),
        P(),
        P(),
        P("row", "col", None),
        P("row", "col", None),
        P("row", "col", None),
        P("row", "col", None),
        P("row", "col", None),
    )
    out_specs = (P(("row", "col"), None), P(("row", "col"), None), P())
    return jax.shard_map(
        on_device, mesh=mesh, in_specs=in_specs, out_specs=out_specs, check_vma=False
    )
```

```python
import functools
import jax
import jax.numpy as jnp
from jax import lax
from jax.experimental import pallas as pl
from jax.experimental.pallas import tpu as pltpu
from jax.sharding import PartitionSpec as P

EDGE_BLOCK = 128
TILE = 16
LANES = 128
PAIR = 2
F32 = jnp.float32
BF16 = jnp.bfloat16
I32 = jnp.int32
VMEM_LIMIT = 32 * 1024 * 1024


def round_up(value, unit):
    return (value + unit - 1) // unit * unit


def split_index(ids, size):
    if size & (size - 1) == 0:
        shift = size.bit_length() - 1
        return ids >> shift, ids & (size - 1)
    return ids // size, ids % size


def wrap(difference, size):
    return jnp.where(difference < 0, difference + size, difference)


def one_hot(ids, depth):
    if depth <= 256:
        rows = lax.broadcasted_iota(I32, (depth, ids.shape[1]), 0).astype(F32).astype(BF16)
        one, zero = jnp.ones((), BF16), jnp.zeros((), BF16)
        return jnp.where(rows == ids.astype(F32).astype(BF16), one, zero)
    rows = lax.broadcasted_iota(I32, (depth, ids.shape[1]), 0)
    return jnp.where(rows == ids, 1.0, 0.0).astype(BF16)


def slot_hot(slot, local, slots, depth):
    return jnp.concatenate(
        [one_hot(jnp.where(slot == at, local, -1), depth) for at in range(slots)], axis=0
    )


def eye(width):
    first = lax.broadcasted_iota(I32, (width, width), 0)
    second = lax.broadcasted_iota(I32, (width, width), 1)
    return jnp.where(first == second, 1.0, 0.0).astype(BF16)


def dot(left, right):
    return lax.dot_general(left, right, (((1,), (0,)), ((), ())), preferred_element_type=F32)


def dot_t(left, right):
    return lax.dot_general(left, right, (((1,), (1,)), ((), ())), preferred_element_type=F32)


def tree_sum(values):
    if len(values) == 1:
        return values[0]
    return tree_sum(values[0::2]) + tree_sum(values[1::2])


def vmem():
    return pl.BlockSpec(memory_space=pltpu.VMEM)


def smem():
    return pl.BlockSpec(memory_space=pltpu.SMEM)


def call(body, out_shape, n_in, scratch, flops, name, unread=0):
    many = isinstance(out_shape, (tuple, list))
    moved = 1 << 22
    return pl.pallas_call(
        body,
        out_shape=out_shape,
        in_specs=[smem()] + [vmem()] * n_in + [pl.BlockSpec(memory_space=pl.ANY)] * unread,
        out_specs=[vmem()] * len(out_shape) if many else vmem(),
        scratch_shapes=scratch,
        compiler_params=pltpu.CompilerParams(vmem_limit_bytes=VMEM_LIMIT),
        cost_estimate=pl.CostEstimate(flops=flops, bytes_accessed=moved, transcendentals=0),
        name=name,
    )


def prepare_kernel(fills, src, dst, rel, norm, out_ref):
    blocks = fills.shape[-1]
    out_ref[0:1, :] = src[0].astype(F32)
    out_ref[1:2, :] = dst[0].astype(F32)
    out_ref[2:3, :] = rel[0].astype(F32)
    lane = lax.broadcasted_iota(I32, (1, EDGE_BLOCK), 1)
    for at in range(blocks):
        here = slice(at * EDGE_BLOCK, (at + 1) * EDGE_BLOCK)
        live = jnp.where(lane < fills[0, 0, at], 1.0, 0.0)
        out_ref[3:4, here] = norm[0, :, here] * live


def source_kernel(sizes, place, meta, meta_core, feats, feats_core, *refs):
    cols, shard, span, extra = sizes
    xt_ref, table = refs[extra:]
    count = cols // PAIR
    y, core = place[2], place[3]
    width = feats.shape[-1]
    edges = meta.shape[-1]
    unit = eye(width)
    for far, block in enumerate((feats, feats_core)):
        for sy in range(count):
            for xr in range(PAIR):
                at = (far * count + sy) * shard
                table[xr, :, at : at + shard] = dot_t(unit, block[sy, xr]).astype(BF16)
    for far, source in enumerate((meta, meta_core)):

        def step(index, carry, far=far, source=source):
            xr = index // (edges // span)
            at = pl.multiple_of(index % (edges // span) * span, span)
            ids = source[xr, 0:1, pl.ds(at, span)].astype(I32)
            owner, local = split_index(ids, shard)
            owner_y, owner_core = split_index(owner, PAIR)
            slot = (owner_core ^ core) * count + wrap(y - owner_y, count)
            rows = dot(table[xr], slot_hot(slot, local, cols, shard))
            xt_ref[far * PAIR + xr, :, pl.ds(at, span)] = rows.astype(BF16)
            return carry

        lax.fori_loop(0, PAIR * (edges // span), step, 0, unroll=2)


def grad_kernel(sizes, place, meta, meta_core, coefs_t, *refs):
    rows_total, shard, span, heads, padded = sizes
    count = rows_total // PAIR
    blocks = refs[:rows_total]
    gt_ref, ct_ref, table, coefs = refs[rows_total + 1 :]
    a, x = place[0], place[1]
    width = blocks[0].shape[-1]
    edges = meta.shape[-1]
    unit = eye(width)
    for at, block in enumerate(blocks):
        table[:, at * shard : (at + 1) * shard] = dot_t(unit, block[...]).astype(BF16)

    basis_count, relation_count = coefs_t.shape
    coefs[...] = jnp.zeros_like(coefs)
    for head in range(heads):
        live = min(LANES, relation_count - head * LANES)
        if live > 0:
            coefs[head * padded : head * padded + basis_count, 0:live] = coefs_t[
                :, head * LANES : head * LANES + live
            ]

    def step(index, carry):
        xr = index // (edges // span)
        at = pl.multiple_of(index % (edges // span) * span, span)
        ids = meta[xr, 1:2, pl.ds(at, span)].astype(I32)
        owner, local = split_index(ids, shard)
        owner_a, owner_x = split_index(owner, PAIR)
        slot = (owner_x ^ x) * count + wrap(a - owner_a, count)
        rows = dot(table[...], slot_hot(slot, local, rows_total, shard))
        weight = meta[xr, 3:4, pl.ds(at, span)]
        gt_ref[:, pl.ds(pl.multiple_of(index * span, span), span)] = (rows * weight).astype(BF16)
        for far, source in enumerate((meta, meta_core)):
            relation = source[xr, 2:3, pl.ds(at, span)].astype(I32)
            high, low = split_index(relation, LANES)
            parts = dot(coefs[...], one_hot(low, LANES))
            total = jnp.zeros((padded, span), F32)
            for head in range(heads):
                total = total + jnp.where(
                    high == head, parts[head * padded : (head + 1) * padded], 0.0
                )
            ct_ref[far * PAIR + xr, :, pl.ds(at, span)] = total
        return carry

    lax.fori_loop(0, PAIR * (edges // span), step, 0, unroll=2)


def forward_kernel(
    sizes, place, meta, gt_ref, xt_ref, ct_ref, bases_ref, *refs
):
    cols, shard, span, heads, padded, group = sizes
    outs, halves = refs[:cols], refs[cols : cols + PAIR]
    total, inner, wide, coef_sum = refs[cols + PAIR :]
    count = cols // PAIR
    y, core = place[2], place[3]
    edges = meta.shape[-1]
    width = bases_ref.shape[-1]
    total[...] = jnp.zeros_like(total)
    inner[...] = jnp.zeros_like(inner)

    def step(number, carry):
        stacked = bases_ref[pl.ds(number * group, group)].reshape(group * width, width)
        for index in range(edges // span):
            at = slice(index * span, (index + 1) * span)
            backed = dot(stacked, gt_ref[:, at])
            rows = xt_ref[0, :, at].astype(F32)
            sums = total[:, at]
            for t in range(group):
                base = number * group + t
                mine = backed[t * width : (t + 1) * width]
                sums = sums + ct_ref[0, pl.ds(base, 1), at] * mine
                inner[pl.ds(base, 1), at] = jnp.sum(mine * rows, axis=0, keepdims=True)
            total[:, at] = sums
        return carry

    lax.fori_loop(0, bases_ref.shape[0] // group, step, 0)

    ids = meta[0, 0:1, :].astype(I32)
    owner, local = split_index(ids, shard)
    owner_y, owner_core = split_index(owner, PAIR)
    slot = (owner_core ^ core) * count + wrap(owner_y - y, count)
    values = total[...].astype(BF16)
    for at in range(cols):
        hot = one_hot(jnp.where(slot == at, local, -1), shard)
        outs[at][...] = dot_t(hot, values).astype(BF16)
    high, low = split_index(meta[0, 2:3, :].astype(I32), LANES)
    for head in range(heads):
        wide[head * padded : (head + 1) * padded, :] = jnp.where(
            high == head, inner[...], 0.0
        ).astype(BF16)
    coef_sum[...] = dot_t(wide[...], one_hot(low, LANES))
    share = heads * padded // PAIR
    half = share // 2
    for far in range(PAIR):
        for side in range(2):
            at = pl.multiple_of((core ^ far) * share + side * half, 8)
            halves[far][:, side * LANES : (side + 1) * LANES] = coef_sum[pl.ds(at, half), :]


def basis_kernel(sizes, place, gt_ref, gt_core, xt_ref, ct_ref, *refs):
    rows_total, cols, block, groups, basis_count, span, turns = sizes
    a_count, y_count = rows_total // PAIR, cols // PAIR
    a, x, y, core = place[0], place[1], place[2], place[3]
    outs = refs[:y_count]
    acc, left_even, left_odd, tiles = refs[len(outs) :]
    width, edges = xt_ref.shape[1], xt_ref.shape[2]
    tiles_wide = width // TILE
    cover = groups * TILE
    spread = tiles.shape[0] // (y_count * len(turns))
    steps = edges // span
    firsts = []
    for sy in range(y_count):
        for sz in turns:
            owner = ((a + sz) % a_count * PAIR + x) * cols + (y + sy) % y_count * PAIR + core
            firsts.append(owner * block // TILE)

    def build(part, at, left):
        for order, first in enumerate(firsts):
            base = first // tiles_wide
            for extra in range(spread):
                row = ct_ref[part, pl.ds(jnp.minimum(base + extra, basis_count - 1), 1), at]
                tiles[order * spread + extra] = jnp.broadcast_to(row, (TILE, span)).astype(BF16)
            for q in range(groups):
                tile = jnp.minimum(first + q, basis_count * tiles_wide - 1)
                lower = pl.multiple_of(tile % tiles_wide * TILE, TILE)
                to = (order * groups + q) * TILE
                left[to : to + TILE, :] = (
                    tiles[order * spread + tile // tiles_wide - base]
                    * xt_ref[part, pl.ds(lower, TILE), at]
                )

    for index in range(2 * PAIR * steps):
        part = index // steps
        at = slice(index % steps * span, (index % steps + 1) * span)
        left = left_even if index % 2 == 0 else left_odd
        build(part, at, left)
        grads = gt_ref if part < PAIR else gt_core
        here = index % (PAIR * steps) * span
        term = dot_t(left[...], grads[:, here : here + span])
        if index:
            acc[...] += term
        else:
            acc[...] = term
    size = len(turns) * cover
    for sy, out in enumerate(outs):
        out[...] = acc[sy * size : (sy + 1) * size, :].astype(out.dtype)


def coef_kernel(sizes, place, own, other, out_ref, whole):
    heads, padded, divisor = sizes
    core = place[3]
    share = heads * padded // PAIR
    half = share // 2
    for far, part in enumerate((own, other)):
        for side in range(2):
            at = pl.multiple_of((core ^ far) * share + side * half, 8)
            whole[pl.ds(at, half), :] = part[:, side * LANES : (side + 1) * LANES]
    width, total = out_ref.shape
    for head in range(heads):
        live = min(LANES, total - head * LANES)
        if live > 0:
            out_ref[:, head * LANES : head * LANES + live] = (
                whole[head * padded : head * padded + width, 0:live] / divisor
            )


def on_device(
    node_feats, dest_grad, bases, coefs, src_ids, dst_ids, rel_ids, edge_norm, block_fill
):
    rows_total = lax.axis_size("row")
    cols = lax.axis_size("col")
    a_count, y_count = rows_total // PAIR, cols // PAIR
    shard, width = node_feats.shape
    basis_count = bases.shape[0]
    relation_count = coefs.shape[0]
    edges = src_ids.size
    padded = round_up(basis_count, TILE)
    heads = round_up(relation_count, LANES) // LANES
    while heads * padded % (PAIR * 2 * TILE):
        heads += 1
    span = 256
    i = lax.axis_index("row")
    j = lax.axis_index("col")
    place = jnp.stack([i // PAIR, i % PAIR, j // PAIR, j % PAIR]).astype(I32)

    def flip_x(value):
        return lax.ppermute(value, "row", [(r, r ^ 1) for r in range(rows_total)])

    def flip_core(value):
        return lax.ppermute(value, "col", [(c, c ^ 1) for c in range(cols)])

    def turn_z(value, by):
        return lax.ppermute(
            value, "row", [(r, (r + by * PAIR) % rows_total) for r in range(rows_total)]
        )

    def turn_y(value, by):
        return lax.ppermute(value, "col", [(c, (c + by * PAIR) % cols) for c in range(cols)])

    own_dest = dest_grad[0]
    turned = [turn_z(own_dest, s) for s in range(1, a_count)]
    across_own = flip_x(own_dest)
    near = flip_x(node_feats)
    meta = pl.pallas_call(
        prepare_kernel,
        out_shape=jax.ShapeDtypeStruct((4, edges), F32),
        in_specs=[smem()] + [vmem()] * 4,
        out_specs=vmem(),
        name="edge_table",
    )(block_fill, src_ids, dst_ids, rel_ids, edge_norm)
    meta = jnp.stack([meta, flip_x(meta)])
    middle = (a_count - 1) // 2
    sides = [s for s in range(a_count - 1) if s != middle]
    feats, meta, across_own, *early = lax.optimization_barrier(
        (jnp.stack([node_feats, near]), meta, across_own, *[turned[s] for s in sides])
    )
    for s, value in zip(sides, early):
        turned[s] = value
    feats = jnp.stack([feats] + [turn_y(feats, s) for s in range(1, y_count)])
    across = [None if s == middle else flip_x(turned[s]) for s in range(a_count - 1)]
    feats, turned[middle], *early = lax.optimization_barrier(
        (feats, turned[middle], *[across[s] for s in sides])
    )
    for s, value in zip(sides, early):
        across[s] = value
    across[middle] = flip_x(turned[middle])
    dest = [own_dest] + turned
    across = [across_own] + across
    meta_core = flip_core(meta)
    feats_core = flip_core(feats)

    xt = call(
        functools.partial(source_kernel, (cols, shard, span, a_count - 1)),
        jax.ShapeDtypeStruct((2 * PAIR, width, edges), BF16),
        4,
        [pltpu.VMEM((PAIR, width, cols * shard), BF16)],
        2 * 4 * edges * cols * shard * width,
        "source_rows",
        a_count - 1,
    )(place, meta, meta_core, feats, feats_core, *turned)

    dest_shard = own_dest.shape[0]
    gt, ct = call(
        functools.partial(grad_kernel, (rows_total, dest_shard, span, heads, padded)),
        (
            jax.ShapeDtypeStruct((width, PAIR * edges), BF16),
            jax.ShapeDtypeStruct((2 * PAIR, padded, edges), F32),
        ),
        3 + rows_total,
        [
            pltpu.VMEM((width, rows_total * dest_shard), BF16),
            pltpu.VMEM((heads * padded, LANES), BF16),
        ],
        2 * 2 * edges * rows_total * dest_shard * width,
        "edge_grads",
        1,
    )(place, meta, meta_core, coefs.T, *dest, *across, xt)
    gt_core = flip_core(gt)

    group = max(g for g in range(1, 6) if basis_count % g == 0)
    share_rows = heads * padded // PAIR // 2
    packed = call(
        functools.partial(forward_kernel, (cols, shard, span, heads, padded, group)),
        [jax.ShapeDtypeStruct((shard, width), BF16)] * cols
        + [jax.ShapeDtypeStruct((share_rows, width), F32)] * PAIR,
        5,
        [
            pltpu.VMEM((width, edges), F32),
            pltpu.VMEM((padded, edges), F32),
            pltpu.VMEM((heads * padded, edges), BF16),
            pltpu.VMEM((heads * padded, LANES), F32),
        ],
        2 * edges * width * width * basis_count,
        "backed_sums",
    )(place, meta, gt, xt, ct, bases)

    block = basis_count * width // (rows_total * cols)
    cover = block if block % TILE == 0 else round_up(block, TILE) + TILE

    def basis_blocks(place, turns):
        count = len(turns) * y_count
        return call(
            functools.partial(
                basis_kernel,
                (rows_total, cols, block, cover // TILE, basis_count, 2 * span, turns),
            ),
            [
                jax.ShapeDtypeStruct((len(turns) * cover, width), BF16 if sy else F32)
                for sy in range(y_count)
            ],
            4,
            [
                pltpu.VMEM((count * cover, width), F32),
                pltpu.VMEM((count * cover, 2 * span), BF16),
                pltpu.VMEM((count * cover, 2 * span), BF16),
                pltpu.VMEM((count * (round_up(cover, width) // width + 1), TILE, 2 * span), BF16),
            ],
            2 * 4 * edges * count * cover * width,
            "basis_terms",
        )(place, gt, gt_core, xt, ct)

    def to_col(value, far, sy):
        return lax.ppermute(
            value,
            "col",
            [(c, (c // PAIR + sy) % y_count * PAIR + (c % PAIR ^ far)) for c in range(cols)],
        )

    def after(value, other):
        return lax.optimization_barrier((value, other))[0]

    others = [(far, sy) for far in range(PAIR) for sy in range(y_count) if far or sy]

    order = tuple(range(1, a_count)) + (0,)
    half = (a_count + 1) // 2
    sums, landed, marks = {}, [], []

    def add_blocks(start, turns):
        blocks = basis_blocks(start, turns)
        marks.append(blocks[0])
        value = blocks[0]
        for sy in range(1, y_count):
            landed.append(turn_y(blocks[sy], sy))
            value = value + landed[-1].astype(F32)
        for at, sz in enumerate(turns):
            piece = value[at * cover : (at + 1) * cover]
            sums[sz] = turn_z(piece.astype(BF16), sz) if sz else piece

    coef_part = packed[cols] + flip_core(packed[cols + 1])
    add_blocks(after(place, coef_part), order[:half])
    coef_part = coef_part + after(flip_x(coef_part), marks[0])
    low = coef_part.astype(BF16)
    coef_part = tree_sum([low.astype(F32)] + [turn_z(low, s).astype(F32) for s in range(1, a_count)])
    add_blocks(after(after(place, low), marks[0]), order[half:])
    joined = packed[0].astype(F32)
    for far, sy in others:
        value = after(packed[far * y_count + sy], landed[-1])
        joined = joined + to_col(value, far, sy).astype(F32)
    basis_sum = sums[0]
    for sz in range(1, a_count):
        basis_sum = basis_sum + sums[sz].astype(F32)
    if cover != block:
        owner = i * cols + j
        basis_sum = lax.dynamic_slice_in_dim(basis_sum, owner * block % TILE, block, axis=0)
    basis_grad = basis_sum / cols

    node_grad = joined.astype(BF16)
    low = after(coef_part.astype(BF16), landed[0])
    coef_part = tree_sum([low.astype(F32)] + [turn_y(low, s).astype(F32) for s in range(1, y_count)])
    coef_grad = call(
        functools.partial(coef_kernel, (heads, padded, cols)),
        jax.ShapeDtypeStruct((basis_count, relation_count), F32),
        2,
        [pltpu.VMEM((heads * padded, LANES), F32)],
        1 << 20,
        "coef_rows",
    )(place, coef_part, flip_core(coef_part))
    return (node_grad, basis_grad, coef_grad.T)


def solution(mesh):
    in_specs = (
        P(("row", "col"), None),
        P("col", "row", None),
        P(),
        P(),
        P("row", "col", None),
        P("row", "col", None),
        P("row", "col", None),
        P("row", "col", None),
        P("row", "col", None),
    )
    out_specs = (P(("row", "col"), None), P(("row", "col"), None), P())
    return jax.shard_map(
        on_device, mesh=mesh, in_specs=in_specs, out_specs=out_specs, check_vma=False
    )
```

```python
import functools
import jax
import jax.numpy as jnp
from jax import lax
from jax.experimental import pallas as pl
from jax.experimental.pallas import tpu as pltpu
from jax.sharding import PartitionSpec as P

EDGE_BLOCK = 128
TILE = 16
LANES = 128
PAIR = 2
F32 = jnp.float32
BF16 = jnp.bfloat16
I32 = jnp.int32
VMEM_LIMIT = 32 * 1024 * 1024


def round_up(value, unit):
    return (value + unit - 1) // unit * unit


def split_index(ids, size):
    if size & (size - 1) == 0:
        shift = size.bit_length() - 1
        return ids >> shift, ids & (size - 1)
    return ids // size, ids % size


def wrap(difference, size):
    return jnp.where(difference < 0, difference + size, difference)


def one_hot(ids, depth):
    if depth <= 256:
        rows = lax.broadcasted_iota(I32, (depth, ids.shape[1]), 0).astype(F32).astype(BF16)
        one, zero = jnp.ones((), BF16), jnp.zeros((), BF16)
        return jnp.where(rows == ids.astype(F32).astype(BF16), one, zero)
    rows = lax.broadcasted_iota(I32, (depth, ids.shape[1]), 0)
    return jnp.where(rows == ids, 1.0, 0.0).astype(BF16)


def slot_hot(slot, local, slots, depth):
    return jnp.concatenate(
        [one_hot(jnp.where(slot == at, local, -1), depth) for at in range(slots)], axis=0
    )


def eye(width):
    first = lax.broadcasted_iota(I32, (width, width), 0)
    second = lax.broadcasted_iota(I32, (width, width), 1)
    return jnp.where(first == second, 1.0, 0.0).astype(BF16)


def dot(left, right):
    return lax.dot_general(left, right, (((1,), (0,)), ((), ())), preferred_element_type=F32)


def dot_t(left, right):
    return lax.dot_general(left, right, (((1,), (1,)), ((), ())), preferred_element_type=F32)


def tree_sum(values):
    if len(values) == 1:
        return values[0]
    return tree_sum(values[0::2]) + tree_sum(values[1::2])


def vmem():
    return pl.BlockSpec(memory_space=pltpu.VMEM)


def smem():
    return pl.BlockSpec(memory_space=pltpu.SMEM)


def call(body, out_shape, n_in, scratch, flops, name, unread=0):
    many = isinstance(out_shape, (tuple, list))
    moved = 1 << 22
    return pl.pallas_call(
        body,
        out_shape=out_shape,
        in_specs=[smem()] + [vmem()] * n_in + [pl.BlockSpec(memory_space=pl.ANY)] * unread,
        out_specs=[vmem()] * len(out_shape) if many else vmem(),
        scratch_shapes=scratch,
        compiler_params=pltpu.CompilerParams(vmem_limit_bytes=VMEM_LIMIT),
        cost_estimate=pl.CostEstimate(flops=flops, bytes_accessed=moved, transcendentals=0),
        name=name,
    )


def prepare_kernel(fills, src, dst, rel, norm, out_ref):
    blocks = fills.shape[-1]
    out_ref[0:1, :] = src[0].astype(F32)
    out_ref[1:2, :] = dst[0].astype(F32)
    out_ref[2:3, :] = rel[0].astype(F32)
    lane = lax.broadcasted_iota(I32, (1, EDGE_BLOCK), 1)
    for at in range(blocks):
        here = slice(at * EDGE_BLOCK, (at + 1) * EDGE_BLOCK)
        live = jnp.where(lane < fills[0, 0, at], 1.0, 0.0)
        out_ref[3:4, here] = norm[0, :, here] * live


def source_kernel(sizes, place, meta, meta_core, feats, feats_core, *refs):
    cols, shard, span, extra = sizes
    xt_ref, table = refs[extra:]
    count = cols // PAIR
    y, core = place[2], place[3]
    width = feats.shape[-1]
    edges = meta.shape[-1]
    unit = eye(width)
    for far, block in enumerate((feats, feats_core)):
        for sy in range(count):
            for xr in range(PAIR):
                at = (far * count + sy) * shard
                table[xr, :, at : at + shard] = dot_t(unit, block[sy, xr]).astype(BF16)
    for far, source in enumerate((meta, meta_core)):

        def step(index, carry, far=far, source=source):
            xr = index // (edges // span)
            at = pl.multiple_of(index % (edges // span) * span, span)
            ids = source[xr, 0:1, pl.ds(at, span)].astype(I32)
            owner, local = split_index(ids, shard)
            owner_y, owner_core = split_index(owner, PAIR)
            slot = (owner_core ^ core) * count + wrap(y - owner_y, count)
            rows = dot(table[xr], slot_hot(slot, local, cols, shard))
            xt_ref[far * PAIR + xr, :, pl.ds(at, span)] = rows.astype(BF16)
            return carry

        lax.fori_loop(0, PAIR * (edges // span), step, 0, unroll=2)


def grad_kernel(sizes, place, meta, meta_core, coefs_t, *refs):
    rows_total, shard, span, heads, padded = sizes
    count = rows_total // PAIR
    blocks = refs[:rows_total]
    gt_ref, ct_ref, table, coefs = refs[rows_total + 1 :]
    a, x = place[0], place[1]
    width = blocks[0].shape[-1]
    edges = meta.shape[-1]
    unit = eye(width)
    for at, block in enumerate(blocks):
        table[:, at * shard : (at + 1) * shard] = dot_t(unit, block[...]).astype(BF16)

    basis_count, relation_count = coefs_t.shape
    coefs[...] = jnp.zeros_like(coefs)
    for head in range(heads):
        live = min(LANES, relation_count - head * LANES)
        if live > 0:
            coefs[head * padded : head * padded + basis_count, 0:live] = coefs_t[
                :, head * LANES : head * LANES + live
            ]

    def step(index, carry):
        xr = index // (edges // span)
        at = pl.multiple_of(index % (edges // span) * span, span)
        ids = meta[xr, 1:2, pl.ds(at, span)].astype(I32)
        owner, local = split_index(ids, shard)
        owner_a, owner_x = split_index(owner, PAIR)
        slot = (owner_x ^ x) * count + wrap(a - owner_a, count)
        rows = dot(table[...], slot_hot(slot, local, rows_total, shard))
        weight = meta[xr, 3:4, pl.ds(at, span)]
        gt_ref[:, pl.ds(pl.multiple_of(index * span, span), span)] = (rows * weight).astype(BF16)
        for far, source in enumerate((meta, meta_core)):
            relation = source[xr, 2:3, pl.ds(at, span)].astype(I32)
            high, low = split_index(relation, LANES)
            parts = dot(coefs[...], one_hot(low, LANES))
            total = jnp.zeros((padded, span), F32)
            for head in range(heads):
                total = total + jnp.where(
                    high == head, parts[head * padded : (head + 1) * padded], 0.0
                )
            ct_ref[far * PAIR + xr, :, pl.ds(at, span)] = total
        return carry

    lax.fori_loop(0, PAIR * (edges // span), step, 0, unroll=2)


def forward_kernel(
    sizes, place, meta, gt_ref, xt_ref, ct_ref, bases_ref, *refs
):
    cols, shard, span, heads, padded, group = sizes
    outs, halves = refs[:PAIR], refs[PAIR : 2 * PAIR]
    total, inner, wide, coef_sum = refs[2 * PAIR :]
    count = cols // PAIR
    y, core = place[2], place[3]
    edges = meta.shape[-1]
    width = bases_ref.shape[-1]
    total[...] = jnp.zeros_like(total)
    inner[...] = jnp.zeros_like(inner)

    def step(number, carry):
        stacked = bases_ref[pl.ds(number * group, group)].reshape(group * width, width)
        for index in range(edges // span):
            at = slice(index * span, (index + 1) * span)
            backed = dot(stacked, gt_ref[:, at])
            rows = xt_ref[0, :, at].astype(F32)
            sums = total[:, at]
            for t in range(group):
                base = number * group + t
                mine = backed[t * width : (t + 1) * width]
                sums = sums + ct_ref[0, pl.ds(base, 1), at] * mine
                inner[pl.ds(base, 1), at] = jnp.sum(mine * rows, axis=0, keepdims=True)
            total[:, at] = sums
        return carry

    lax.fori_loop(0, bases_ref.shape[0] // group, step, 0)

    ids = meta[0, 0:1, :].astype(I32)
    owner, local = split_index(ids, shard)
    owner_y, owner_core = split_index(owner, PAIR)
    slot = (owner_core ^ core) * count + wrap(owner_y - y, count)
    values = total[...].astype(BF16)
    for at in range(cols):
        hot = one_hot(jnp.where(slot == at, local, -1), shard)
        row = at % count * shard
        outs[at // count][row : row + shard, :] = dot_t(hot, values).astype(BF16)
    high, low = split_index(meta[0, 2:3, :].astype(I32), LANES)
    for head in range(heads):
        wide[head * padded : (head + 1) * padded, :] = jnp.where(
            high == head, inner[...], 0.0
        ).astype(BF16)
    coef_sum[...] = dot_t(wide[...], one_hot(low, LANES))
    share = heads * padded // PAIR
    half = share // 2
    for far in range(PAIR):
        for side in range(2):
            at = pl.multiple_of((core ^ far) * share + side * half, 8)
            halves[far][:, side * LANES : (side + 1) * LANES] = coef_sum[pl.ds(at, half), :]


def basis_kernel(sizes, place, gt_ref, gt_core, xt_ref, ct_ref, *refs):
    rows_total, cols, block, groups, basis_count, span, turns = sizes
    a_count, y_count = rows_total // PAIR, cols // PAIR
    a, x, y, core = place[0], place[1], place[2], place[3]
    outs = refs[:y_count]
    acc, left_even, left_odd, tiles = refs[len(outs) :]
    width, edges = xt_ref.shape[1], xt_ref.shape[2]
    tiles_wide = width // TILE
    cover = groups * TILE
    spread = tiles.shape[0] // (y_count * len(turns))
    steps = edges // span
    firsts = []
    for sy in range(y_count):
        for sz in turns:
            owner = ((a + sz) % a_count * PAIR + x) * cols + (y + sy) % y_count * PAIR + core
            firsts.append(owner * block // TILE)

    def build(part, at, left):
        for order, first in enumerate(firsts):
            base = first // tiles_wide
            for extra in range(spread):
                row = ct_ref[part, pl.ds(jnp.minimum(base + extra, basis_count - 1), 1), at]
                tiles[order * spread + extra] = jnp.broadcast_to(row, (TILE, span)).astype(BF16)
            for q in range(groups):
                tile = jnp.minimum(first + q, basis_count * tiles_wide - 1)
                lower = pl.multiple_of(tile % tiles_wide * TILE, TILE)
                to = (order * groups + q) * TILE
                left[to : to + TILE, :] = (
                    tiles[order * spread + tile // tiles_wide - base]
                    * xt_ref[part, pl.ds(lower, TILE), at]
                )

    for index in range(2 * PAIR * steps):
        part = index // steps
        at = slice(index % steps * span, (index % steps + 1) * span)
        left = left_even if index % 2 == 0 else left_odd
        build(part, at, left)
        grads = gt_ref if part < PAIR else gt_core
        here = index % (PAIR * steps) * span
        term = dot_t(left[...], grads[:, here : here + span])
        if index:
            acc[...] += term
        else:
            acc[...] = term
    size = len(turns) * cover
    for sy, out in enumerate(outs):
        out[...] = acc[sy * size : (sy + 1) * size, :].astype(out.dtype)


def coef_kernel(sizes, place, own, other, out_ref, whole):
    heads, padded, divisor = sizes
    core = place[3]
    share = heads * padded // PAIR
    half = share // 2
    for far, part in enumerate((own, other)):
        for side in range(2):
            at = pl.multiple_of((core ^ far) * share + side * half, 8)
            whole[pl.ds(at, half), :] = part[:, side * LANES : (side + 1) * LANES]
    width, total = out_ref.shape
    for head in range(heads):
        live = min(LANES, total - head * LANES)
        if live > 0:
            out_ref[:, head * LANES : head * LANES + live] = (
                whole[head * padded : head * padded + width, 0:live] / divisor
            )


def on_device(
    node_feats, dest_grad, bases, coefs, src_ids, dst_ids, rel_ids, edge_norm, block_fill
):
    rows_total = lax.axis_size("row")
    cols = lax.axis_size("col")
    a_count, y_count = rows_total // PAIR, cols // PAIR
    shard, width = node_feats.shape
    basis_count = bases.shape[0]
    relation_count = coefs.shape[0]
    edges = src_ids.size
    padded = round_up(basis_count, TILE)
    heads = round_up(relation_count, LANES) // LANES
    while heads * padded % (PAIR * 2 * TILE):
        heads += 1
    span = 256
    i = lax.axis_index("row")
    j = lax.axis_index("col")
    place = jnp.stack([i // PAIR, i % PAIR, j // PAIR, j % PAIR]).astype(I32)

    def flip_x(value):
        return lax.ppermute(value, "row", [(r, r ^ 1) for r in range(rows_total)])

    def flip_core(value):
        return lax.ppermute(value, "col", [(c, c ^ 1) for c in range(cols)])

    def turn_z(value, by):
        return lax.ppermute(
            value, "row", [(r, (r + by * PAIR) % rows_total) for r in range(rows_total)]
        )

    def turn_y(value, by):
        return lax.ppermute(value, "col", [(c, (c + by * PAIR) % cols) for c in range(cols)])

    own_dest = dest_grad[0]
    turned = [turn_z(own_dest, s) for s in range(1, a_count)]
    across_own = flip_x(own_dest)
    near = flip_x(node_feats)
    meta = pl.pallas_call(
        prepare_kernel,
        out_shape=jax.ShapeDtypeStruct((4, edges), F32),
        in_specs=[smem()] + [vmem()] * 4,
        out_specs=vmem(),
        name="edge_table",
    )(block_fill, src_ids, dst_ids, rel_ids, edge_norm)
    meta = jnp.stack([meta, flip_x(meta)])
    middle = (a_count - 1) // 2
    sides = [s for s in range(a_count - 1) if s != middle]
    feats, meta, across_own, *early = lax.optimization_barrier(
        (jnp.stack([node_feats, near]), meta, across_own, *[turned[s] for s in sides])
    )
    for s, value in zip(sides, early):
        turned[s] = value
    feats = jnp.stack([feats] + [turn_y(feats, s) for s in range(1, y_count)])
    across = [None if s == middle else flip_x(turned[s]) for s in range(a_count - 1)]
    feats, turned[middle], *early = lax.optimization_barrier(
        (feats, turned[middle], *[across[s] for s in sides])
    )
    for s, value in zip(sides, early):
        across[s] = value
    across[middle] = flip_x(turned[middle])
    dest = [own_dest] + turned
    across = [across_own] + across
    meta_core = flip_core(meta)
    feats_core = flip_core(feats)

    xt = call(
        functools.partial(source_kernel, (cols, shard, span, a_count - 1)),
        jax.ShapeDtypeStruct((2 * PAIR, width, edges), BF16),
        4,
        [pltpu.VMEM((PAIR, width, cols * shard), BF16)],
        2 * 4 * edges * cols * shard * width,
        "source_rows",
        a_count - 1,
    )(place, meta, meta_core, feats, feats_core, *turned)

    dest_shard = own_dest.shape[0]
    gt, ct = call(
        functools.partial(grad_kernel, (rows_total, dest_shard, span, heads, padded)),
        (
            jax.ShapeDtypeStruct((width, PAIR * edges), BF16),
            jax.ShapeDtypeStruct((2 * PAIR, padded, edges), F32),
        ),
        3 + rows_total,
        [
            pltpu.VMEM((width, rows_total * dest_shard), BF16),
            pltpu.VMEM((heads * padded, LANES), BF16),
        ],
        2 * 2 * edges * rows_total * dest_shard * width,
        "edge_grads",
        1,
    )(place, meta, meta_core, coefs.T, *dest, *across, xt)
    gt_core = flip_core(gt)

    group = max(g for g in range(1, 6) if basis_count % g == 0)
    share_rows = heads * padded // PAIR // 2
    packed = call(
        functools.partial(forward_kernel, (cols, shard, span, heads, padded, group)),
        [jax.ShapeDtypeStruct((y_count * shard, width), BF16)] * PAIR
        + [jax.ShapeDtypeStruct((share_rows, width), F32)] * PAIR,
        5,
        [
            pltpu.VMEM((width, edges), F32),
            pltpu.VMEM((padded, edges), F32),
            pltpu.VMEM((heads * padded, edges), BF16),
            pltpu.VMEM((heads * padded, LANES), F32),
        ],
        2 * edges * width * width * basis_count,
        "backed_sums",
    )(place, meta, gt, xt, ct, bases)

    block = basis_count * width // (rows_total * cols)
    cover = block if block % TILE == 0 else round_up(block, TILE) + TILE

    def basis_blocks(place, turns):
        count = len(turns) * y_count
        return call(
            functools.partial(
                basis_kernel,
                (rows_total, cols, block, cover // TILE, basis_count, 2 * span, turns),
            ),
            [
                jax.ShapeDtypeStruct((len(turns) * cover, width), BF16 if sy else F32)
                for sy in range(y_count)
            ],
            4,
            [
                pltpu.VMEM((count * cover, width), F32),
                pltpu.VMEM((count * cover, 2 * span), BF16),
                pltpu.VMEM((count * cover, 2 * span), BF16),
                pltpu.VMEM((count * (round_up(cover, width) // width + 1), TILE, 2 * span), BF16),
            ],
            2 * 4 * edges * count * cover * width,
            "basis_terms",
        )(place, gt, gt_core, xt, ct)

    def after(value, other):
        return lax.optimization_barrier((value, other))[0]

    order = tuple(range(1, a_count)) + (0,)
    half = (a_count + 1) // 2
    sums, landed, marks = {}, [], []

    def add_blocks(start, turns):
        blocks = basis_blocks(start, turns)
        marks.append(blocks[0])
        value = blocks[0]
        for sy in range(1, y_count):
            landed.append(turn_y(blocks[sy], sy))
            value = value + landed[-1].astype(F32)
        for at, sz in enumerate(turns):
            piece = value[at * cover : (at + 1) * cover]
            sums[sz] = turn_z(piece.astype(BF16), sz) if sz else piece

    coef_part = packed[PAIR] + flip_core(packed[PAIR + 1])
    add_blocks(after(place, coef_part), order[:half])
    coef_part = coef_part + after(flip_x(coef_part), marks[0])
    low = coef_part.astype(BF16)
    coef_part = tree_sum([low.astype(F32)] + [turn_z(low, s).astype(F32) for s in range(1, a_count)])
    add_blocks(after(after(place, low), marks[0]), order[half:])
    joined = packed[0].astype(F32) + after(flip_core(packed[1]), marks[-1]).astype(F32)
    node_sum = joined[:shard]
    for sy in range(1, y_count):
        value = joined[sy * shard : (sy + 1) * shard].astype(BF16)
        node_sum = node_sum + turn_y(after(value, landed[-1]), sy).astype(F32)
    node_grad = node_sum.astype(BF16)
    low = after(coef_part.astype(BF16), landed[0])
    coef_part = tree_sum([low.astype(F32)] + [turn_y(low, s).astype(F32) for s in range(1, y_count)])
    coef_grad = call(
        functools.partial(coef_kernel, (heads, padded, cols)),
        jax.ShapeDtypeStruct((basis_count, relation_count), F32),
        2,
        [pltpu.VMEM((heads * padded, LANES), F32)],
        1 << 20,
        "coef_rows",
    )(place, coef_part, flip_core(coef_part))
    basis_sum = sums[0]
    for sz in range(1, a_count):
        basis_sum = basis_sum + after(sums[sz], coef_grad).astype(F32)
    if cover != block:
        owner = i * cols + j
        basis_sum = lax.dynamic_slice_in_dim(basis_sum, owner * block % TILE, block, axis=0)
    basis_grad = basis_sum / cols
    return (node_grad, basis_grad, coef_grad.T)


def solution(mesh):
    in_specs = (
        P(("row", "col"), None),
        P("col", "row", None),
        P(),
        P(),
        P("row", "col", None),
        P("row", "col", None),
        P("row", "col", None),
        P("row", "col", None),
        P("row", "col", None),
    )
    out_specs = (P(("row", "col"), None), P(("row", "col"), None), P())
    return jax.shard_map(
        on_device, mesh=mesh, in_specs=in_specs, out_specs=out_specs, check_vma=False
    )
```

```python
import functools
import jax
import jax.numpy as jnp
from jax import lax
from jax.experimental import pallas as pl
from jax.experimental.pallas import tpu as pltpu
from jax.sharding import PartitionSpec as P

EDGE_BLOCK = 128
TILE = 16
LANES = 128
PAIR = 2
F32 = jnp.float32
BF16 = jnp.bfloat16
I32 = jnp.int32
VMEM_LIMIT = 32 * 1024 * 1024


def round_up(value, unit):
    return (value + unit - 1) // unit * unit


def split_index(ids, size):
    if size & (size - 1) == 0:
        shift = size.bit_length() - 1
        return ids >> shift, ids & (size - 1)
    return ids // size, ids % size


def wrap(difference, size):
    return jnp.where(difference < 0, difference + size, difference)


def one_hot(ids, depth):
    if depth <= 256:
        rows = lax.broadcasted_iota(I32, (depth, ids.shape[1]), 0).astype(F32).astype(BF16)
        one, zero = jnp.ones((), BF16), jnp.zeros((), BF16)
        return jnp.where(rows == ids.astype(F32).astype(BF16), one, zero)
    rows = lax.broadcasted_iota(I32, (depth, ids.shape[1]), 0)
    return jnp.where(rows == ids, 1.0, 0.0).astype(BF16)


def slot_hot(slot, local, slots, depth):
    return jnp.concatenate(
        [one_hot(jnp.where(slot == at, local, -1), depth) for at in range(slots)], axis=0
    )


def eye(width):
    first = lax.broadcasted_iota(I32, (width, width), 0)
    second = lax.broadcasted_iota(I32, (width, width), 1)
    return jnp.where(first == second, 1.0, 0.0).astype(BF16)


def dot(left, right):
    return lax.dot_general(left, right, (((1,), (0,)), ((), ())), preferred_element_type=F32)


def dot_t(left, right):
    return lax.dot_general(left, right, (((1,), (1,)), ((), ())), preferred_element_type=F32)


def tree_sum(values):
    if len(values) == 1:
        return values[0]
    return tree_sum(values[0::2]) + tree_sum(values[1::2])


def vmem():
    return pl.BlockSpec(memory_space=pltpu.VMEM)


def smem():
    return pl.BlockSpec(memory_space=pltpu.SMEM)


def call(body, out_shape, n_in, scratch, flops, name, unread=0):
    many = isinstance(out_shape, (tuple, list))
    moved = 1 << 22
    return pl.pallas_call(
        body,
        out_shape=out_shape,
        in_specs=[smem()] + [vmem()] * n_in + [pl.BlockSpec(memory_space=pl.ANY)] * unread,
        out_specs=[vmem()] * len(out_shape) if many else vmem(),
        scratch_shapes=scratch,
        compiler_params=pltpu.CompilerParams(vmem_limit_bytes=VMEM_LIMIT),
        cost_estimate=pl.CostEstimate(flops=flops, bytes_accessed=moved, transcendentals=0),
        name=name,
    )


def prepare_kernel(fills, src, dst, rel, norm, out_ref):
    blocks = fills.shape[-1]
    out_ref[0:1, :] = src[0].astype(F32)
    out_ref[1:2, :] = dst[0].astype(F32)
    out_ref[2:3, :] = rel[0].astype(F32)
    lane = lax.broadcasted_iota(I32, (1, EDGE_BLOCK), 1)
    for at in range(blocks):
        here = slice(at * EDGE_BLOCK, (at + 1) * EDGE_BLOCK)
        live = jnp.where(lane < fills[0, 0, at], 1.0, 0.0)
        out_ref[3:4, here] = norm[0, :, here] * live


def source_kernel(sizes, place, meta, meta_core, feats, feats_core, *refs):
    cols, shard, span, extra = sizes
    xt_ref, table = refs[extra:]
    count = cols // PAIR
    y, core = place[2], place[3]
    width = feats.shape[-1]
    edges = meta.shape[-1]
    unit = eye(width)
    for far, block in enumerate((feats, feats_core)):
        for sy in range(count):
            for xr in range(PAIR):
                at = (far * count + sy) * shard
                table[xr, :, at : at + shard] = dot_t(unit, block[sy, xr]).astype(BF16)
    for far, source in enumerate((meta, meta_core)):

        def step(index, carry, far=far, source=source):
            xr = index // (edges // span)
            at = pl.multiple_of(index % (edges // span) * span, span)
            ids = source[xr, 0:1, pl.ds(at, span)].astype(I32)
            owner, local = split_index(ids, shard)
            owner_y, owner_core = split_index(owner, PAIR)
            slot = (owner_core ^ core) * count + wrap(y - owner_y, count)
            rows = dot(table[xr], slot_hot(slot, local, cols, shard))
            xt_ref[far * PAIR + xr, :, pl.ds(at, span)] = rows.astype(BF16)
            return carry

        lax.fori_loop(0, PAIR * (edges // span), step, 0, unroll=2)


def grad_kernel(sizes, place, meta, meta_core, coefs_t, *refs):
    rows_total, shard, span, heads, padded = sizes
    count = rows_total // PAIR
    blocks = refs[:rows_total]
    gt_ref, ct_ref, table, coefs = refs[rows_total + 1 :]
    a, x = place[0], place[1]
    width = blocks[0].shape[-1]
    edges = meta.shape[-1]
    unit = eye(width)
    for at, block in enumerate(blocks):
        table[:, at * shard : (at + 1) * shard] = dot_t(unit, block[...]).astype(BF16)

    basis_count, relation_count = coefs_t.shape
    coefs[...] = jnp.zeros_like(coefs)
    for head in range(heads):
        live = min(LANES, relation_count - head * LANES)
        if live > 0:
            coefs[head * padded : head * padded + basis_count, 0:live] = coefs_t[
                :, head * LANES : head * LANES + live
            ]

    def step(index, carry):
        xr = index // (edges // span)
        at = pl.multiple_of(index % (edges // span) * span, span)
        ids = meta[xr, 1:2, pl.ds(at, span)].astype(I32)
        owner, local = split_index(ids, shard)
        owner_a, owner_x = split_index(owner, PAIR)
        slot = (owner_x ^ x) * count + wrap(a - owner_a, count)
        rows = dot(table[...], slot_hot(slot, local, rows_total, shard))
        weight = meta[xr, 3:4, pl.ds(at, span)]
        gt_ref[:, pl.ds(pl.multiple_of(index * span, span), span)] = (rows * weight).astype(BF16)
        for far, source in enumerate((meta, meta_core)):
            relation = source[xr, 2:3, pl.ds(at, span)].astype(I32)
            high, low = split_index(relation, LANES)
            parts = dot(coefs[...], one_hot(low, LANES))
            total = jnp.zeros((padded, span), F32)
            for head in range(heads):
                total = total + jnp.where(
                    high == head, parts[head * padded : (head + 1) * padded], 0.0
                )
            ct_ref[far * PAIR + xr, :, pl.ds(at, span)] = total
        return carry

    lax.fori_loop(0, PAIR * (edges // span), step, 0, unroll=2)


def forward_kernel(
    sizes, place, meta, gt_ref, xt_ref, ct_ref, bases_ref, *refs
):
    cols, shard, span, heads, padded, group = sizes
    outs, halves = refs[:PAIR], refs[PAIR : 2 * PAIR]
    total, inner, wide, coef_sum = refs[2 * PAIR :]
    count = cols // PAIR
    y, core = place[2], place[3]
    edges = meta.shape[-1]
    width = bases_ref.shape[-1]
    total[...] = jnp.zeros_like(total)
    inner[...] = jnp.zeros_like(inner)

    def step(number, carry):
        stacked = bases_ref[pl.ds(number * group, group)].reshape(group * width, width)
        for index in range(edges // span):
            at = slice(index * span, (index + 1) * span)
            backed = dot(stacked, gt_ref[:, at])
            rows = xt_ref[0, :, at].astype(F32)
            sums = total[:, at]
            for t in range(group):
                base = number * group + t
                mine = backed[t * width : (t + 1) * width]
                sums = sums + ct_ref[0, pl.ds(base, 1), at] * mine
                inner[pl.ds(base, 1), at] = jnp.sum(mine * rows, axis=0, keepdims=True)
            total[:, at] = sums
        return carry

    lax.fori_loop(0, bases_ref.shape[0] // group, step, 0)

    ids = meta[0, 0:1, :].astype(I32)
    owner, local = split_index(ids, shard)
    owner_y, owner_core = split_index(owner, PAIR)
    slot = (owner_core ^ core) * count + wrap(owner_y - y, count)
    values = total[...].astype(BF16)
    for at in range(cols):
        hot = one_hot(jnp.where(slot == at, local, -1), shard)
        row = at % count * shard
        outs[at // count][row : row + shard, :] = dot_t(hot, values).astype(BF16)
    high, low = split_index(meta[0, 2:3, :].astype(I32), LANES)
    for head in range(heads):
        wide[head * padded : (head + 1) * padded, :] = jnp.where(
            high == head, inner[...], 0.0
        ).astype(BF16)
    coef_sum[...] = dot_t(wide[...], one_hot(low, LANES))
    share = heads * padded // PAIR
    half = share // 2
    for far in range(PAIR):
        for side in range(2):
            at = pl.multiple_of((core ^ far) * share + side * half, 8)
            halves[far][:, side * LANES : (side + 1) * LANES] = coef_sum[pl.ds(at, half), :]


def basis_kernel(sizes, place, gt_ref, gt_core, xt_ref, ct_ref, *refs):
    rows_total, cols, block, groups, basis_count, span, turns = sizes
    a_count, y_count = rows_total // PAIR, cols // PAIR
    a, x, y, core = place[0], place[1], place[2], place[3]
    outs = refs[:y_count]
    acc, left_even, left_odd, tiles = refs[len(outs) :]
    width, edges = xt_ref.shape[1], xt_ref.shape[2]
    tiles_wide = width // TILE
    cover = groups * TILE
    spread = tiles.shape[0] // (y_count * len(turns))
    steps = edges // span
    firsts = []
    for sy in range(y_count):
        for sz in turns:
            owner = ((a + sz) % a_count * PAIR + x) * cols + (y + sy) % y_count * PAIR + core
            firsts.append(owner * block // TILE)

    def build(part, at, left):
        for order, first in enumerate(firsts):
            base = first // tiles_wide
            for extra in range(spread):
                row = ct_ref[part, pl.ds(jnp.minimum(base + extra, basis_count - 1), 1), at]
                tiles[order * spread + extra] = jnp.broadcast_to(row, (TILE, span)).astype(BF16)
            for q in range(groups):
                tile = jnp.minimum(first + q, basis_count * tiles_wide - 1)
                lower = pl.multiple_of(tile % tiles_wide * TILE, TILE)
                to = (order * groups + q) * TILE
                left[to : to + TILE, :] = (
                    tiles[order * spread + tile // tiles_wide - base]
                    * xt_ref[part, pl.ds(lower, TILE), at]
                )

    for index in range(2 * PAIR * steps):
        part = index // steps
        at = slice(index % steps * span, (index % steps + 1) * span)
        left = left_even if index % 2 == 0 else left_odd
        build(part, at, left)
        grads = gt_ref if part < PAIR else gt_core
        here = index % (PAIR * steps) * span
        term = dot_t(left[...], grads[:, here : here + span])
        if index:
            acc[...] += term
        else:
            acc[...] = term
    size = len(turns) * cover
    for sy, out in enumerate(outs):
        out[...] = acc[sy * size : (sy + 1) * size, :].astype(out.dtype)


def coef_kernel(sizes, place, own, other, out_ref, whole):
    heads, padded, divisor = sizes
    core = place[3]
    share = heads * padded // PAIR
    half = share // 2
    for far, part in enumerate((own, other)):
        for side in range(2):
            at = pl.multiple_of((core ^ far) * share + side * half, 8)
            whole[pl.ds(at, half), :] = part[:, side * LANES : (side + 1) * LANES]
    width, total = out_ref.shape
    for head in range(heads):
        live = min(LANES, total - head * LANES)
        if live > 0:
            out_ref[:, head * LANES : head * LANES + live] = (
                whole[head * padded : head * padded + width, 0:live] / divisor
            )


def on_device(
    node_feats, dest_grad, bases, coefs, src_ids, dst_ids, rel_ids, edge_norm, block_fill
):
    rows_total = lax.axis_size("row")
    cols = lax.axis_size("col")
    a_count, y_count = rows_total // PAIR, cols // PAIR
    shard, width = node_feats.shape
    basis_count = bases.shape[0]
    relation_count = coefs.shape[0]
    edges = src_ids.size
    padded = round_up(basis_count, TILE)
    heads = round_up(relation_count, LANES) // LANES
    while heads * padded % (PAIR * 2 * TILE):
        heads += 1
    span = 256
    i = lax.axis_index("row")
    j = lax.axis_index("col")
    place = jnp.stack([i // PAIR, i % PAIR, j // PAIR, j % PAIR]).astype(I32)

    def flip_x(value):
        return lax.ppermute(value, "row", [(r, r ^ 1) for r in range(rows_total)])

    def flip_core(value):
        return lax.ppermute(value, "col", [(c, c ^ 1) for c in range(cols)])

    def turn_z(value, by):
        return lax.ppermute(
            value, "row", [(r, (r + by * PAIR) % rows_total) for r in range(rows_total)]
        )

    def turn_y(value, by):
        return lax.ppermute(value, "col", [(c, (c + by * PAIR) % cols) for c in range(cols)])

    own_dest = dest_grad[0]
    turned = [turn_z(own_dest, s) for s in range(1, a_count)]
    across_own = flip_x(own_dest)
    near = flip_x(node_feats)
    meta = pl.pallas_call(
        prepare_kernel,
        out_shape=jax.ShapeDtypeStruct((4, edges), F32),
        in_specs=[smem()] + [vmem()] * 4,
        out_specs=vmem(),
        name="edge_table",
    )(block_fill, src_ids, dst_ids, rel_ids, edge_norm)
    meta = jnp.stack([meta, flip_x(meta)])
    middle = (a_count - 1) // 2
    sides = [s for s in range(a_count - 1) if s != middle]
    feats, meta, across_own, *early = lax.optimization_barrier(
        (jnp.stack([node_feats, near]), meta, across_own, *[turned[s] for s in sides])
    )
    for s, value in zip(sides, early):
        turned[s] = value
    feats = jnp.stack([feats] + [turn_y(feats, s) for s in range(1, y_count)])
    across = [None if s == middle else flip_x(turned[s]) for s in range(a_count - 1)]
    feats, turned[middle], *early = lax.optimization_barrier(
        (feats, turned[middle], *[across[s] for s in sides])
    )
    for s, value in zip(sides, early):
        across[s] = value
    across[middle] = flip_x(turned[middle])
    dest = [own_dest] + turned
    across = [across_own] + across
    meta_core = flip_core(meta)
    feats_core = flip_core(feats)

    xt = call(
        functools.partial(source_kernel, (cols, shard, span, a_count - 1)),
        jax.ShapeDtypeStruct((2 * PAIR, width, edges), BF16),
        4,
        [pltpu.VMEM((PAIR, width, cols * shard), BF16)],
        2 * 4 * edges * cols * shard * width,
        "source_rows",
        a_count - 1,
    )(place, meta, meta_core, feats, feats_core, *turned)

    dest_shard = own_dest.shape[0]
    gt, ct = call(
        functools.partial(grad_kernel, (rows_total, dest_shard, span, heads, padded)),
        (
            jax.ShapeDtypeStruct((width, PAIR * edges), BF16),
            jax.ShapeDtypeStruct((2 * PAIR, padded, edges), F32),
        ),
        3 + rows_total,
        [
            pltpu.VMEM((width, rows_total * dest_shard), BF16),
            pltpu.VMEM((heads * padded, LANES), BF16),
        ],
        2 * 2 * edges * rows_total * dest_shard * width,
        "edge_grads",
        1,
    )(place, meta, meta_core, coefs.T, *dest, *across, xt)
    gt_core = flip_core(gt)

    group = max(g for g in range(1, 6) if basis_count % g == 0)
    share_rows = heads * padded // PAIR // 2
    packed = call(
        functools.partial(forward_kernel, (cols, shard, span, heads, padded, group)),
        [jax.ShapeDtypeStruct((y_count * shard, width), BF16)] * PAIR
        + [jax.ShapeDtypeStruct((share_rows, width), F32)] * PAIR,
        5,
        [
            pltpu.VMEM((width, edges), F32),
            pltpu.VMEM((padded, edges), F32),
            pltpu.VMEM((heads * padded, edges), BF16),
            pltpu.VMEM((heads * padded, LANES), F32),
        ],
        2 * edges * width * width * basis_count,
        "backed_sums",
    )(place, meta, gt, xt, ct, bases)

    block = basis_count * width // (rows_total * cols)
    cover = block if block % TILE == 0 else round_up(block, TILE) + TILE

    def basis_blocks(place, turns):
        count = len(turns) * y_count
        return call(
            functools.partial(
                basis_kernel,
                (rows_total, cols, block, cover // TILE, basis_count, 2 * span, turns),
            ),
            [
                jax.ShapeDtypeStruct((len(turns) * cover, width), BF16 if sy else F32)
                for sy in range(y_count)
            ],
            4,
            [
                pltpu.VMEM((count * cover, width), F32),
                pltpu.VMEM((count * cover, 2 * span), BF16),
                pltpu.VMEM((count * cover, 2 * span), BF16),
                pltpu.VMEM((count * (round_up(cover, width) // width + 1), TILE, 2 * span), BF16),
            ],
            2 * 4 * edges * count * cover * width,
            "basis_terms",
        )(place, gt, gt_core, xt, ct)

    def after(value, other):
        return lax.optimization_barrier((value, other))[0]

    order = tuple(range(1, a_count)) + (0,)
    half = (a_count + 1) // 2
    sums, landed, marks = {}, [], []

    def add_blocks(start, turns):
        blocks = basis_blocks(start, turns)
        marks.append(blocks[0])
        value = blocks[0]
        for sy in range(1, y_count):
            landed.append(turn_y(blocks[sy], sy))
            value = value + landed[-1].astype(F32)
        for at, sz in enumerate(turns):
            piece = value[at * cover : (at + 1) * cover]
            sums[sz] = turn_z(piece.astype(BF16), sz) if sz else piece

    coef_part = packed[PAIR] + flip_core(packed[PAIR + 1])
    add_blocks(after(place, coef_part), order[:half])
    coef_part = coef_part + after(flip_x(coef_part), marks[0])
    low = coef_part.astype(BF16)
    coef_part = tree_sum([low.astype(F32)] + [turn_z(low, s).astype(F32) for s in range(1, a_count)])
    add_blocks(after(after(place, low), marks[0]), order[half:])
    joined = packed[0].astype(F32) + after(flip_core(packed[1]), marks[-1]).astype(F32)
    halved = [joined[:shard]] + [
        turn_y(after(joined[sy * shard : (sy + 1) * shard].astype(BF16), landed[-1]), sy)
        for sy in range(1, y_count)
    ]
    low = after(coef_part.astype(BF16), landed[0])
    coef_part = tree_sum([low.astype(F32)] + [turn_y(low, s).astype(F32) for s in range(1, y_count)])
    coef_grad = call(
        functools.partial(coef_kernel, (heads, padded, cols)),
        jax.ShapeDtypeStruct((basis_count, relation_count), F32),
        2,
        [pltpu.VMEM((heads * padded, LANES), F32)],
        1 << 20,
        "coef_rows",
    )(place, coef_part, flip_core(coef_part))
    basis_sum = sums[0]
    for sz in range(1, a_count):
        basis_sum = basis_sum + after(sums[sz], coef_grad).astype(F32)
    if cover != block:
        owner = i * cols + j
        basis_sum = lax.dynamic_slice_in_dim(basis_sum, owner * block % TILE, block, axis=0)
    basis_grad = basis_sum / cols
    node_sum = halved[0]
    for value in halved[1:]:
        node_sum = node_sum + after(value, basis_grad).astype(F32)
    node_grad = node_sum.astype(BF16)
    return (node_grad, basis_grad, coef_grad.T)


def solution(mesh):
    in_specs = (
        P(("row", "col"), None),
        P("col", "row", None),
        P(),
        P(),
        P("row", "col", None),
        P("row", "col", None),
        P("row", "col", None),
        P("row", "col", None),
        P("row", "col", None),
    )
    out_specs = (P(("row", "col"), None), P(("row", "col"), None), P())
    return jax.shard_map(
        on_device, mesh=mesh, in_specs=in_specs, out_specs=out_specs, check_vma=False
    )
```

```python
import functools
import jax
import jax.numpy as jnp
from jax import lax
from jax.experimental import pallas as pl
from jax.experimental.pallas import tpu as pltpu
from jax.sharding import PartitionSpec as P

EDGE_BLOCK = 128
TILE = 16
LANES = 128
PAIR = 2
F32 = jnp.float32
BF16 = jnp.bfloat16
I32 = jnp.int32
VMEM_LIMIT = 32 * 1024 * 1024


def round_up(value, unit):
    return (value + unit - 1) // unit * unit


def split_index(ids, size):
    if size & (size - 1) == 0:
        shift = size.bit_length() - 1
        return ids >> shift, ids & (size - 1)
    return ids // size, ids % size


def wrap(difference, size):
    return jnp.where(difference < 0, difference + size, difference)


def one_hot(ids, depth):
    if depth <= 256:
        rows = lax.broadcasted_iota(I32, (depth, ids.shape[1]), 0).astype(F32).astype(BF16)
        one, zero = jnp.ones((), BF16), jnp.zeros((), BF16)
        return jnp.where(rows == ids.astype(F32).astype(BF16), one, zero)
    rows = lax.broadcasted_iota(I32, (depth, ids.shape[1]), 0)
    return jnp.where(rows == ids, 1.0, 0.0).astype(BF16)


def slot_hot(slot, local, slots, depth):
    return jnp.concatenate(
        [one_hot(jnp.where(slot == at, local, -1), depth) for at in range(slots)], axis=0
    )


def eye(width):
    first = lax.broadcasted_iota(I32, (width, width), 0)
    second = lax.broadcasted_iota(I32, (width, width), 1)
    return jnp.where(first == second, 1.0, 0.0).astype(BF16)


def dot(left, right):
    return lax.dot_general(left, right, (((1,), (0,)), ((), ())), preferred_element_type=F32)


def dot_t(left, right):
    return lax.dot_general(left, right, (((1,), (1,)), ((), ())), preferred_element_type=F32)


def tree_sum(values):
    if len(values) == 1:
        return values[0]
    return tree_sum(values[0::2]) + tree_sum(values[1::2])


def vmem():
    return pl.BlockSpec(memory_space=pltpu.VMEM)


def smem():
    return pl.BlockSpec(memory_space=pltpu.SMEM)


def call(body, out_shape, n_in, scratch, flops, name, unread=0):
    many = isinstance(out_shape, (tuple, list))
    moved = 1 << 22
    return pl.pallas_call(
        body,
        out_shape=out_shape,
        in_specs=[smem()] + [vmem()] * n_in + [pl.BlockSpec(memory_space=pl.ANY)] * unread,
        out_specs=[vmem()] * len(out_shape) if many else vmem(),
        scratch_shapes=scratch,
        compiler_params=pltpu.CompilerParams(vmem_limit_bytes=VMEM_LIMIT),
        cost_estimate=pl.CostEstimate(flops=flops, bytes_accessed=moved, transcendentals=0),
        name=name,
    )


def prepare_kernel(fills, src, dst, rel, norm, out_ref):
    blocks = fills.shape[-1]
    out_ref[0:1, :] = src[0].astype(F32)
    out_ref[1:2, :] = dst[0].astype(F32)
    out_ref[2:3, :] = rel[0].astype(F32)
    lane = lax.broadcasted_iota(I32, (1, EDGE_BLOCK), 1)
    for at in range(blocks):
        here = slice(at * EDGE_BLOCK, (at + 1) * EDGE_BLOCK)
        live = jnp.where(lane < fills[0, 0, at], 1.0, 0.0)
        out_ref[3:4, here] = norm[0, :, here] * live


def source_kernel(sizes, place, meta, meta_core, feats, feats_core, *refs):
    cols, shard, span, extra = sizes
    xt_ref, table = refs[extra:]
    count = cols // PAIR
    y, core = place[2], place[3]
    width = feats.shape[-1]
    edges = meta.shape[-1]
    unit = eye(width)
    for far, block in enumerate((feats, feats_core)):
        for sy in range(count):
            for xr in range(PAIR):
                at = (far * count + sy) * shard
                table[xr, :, at : at + shard] = dot_t(unit, block[sy, xr]).astype(BF16)
    for far, source in enumerate((meta, meta_core)):

        def step(index, carry, far=far, source=source):
            xr = index // (edges // span)
            at = pl.multiple_of(index % (edges // span) * span, span)
            ids = source[xr, 0:1, pl.ds(at, span)].astype(I32)
            owner, local = split_index(ids, shard)
            owner_y, owner_core = split_index(owner, PAIR)
            slot = (owner_core ^ core) * count + wrap(y - owner_y, count)
            rows = dot(table[xr], slot_hot(slot, local, cols, shard))
            xt_ref[far * PAIR + xr, :, pl.ds(at, span)] = rows.astype(BF16)
            return carry

        lax.fori_loop(0, PAIR * (edges // span), step, 0, unroll=2)


def grad_kernel(sizes, place, meta, meta_core, coefs_t, *refs):
    rows_total, shard, span, heads, padded = sizes
    count = rows_total // PAIR
    blocks = refs[:rows_total]
    gt_ref, ct_ref, table, coefs = refs[rows_total + 1 :]
    a, x = place[0], place[1]
    width = blocks[0].shape[-1]
    edges = meta.shape[-1]
    unit = eye(width)
    for at, block in enumerate(blocks):
        table[:, at * shard : (at + 1) * shard] = dot_t(unit, block[...]).astype(BF16)

    basis_count, relation_count = coefs_t.shape
    coefs[...] = jnp.zeros_like(coefs)
    for head in range(heads):
        live = min(LANES, relation_count - head * LANES)
        if live > 0:
            coefs[head * padded : head * padded + basis_count, 0:live] = coefs_t[
                :, head * LANES : head * LANES + live
            ]

    def step(index, carry):
        xr = index // (edges // span)
        at = pl.multiple_of(index % (edges // span) * span, span)
        ids = meta[xr, 1:2, pl.ds(at, span)].astype(I32)
        owner, local = split_index(ids, shard)
        owner_a, owner_x = split_index(owner, PAIR)
        slot = (owner_x ^ x) * count + wrap(a - owner_a, count)
        rows = dot(table[...], slot_hot(slot, local, rows_total, shard))
        weight = meta[xr, 3:4, pl.ds(at, span)]
        gt_ref[:, pl.ds(pl.multiple_of(index * span, span), span)] = (rows * weight).astype(BF16)
        for far, source in enumerate((meta, meta_core)):
            relation = source[xr, 2:3, pl.ds(at, span)].astype(I32)
            high, low = split_index(relation, LANES)
            parts = dot(coefs[...], one_hot(low, LANES))
            total = jnp.zeros((padded, span), F32)
            for head in range(heads):
                total = total + jnp.where(
                    high == head, parts[head * padded : (head + 1) * padded], 0.0
                )
            ct_ref[far * PAIR + xr, :, pl.ds(at, span)] = total
        return carry

    lax.fori_loop(0, PAIR * (edges // span), step, 0, unroll=2)


def forward_kernel(
    sizes, place, meta, gt_ref, xt_ref, ct_ref, bases_ref, *refs
):
    cols, shard, span, heads, padded, group = sizes
    outs, halves = refs[:PAIR], refs[PAIR : 2 * PAIR]
    total, inner, wide, coef_sum = refs[2 * PAIR :]
    count = cols // PAIR
    y, core = place[2], place[3]
    edges = meta.shape[-1]
    width = bases_ref.shape[-1]
    total[...] = jnp.zeros_like(total)
    inner[...] = jnp.zeros_like(inner)

    def step(number, carry):
        stacked = bases_ref[pl.ds(number * group, group)].reshape(group * width, width)
        for index in range(edges // span):
            at = slice(index * span, (index + 1) * span)
            backed = dot(stacked, gt_ref[:, at])
            rows = xt_ref[0, :, at].astype(F32)
            sums = total[:, at]
            for t in range(group):
                base = number * group + t
                mine = backed[t * width : (t + 1) * width]
                sums = sums + ct_ref[0, pl.ds(base, 1), at] * mine
                inner[pl.ds(base, 1), at] = jnp.sum(mine * rows, axis=0, keepdims=True)
            total[:, at] = sums
        return carry

    lax.fori_loop(0, bases_ref.shape[0] // group, step, 0)

    ids = meta[0, 0:1, :].astype(I32)
    owner, local = split_index(ids, shard)
    owner_y, owner_core = split_index(owner, PAIR)
    slot = (owner_core ^ core) * count + wrap(owner_y - y, count)
    values = total[...].astype(BF16)
    for at in range(cols):
        hot = one_hot(jnp.where(slot == at, local, -1), shard)
        row = at % count * shard
        outs[at // count][row : row + shard, :] = dot_t(hot, values).astype(BF16)
    high, low = split_index(meta[0, 2:3, :].astype(I32), LANES)
    for head in range(heads):
        wide[head * padded : (head + 1) * padded, :] = jnp.where(
            high == head, inner[...], 0.0
        ).astype(BF16)
    coef_sum[...] = dot_t(wide[...], one_hot(low, LANES))
    share = heads * padded // PAIR
    half = share // 2
    for far in range(PAIR):
        for side in range(2):
            at = pl.multiple_of((core ^ far) * share + side * half, 8)
            halves[far][:, side * LANES : (side + 1) * LANES] = coef_sum[pl.ds(at, half), :]


def basis_kernel(sizes, place, gt_ref, gt_core, xt_ref, ct_ref, *refs):
    rows_total, cols, block, groups, basis_count, span, turns = sizes
    a_count, y_count = rows_total // PAIR, cols // PAIR
    a, x, y, core = place[0], place[1], place[2], place[3]
    outs = refs[:y_count]
    acc, left_even, left_odd, tiles = refs[len(outs) :]
    width, edges = xt_ref.shape[1], xt_ref.shape[2]
    tiles_wide = width // TILE
    cover = groups * TILE
    spread = tiles.shape[0] // (y_count * len(turns))
    steps = edges // span
    firsts = []
    for sy in range(y_count):
        for sz in turns:
            owner = ((a + sz) % a_count * PAIR + x) * cols + (y + sy) % y_count * PAIR + core
            firsts.append(owner * block // TILE)

    def build(part, at, left):
        for order, first in enumerate(firsts):
            base = first // tiles_wide
            for extra in range(spread):
                row = ct_ref[part, pl.ds(jnp.minimum(base + extra, basis_count - 1), 1), at]
                tiles[order * spread + extra] = jnp.broadcast_to(row, (TILE, span)).astype(BF16)
            for q in range(groups):
                tile = jnp.minimum(first + q, basis_count * tiles_wide - 1)
                lower = pl.multiple_of(tile % tiles_wide * TILE, TILE)
                to = (order * groups + q) * TILE
                left[to : to + TILE, :] = (
                    tiles[order * spread + tile // tiles_wide - base]
                    * xt_ref[part, pl.ds(lower, TILE), at]
                )

    for index in range(2 * PAIR * steps):
        part = index // steps
        at = slice(index % steps * span, (index % steps + 1) * span)
        left = left_even if index % 2 == 0 else left_odd
        build(part, at, left)
        grads = gt_ref if part < PAIR else gt_core
        here = index % (PAIR * steps) * span
        term = dot_t(left[...], grads[:, here : here + span])
        if index:
            acc[...] += term
        else:
            acc[...] = term
    size = len(turns) * cover
    for sy, out in enumerate(outs):
        out[...] = acc[sy * size : (sy + 1) * size, :].astype(out.dtype)


def coef_kernel(sizes, place, own, other, out_ref, whole):
    heads, padded, divisor = sizes
    core = place[3]
    share = heads * padded // PAIR
    half = share // 2
    for far, part in enumerate((own, other)):
        for side in range(2):
            at = pl.multiple_of((core ^ far) * share + side * half, 8)
            whole[pl.ds(at, half), :] = part[:, side * LANES : (side + 1) * LANES]
    width, total = out_ref.shape
    for head in range(heads):
        live = min(LANES, total - head * LANES)
        if live > 0:
            out_ref[:, head * LANES : head * LANES + live] = (
                whole[head * padded : head * padded + width, 0:live] / divisor
            )


def on_device(
    node_feats, dest_grad, bases, coefs, src_ids, dst_ids, rel_ids, edge_norm, block_fill
):
    rows_total = lax.axis_size("row")
    cols = lax.axis_size("col")
    a_count, y_count = rows_total // PAIR, cols // PAIR
    shard, width = node_feats.shape
    basis_count = bases.shape[0]
    relation_count = coefs.shape[0]
    edges = src_ids.size
    padded = round_up(basis_count, TILE)
    heads = round_up(relation_count, LANES) // LANES
    while heads * padded % (PAIR * 2 * TILE):
        heads += 1
    span = 256
    i = lax.axis_index("row")
    j = lax.axis_index("col")
    place = jnp.stack([i // PAIR, i % PAIR, j // PAIR, j % PAIR]).astype(I32)

    def flip_x(value):
        return lax.ppermute(value, "row", [(r, r ^ 1) for r in range(rows_total)])

    def flip_core(value):
        return lax.ppermute(value, "col", [(c, c ^ 1) for c in range(cols)])

    def turn_z(value, by):
        return lax.ppermute(
            value, "row", [(r, (r + by * PAIR) % rows_total) for r in range(rows_total)]
        )

    def turn_y(value, by):
        return lax.ppermute(value, "col", [(c, (c + by * PAIR) % cols) for c in range(cols)])

    own_dest = dest_grad[0]
    turned = [turn_z(own_dest, s) for s in range(1, a_count)]
    across_own = flip_x(own_dest)
    near = flip_x(node_feats)
    meta = pl.pallas_call(
        prepare_kernel,
        out_shape=jax.ShapeDtypeStruct((4, edges), F32),
        in_specs=[smem()] + [vmem()] * 4,
        out_specs=vmem(),
        name="edge_table",
    )(block_fill, src_ids, dst_ids, rel_ids, edge_norm)
    meta = jnp.stack([meta, flip_x(meta)])
    middle = (a_count - 1) // 2
    sides = [s for s in range(a_count - 1) if s != middle]
    feats, meta, across_own, *early = lax.optimization_barrier(
        (jnp.stack([node_feats, near]), meta, across_own, *[turned[s] for s in sides])
    )
    for s, value in zip(sides, early):
        turned[s] = value
    feats = jnp.stack([feats] + [turn_y(feats, s) for s in range(1, y_count)])
    across = [None if s == middle else flip_x(turned[s]) for s in range(a_count - 1)]
    feats, turned[middle], *early = lax.optimization_barrier(
        (feats, turned[middle], *[across[s] for s in sides[:1]])
    )
    for s, value in zip(sides, early):
        across[s] = value
    across[middle] = flip_x(turned[middle])
    dest = [own_dest] + turned
    across = [across_own] + across
    meta_core = flip_core(meta)
    feats_core = flip_core(feats)

    xt = call(
        functools.partial(source_kernel, (cols, shard, span, a_count - 1)),
        jax.ShapeDtypeStruct((2 * PAIR, width, edges), BF16),
        4,
        [pltpu.VMEM((PAIR, width, cols * shard), BF16)],
        2 * 4 * edges * cols * shard * width,
        "source_rows",
        a_count - 1,
    )(place, meta, meta_core, feats, feats_core, *turned)

    dest_shard = own_dest.shape[0]
    gt, ct = call(
        functools.partial(grad_kernel, (rows_total, dest_shard, span, heads, padded)),
        (
            jax.ShapeDtypeStruct((width, PAIR * edges), BF16),
            jax.ShapeDtypeStruct((2 * PAIR, padded, edges), F32),
        ),
        3 + rows_total,
        [
            pltpu.VMEM((width, rows_total * dest_shard), BF16),
            pltpu.VMEM((heads * padded, LANES), BF16),
        ],
        2 * 2 * edges * rows_total * dest_shard * width,
        "edge_grads",
        1,
    )(place, meta, meta_core, coefs.T, *dest, *across, xt)
    gt_core = flip_core(gt)

    group = max(g for g in range(1, 6) if basis_count % g == 0)
    share_rows = heads * padded // PAIR // 2
    packed = call(
        functools.partial(forward_kernel, (cols, shard, span, heads, padded, group)),
        [jax.ShapeDtypeStruct((y_count * shard, width), BF16)] * PAIR
        + [jax.ShapeDtypeStruct((share_rows, width), F32)] * PAIR,
        5,
        [
            pltpu.VMEM((width, edges), F32),
            pltpu.VMEM((padded, edges), F32),
            pltpu.VMEM((heads * padded, edges), BF16),
            pltpu.VMEM((heads * padded, LANES), F32),
        ],
        2 * edges * width * width * basis_count,
        "backed_sums",
    )(place, meta, gt, xt, ct, bases)

    block = basis_count * width // (rows_total * cols)
    cover = block if block % TILE == 0 else round_up(block, TILE) + TILE

    def basis_blocks(place, turns):
        count = len(turns) * y_count
        return call(
            functools.partial(
                basis_kernel,
                (rows_total, cols, block, cover // TILE, basis_count, 2 * span, turns),
            ),
            [
                jax.ShapeDtypeStruct((len(turns) * cover, width), BF16 if sy else F32)
                for sy in range(y_count)
            ],
            4,
            [
                pltpu.VMEM((count * cover, width), F32),
                pltpu.VMEM((count * cover, 2 * span), BF16),
                pltpu.VMEM((count * cover, 2 * span), BF16),
                pltpu.VMEM((count * (round_up(cover, width) // width + 1), TILE, 2 * span), BF16),
            ],
            2 * 4 * edges * count * cover * width,
            "basis_terms",
        )(place, gt, gt_core, xt, ct)

    def after(value, other):
        return lax.optimization_barrier((value, other))[0]

    order = tuple(range(1, a_count)) + (0,)
    half = (a_count + 1) // 2
    sums, landed, marks = {}, [], []

    def add_blocks(start, turns):
        blocks = basis_blocks(start, turns)
        marks.append(blocks[0])
        value = blocks[0]
        for sy in range(1, y_count):
            landed.append(turn_y(blocks[sy], sy))
            value = value + landed[-1].astype(F32)
        for at, sz in enumerate(turns):
            piece = value[at * cover : (at + 1) * cover]
            sums[sz] = turn_z(piece.astype(BF16), sz) if sz else piece

    coef_part = packed[PAIR] + flip_core(packed[PAIR + 1])
    add_blocks(after(place, coef_part), order[:half])
    coef_part = coef_part + after(flip_x(coef_part), marks[0])
    low = coef_part.astype(BF16)
    coef_part = tree_sum([low.astype(F32)] + [turn_z(low, s).astype(F32) for s in range(1, a_count)])
    add_blocks(after(after(place, low), marks[0]), order[half:])
    joined = packed[0].astype(F32) + after(flip_core(packed[1]), marks[-1]).astype(F32)
    halved = [joined[:shard]] + [
        turn_y(after(joined[sy * shard : (sy + 1) * shard].astype(BF16), landed[-1]), sy)
        for sy in range(1, y_count)
    ]
    low = after(coef_part.astype(BF16), landed[0])
    coef_part = tree_sum([low.astype(F32)] + [turn_y(low, s).astype(F32) for s in range(1, y_count)])
    coef_grad = call(
        functools.partial(coef_kernel, (heads, padded, cols)),
        jax.ShapeDtypeStruct((basis_count, relation_count), F32),
        2,
        [pltpu.VMEM((heads * padded, LANES), F32)],
        1 << 20,
        "coef_rows",
    )(place, coef_part, flip_core(coef_part))
    basis_sum = sums[0]
    for sz in range(1, a_count):
        basis_sum = basis_sum + after(sums[sz], coef_grad).astype(F32)
    if cover != block:
        owner = i * cols + j
        basis_sum = lax.dynamic_slice_in_dim(basis_sum, owner * block % TILE, block, axis=0)
    basis_grad = basis_sum / cols
    node_sum = halved[0]
    for value in halved[1:]:
        node_sum = node_sum + after(value, basis_grad).astype(F32)
    node_grad = node_sum.astype(BF16)
    return (node_grad, basis_grad, coef_grad.T)


def solution(mesh):
    in_specs = (
        P(("row", "col"), None),
        P("col", "row", None),
        P(),
        P(),
        P("row", "col", None),
        P("row", "col", None),
        P("row", "col", None),
        P("row", "col", None),
        P("row", "col", None),
    )
    out_specs = (P(("row", "col"), None), P(("row", "col"), None), P())
    return jax.shard_map(
        on_device, mesh=mesh, in_specs=in_specs, out_specs=out_specs, check_vma=False
    )
```
